128 devices in a mesh: row: 8 (over x, y_lo), col: 16 (over z, y_hi, core).
Axes of the slice: x: 4, y: 4 (y_hi: 2, y_lo: 2; y = y_hi * 2 + y_lo), z: 4, core: 2. Of those that a mesh axis runs over, the one named last changes fastest.
Arguments:
- halves: float32 [2, 4096, 16384], P(None, 'row', 'col'), may hold values from -6 to 6
- diag_rest: float32 [8192, 1024], P(('col', 'row')), may hold values from -6 to 6
- panel_vectors: float32 [16384, 256], P('col'), may hold values from -1 to 1
- tri_factor: float32 [256, 256], replicated, may hold values from -1 to 2, as said below
Outputs:
- updated_halves: float32 [2, 4096, 16384], P(None, 'row', 'col')
- updated_rest: float32 [8192, 1024], P(('col', 'row'))
- w_panel: float32 [16384, 256], P('col')
The draws below stay inside these ranges and needn't reach their ends.
Inputs may be any that keep to these rules, and one draw needn't show every extreme that they name: `tri_factor`: upper triangular, diagonal between 1 and 2.
All inputs are finite; a program needn't handle non-finite values.
Results may differ from the reference program's by a relative error of at most 0.0003.
Values sent between devices are 32-bit elements; how exact they have to be, the bound alone decides.
A program may use at most 64 MiB of HBM per device.

```python
import jax
import jax.numpy as jnp
from jax import lax

TILE = 1024
K = 256
ORDER = 16384
N_ROW = 8
N_COL = 16


def draw_panel_vectors(key, part):
    base = jax.random.normal(key, (ORDER, K), jnp.float32)
    basis, upper = jnp.linalg.qr(base)
    return basis


def draw_tri_factor(key, part):
    first, second = jax.random.split(jax.random.fold_in(key, 7))
    spread = jnp.clip(jax.random.normal(first, (K, K), jnp.float32), -4.0, 4.0) / K ** 0.5
    diagonal = jax.random.uniform(second, (K,), jnp.float32, minval=1.0, maxval=2.0)
    return jnp.triu(spread, 1) + jnp.diag(diagonal)


def block_levels(stream_key, dims, cuts, low, largest):
    factor_of, own = 1.0, jax.random.fold_in(stream_key, 6)
    for axis_at, parts in cuts:
        steps = jnp.exp(jax.random.uniform(jax.random.fold_in(own, axis_at), (parts,), jnp.float32, low / len(cuts), largest / len(cuts)))
        factor_of = factor_of * jnp.repeat(steps, dims[axis_at] // parts).reshape([-1 if axis == axis_at else 1 for axis in range(len(dims))])
    return factor_of


def scatter_about(rng, extent, deviation, reach, pieces=(), kind=jnp.bfloat16):
    values = jax.random.normal(rng, extent, jnp.float32) * deviation
    if len(pieces) > 0:
        values = block_levels(rng, extent, pieces, -0.22, 0.18) * values
    return jnp.clip(values, min=-reach, max=reach).astype(kind)


def setup_inputs(seed: int = 0) -> dict:
    key_list = jax.random.split(jax.random.key(seed), 5)
    halves = scatter_about(key_list[0], (2, N_ROW * TILE // 2, ORDER), 1.0, 6.0, ((1, 8), (2, 16)), jnp.float32)
    diag_rest = scatter_about(key_list[1], (ORDER // 2, TILE), 1.0, 6.0, ((0, 128),), jnp.float32)
    panel_vectors = draw_panel_vectors(jax.random.fold_in(key_list[4], 71), 0)
    tri_factor = draw_tri_factor(jax.random.fold_in(key_list[4], 71), 0)
    return {"halves": halves, "diag_rest": diag_rest, "panel_vectors": panel_vectors, "tri_factor": tri_factor}


precise = lax.Precision.HIGHEST

def reference(halves, diag_rest, panel_vectors, tri_factor):
    blocks = N_COL
    half_size = TILE // 2
    stored = halves.reshape(2, N_ROW, half_size, blocks, TILE).transpose(0, 1, 3, 2, 4).reshape(blocks, blocks, half_size, TILE)
    vectors = panel_vectors.reshape(blocks, TILE, K)
    vec_halves = vectors.reshape(blocks, 2, half_size, K)
    rest = diag_rest.reshape(blocks, half_size, TILE)
    index = jnp.arange(blocks, dtype=jnp.int32)

    def geometry(block_row):
        is_lower = block_row >= index
        low_block = jnp.minimum(block_row, index).astype(jnp.int32)
        high_block = jnp.maximum(block_row, index).astype(jnp.int32)
        which = jnp.where(is_lower, 0, 1).astype(jnp.int32)
        weight = jnp.where(block_row == index, 0.5, 1.0).astype(jnp.float32)
        return (is_lower, low_block, high_block, which, weight)

    def add_terms(block_row, total):
        is_lower, low_block, high_block, which, weight = geometry(block_row)
        tiles = stored[block_row]
        low_vec = vectors[low_block]
        high_half = vec_halves[high_block, which]
        first = jnp.einsum('qhT,qTk->qhk', tiles, low_vec, precision=precise) * weight[:, None, None]
        second = jnp.einsum('qhT,qhk->qTk', tiles, high_half, precision=precise) * weight[:, None, None]
        zeros = jnp.zeros_like(first)
        padded = jnp.where(is_lower[:, None, None], jnp.concatenate([first, zeros], 1), jnp.concatenate([zeros, first], 1))
        one_high = (high_block[:, None] == index[None, :]).astype(jnp.float32)
        one_low = (low_block[:, None] == index[None, :]).astype(jnp.float32)
        total = total + jnp.einsum('qi,qTk->iTk', one_high, padded, precision=precise)
        return total + jnp.einsum('qi,qTk->iTk', one_low, second, precision=precise)
    total = lax.fori_loop(0, blocks, add_terms, jnp.zeros((blocks, TILE, K), jnp.float32))
    first_rest = jnp.einsum('ihT,iTk->ihk', rest, vectors, precision=precise) * 0.5
    second_rest = jnp.einsum('ihT,ihk->iTk', rest, vec_halves[:, 1], precision=precise) * 0.5
    av_blocks = total + jnp.concatenate([jnp.zeros_like(first_rest), first_rest], 1) + second_rest
    inner = jnp.einsum('iTk,iTl->kl', vectors, av_blocks, precision=precise)
    middle = jnp.dot(jnp.dot(tri_factor.T, inner, precision=precise), tri_factor, precision=precise)
    w_blocks = jnp.einsum('iTk,kl->iTl', av_blocks, tri_factor, precision=precise) - 0.5 * jnp.einsum('iTk,kl->iTl', vectors, middle, precision=precise)
    w_halves = w_blocks.reshape(blocks, 2, half_size, K)

    def update_row(block_row):
        is_lower, low_block, high_block, which, weight = geometry(block_row)
        left = jnp.concatenate([vec_halves[high_block, which], w_halves[high_block, which]], -1)
        right = jnp.concatenate([w_blocks[low_block], vectors[low_block]], -1)
        return stored[block_row] - jnp.einsum('qhk,qTk->qhT', left, right, precision=precise)
    new_stored = lax.map(update_row, index)
    new_halves = new_stored.reshape(2, N_ROW, blocks, half_size, TILE).transpose(0, 1, 3, 2, 4).reshape(2, N_ROW * half_size, blocks * TILE)
    left_rest = jnp.concatenate([vec_halves[:, 1], w_halves[:, 1]], -1)
    right_rest = jnp.concatenate([w_blocks, vectors], -1)
    new_rest = rest - jnp.einsum('ihk,iTk->ihT', left_rest, right_rest, precision=precise)
    return (new_halves, new_rest.reshape(blocks * half_size, TILE), w_blocks.reshape(blocks * TILE, K))
```

```python
import functools

import jax
import jax.numpy as jnp
from jax import lax
from jax.experimental import pallas as pl
from jax.experimental.pallas import tpu as pltpu
from jax.sharding import PartitionSpec as P

MESH = pl.DeviceIdType.MESH
NN = (((1,), (0,)), ((), ()))
TN = (((0,), (0,)), ((), ()))
NT = (((1,), (1,)), ((), ()))
TILE = 1024
HALF = 512
WIDTH = 256
UNIT = 256
PIECE = 128
REST = 64


def split(value):
    high = value.astype(jnp.bfloat16)
    low = (value - high.astype(jnp.float32)).astype(jnp.bfloat16)
    return high, low


def product(left, right, dims):
    def dot(a, b):
        return lax.dot_general(a, b, dims, preferred_element_type=jnp.float32)

    return dot(left[0], right[0]) + (dot(left[0], right[1]) + dot(left[1], right[0]))


def rows(start, size):
    return pl.ds(pl.multiple_of(start, 8), size)


def place():
    row, col = lax.axis_index("row"), lax.axis_index("col")
    return dict(row=row, col=col, x=row // 2, lo=row % 2, z=col // 4, hi=(col // 2) % 2, core=col % 2)


def at(x, lo, z, hi, core):
    return (x * 2 + lo, z * 4 + hi * 2 + core)


def moved(me, x=0, y=0, z=0, core=0):
    y_at = (me["hi"] * 2 + me["lo"] + y) % 4
    return at((me["x"] + x) % 4, y_at % 2, (me["z"] + z) % 4, y_at // 2, (me["core"] + core) % 2)


class Copies:
    def __init__(self, send_sems, recv_sems):
        self.send_sems, self.recv_sems, self.used, self.started = send_sems, recv_sems, 0, []

    def make(self, source, target, device):
        copy = pltpu.make_async_remote_copy(
            src_ref=source,
            dst_ref=target,
            send_sem=self.send_sems.at[self.used],
            recv_sem=self.recv_sems.at[self.used],
            device_id=device,
            device_id_type=MESH,
        )
        self.used += 1
        return copy

    def start(self, source, target, device):
        copy = self.make(source, target, device)
        copy.start()
        self.started.append(copy)
        return copy

    def finish(self):
        for copy in self.started:
            copy.wait_send()


def ring_scatter(copies, source, out, relay, index, shift, plus, minus):
    def part(step, half):
        return source.at[rows(((index + step + shift) % 4) * UNIT + half * PIECE, PIECE)]

    far_plus = copies.start(part(2, 0), relay.at[0], plus)
    far_minus = copies.start(part(2, 1), relay.at[1], minus)
    near_plus = copies.start(part(1, 1), relay.at[2], plus)
    near_minus = copies.start(part(3, 0), relay.at[3], minus)
    yield
    far_plus.wait_recv()
    relay[6] = relay[0] + part(1, 0)[...]
    sum_plus = copies.start(relay.at[6], relay.at[4], plus)
    far_minus.wait_recv()
    relay[7] = relay[1] + part(3, 1)[...]
    sum_minus = copies.start(relay.at[7], relay.at[5], minus)
    yield
    near_plus.wait_recv()
    near_minus.wait_recv()
    sum_plus.wait_recv()
    sum_minus.wait_recv()
    out[0:PIECE] = part(0, 0)[...] + (relay[4] + relay[3])
    out[PIECE:UNIT] = part(0, 1)[...] + (relay[2] + relay[5])


def ring_gather(copies, block, index, shift, plus, minus, sibling=None):
    def unit(step):
        return block.at[rows(((index + step + shift) % 4) * UNIT, UNIT)]

    def half(step, which):
        return block.at[rows(((index + step + shift) % 4) * UNIT + which * PIECE, PIECE)]

    shared = []

    def share(ref):
        if sibling is not None:
            shared.append(copies.start(ref, ref, sibling))

    to_plus = copies.start(unit(0), unit(0), plus)
    to_minus = copies.start(unit(0), unit(0), minus)
    share(unit(0))
    yield
    to_plus.wait_recv()
    on_plus = copies.start(half(3, 0), half(3, 0), plus)
    to_minus.wait_recv()
    on_minus = copies.start(half(1, 1), half(1, 1), minus)
    share(unit(3))
    share(unit(1))
    yield
    on_plus.wait_recv()
    share(half(2, 0))
    on_minus.wait_recv()
    share(half(2, 1))
    yield
    for copy in shared:
        copy.wait_recv()


def inner_sum(copies, me, partial, total, work):
    first, first_in, second, second_in, third, third_in, fourth_in, fifth, sixth = work
    sibling = moved(me, core=1)
    core, x, y = me["core"], me["x"], me["hi"] * 2 + me["lo"]
    copy = copies.start(partial.at[rows((1 - core) * 128, 128)], first_in, sibling)
    yield
    copy.wait_recv()
    first[...] = partial[rows(core * 128, 128), :] + first_in[...]
    sent = [
        copies.start(first.at[rows(((x + d) % 4) * 32, 32)], second_in.at[d - 1], moved(me, x=d)) for d in (1, 2, 3)
    ]
    yield
    for copy in sent:
        copy.wait_recv()
    second[...] = first[rows(x * 32, 32), :] + second_in[0] + second_in[1] + second_in[2]
    sent = [copies.start(second.at[rows(((y + d) % 4) * 8, 8)], third_in.at[d - 1], moved(me, y=d)) for d in (1, 2, 3)]
    yield
    for copy in sent:
        copy.wait_recv()
    third[...] = second[rows(y * 8, 8), :] + third_in[0] + third_in[1] + third_in[2]
    sent = [copies.start(third, fourth_in.at[d - 1], moved(me, z=d)) for d in (1, 2, 3)]
    yield
    for copy in sent:
        copy.wait_recv()
    mine = fifth.at[rows(y * 8, 8)]
    mine[...] = third[...] + fourth_in[0] + fourth_in[1] + fourth_in[2]
    sent = [copies.start(mine, mine, moved(me, y=d)) for d in (1, 2, 3)]
    yield
    for copy in sent:
        copy.wait_recv()
    mine = sixth.at[rows(x * 32, 32)]
    mine[...] = fifth[...]
    sent = [copies.start(mine, mine, moved(me, x=d)) for d in (1, 2, 3)]
    yield
    for copy in sent:
        copy.wait_recv()
    mine = total.at[rows(core * 128, 128)]
    mine[...] = sixth[...]
    copy = copies.start(mine, mine, sibling)
    yield
    copy.wait_recv()


def step_all(running):
    still = []
    for item in running:
        if next(item, "done") != "done":
            still.append(item)
    return still


def gather_kernel(
    halves_ref, rest_ref, vec_ref, av_col, av_row, vec_row, inner_ref,
    tiles, parts, vec_high, vec_low, partial, row_sum, sibling_in, row_relay, col_relay,
    row_unit, col_unit, pair_in, swap_out, swap_in,
    first, first_in, second, second_in, third, third_in, fourth_in, fifth, sixth,
    load_sem, send_sems, recv_sems,
):
    me = place()
    row, col, core = me["row"], me["col"], me["core"]
    x, lo, z, hi = me["x"], me["lo"], me["z"], me["hi"]
    sibling = moved(me, core=1)

    row_shift = (x - (x // 2 + 2 * core) + 4) % 4
    row_half = (lo + hi + x) % 2
    as_row = (((z + row_shift) % 4) * 2 + row_half, row + 8 * core)
    row_of = col % 8
    as_col = at(row_of // 2, row_of % 2, (x - row_of // 2 + z + 4) % 4, (lo + row_of + hi) % 2, col // 8)
    alone = jnp.logical_and(as_row[0] == row, as_row[1] == col)

    load = pltpu.make_async_copy(halves_ref, tiles, load_sem)
    load.start()

    barrier = pltpu.get_barrier_semaphore()
    near = [moved(me, x=d) for d in (1, 2, 3)] + [moved(me, y=d) for d in (1, 2, 3)]
    near += [moved(me, z=d) for d in (1, 2, 3)] + [sibling]
    for device in near:
        pl.semaphore_signal(barrier, inc=1, device_id=device, device_id_type=MESH)

    @pl.when(jnp.logical_not(alone))
    def _():
        for device in (as_row, as_col):
            pl.semaphore_signal(barrier, inc=1, device_id=device, device_id_type=MESH)

    pl.semaphore_wait(barrier, len(near) + jnp.where(alone, 0, 2).astype(jnp.int32))

    copies = Copies(send_sems, recv_sems)
    z_ring = (z, row_shift, moved(me, z=1), moved(me, z=3))
    x_ring = (x, 0, moved(me, x=1), moved(me, x=3))

    own_rows = rows(x * UNIT, UNIT)
    mine_row = rows(((z + row_shift) % 4) * UNIT, UNIT)
    vec_block = vec_row.at[core]
    unit_copy = copies.make(vec_ref.at[own_rows], row_unit, as_col)

    @pl.when(jnp.logical_not(alone))
    def _():
        unit_copy.start()

    @pl.when(alone)
    def _():
        row_unit[...] = vec_ref[own_rows, :]

    parts[...] = jnp.zeros_like(parts)
    partial[...] = jnp.zeros_like(partial)
    vec_high[0], vec_low[0] = split(vec_ref[...])

    @pl.when(jnp.logical_not(alone))
    def _():
        unit_copy.wait_recv()
        unit_copy.wait_send()

    vec_block[mine_row, :] = row_unit[...]
    running = [ring_gather(copies, vec_block, *z_ring, sibling)]
    while running:
        running = step_all(running)
    for position in range(2):
        vec_high[1 + position], vec_low[1 + position] = split(vec_row[position])
    load.wait()

    def tile_rows(at_step, carry):
        position, chunk = at_step // 2, at_step % 2
        block_row = row + 8 * position
        is_lower = block_row >= col
        weight = jnp.where(block_row == col, 0.5, 1.0).astype(jnp.float32)
        offset = jnp.where(is_lower, 0, HALF) + chunk * UNIT
        low_at = jnp.where(is_lower, 0, 1 + position)
        high_at = jnp.where(is_lower, 1 + position, 0)
        block = split(tiles[position, rows(chunk * UNIT, UNIT), :])
        high_rows = rows(offset, UNIT)
        upper = (vec_high[high_at, high_rows, :], vec_low[high_at, high_rows, :])
        along = product(block, (vec_high[low_at], vec_low[low_at]), NN) * weight
        parts[high_at, high_rows, :] += along
        partial[...] += product(upper, split(along), TN)
        parts[low_at] += product(block, upper, TN) * weight
        return carry

    lax.fori_loop(0, 4, tile_rows, 0)
    rest_rows = rows(HALF + row * REST, REST)
    block = split(rest_ref[...])
    upper = (vec_high[0, rest_rows, :], vec_low[0, rest_rows, :])
    along = product(block, (vec_high[0], vec_low[0]), NN) * 0.5
    parts[0, rest_rows, :] += along
    partial[...] += product(upper, split(along), TN)
    parts[0] += product(block, upper, TN) * 0.5

    inner = inner_sum(
        copies, me, partial, inner_ref, (first, first_in, second, second_in, third, third_in, fourth_in, fifth, sixth)
    )
    pair = copies.start(parts.at[2 - core], sibling_in, sibling)
    columns = ring_scatter(copies, parts.at[0], col_unit, col_relay, *x_ring)
    next(columns)
    next(inner)
    pair.wait_recv()
    row_sum[...] = parts[1 + core] + sibling_in[...]
    running = [ring_scatter(copies, row_sum, row_unit, row_relay, *z_ring), columns, inner]
    while len(running) > 1:
        running = step_all(running)

    keep_row, keep_col = rows(row_half * PIECE, PIECE), rows(lo * PIECE, PIECE)
    give_row, give_col = rows((1 - row_half) * PIECE, PIECE), rows((1 - lo) * PIECE, PIECE)
    row_partner = moved(me, y=2)
    col_partner = at(x, 1 - lo, z, hi, core)
    row_copy = copies.start(row_unit.at[give_row], pair_in.at[0], row_partner)
    col_copy = copies.start(col_unit.at[give_col], pair_in.at[1], col_partner)
    step_all(running)
    row_copy.wait_recv()
    swap_out[0] = row_unit[keep_row, :] + pair_in[0]
    col_copy.wait_recv()
    swap_out[1] = col_unit[keep_col, :] + pair_in[1]
    row_copy = copies.make(swap_out.at[0], swap_in.at[0], as_row)
    col_copy = copies.make(swap_out.at[1], swap_in.at[1], as_col)

    @pl.when(jnp.logical_not(alone))
    def _():
        row_copy.start()
        col_copy.start()

    @pl.when(alone)
    def _():
        swap_in[...] = swap_out[...]

    step_all(running)

    @pl.when(jnp.logical_not(alone))
    def _():
        row_copy.wait()
        col_copy.wait()

    row_piece = av_row.at[core, rows(((z + row_shift) % 4) * UNIT + row_half * PIECE, PIECE)]
    col_piece = av_col.at[rows(x * UNIT + lo * PIECE, PIECE)]
    row_piece[...] = swap_out[0] + swap_in[1]
    col_piece[...] = swap_out[1] + swap_in[0]
    row_copy = copies.start(row_piece, row_piece, row_partner)
    col_copy = copies.start(col_piece, col_piece, col_partner)
    step_all(running)
    row_copy.wait_recv()
    col_copy.wait_recv()
    running = [
        ring_gather(copies, av_row.at[core], *z_ring, sibling),
        ring_gather(copies, av_col, *x_ring),
    ] + running
    while running:
        running = step_all(running)
    copies.finish()


def update_kernel(
    halves_ref, rest_ref, vec_ref, vec_row, av_col, av_row, inner_ref, tri_ref,
    out_ref, out_rest, out_w, vec_high, vec_low, w_high, w_low,
):
    row, col = lax.axis_index("row"), lax.axis_index("col")
    position, chunk = pl.program_id(0), pl.program_id(1)

    @pl.when(jnp.logical_and(position == 0, chunk == 0))
    def _():
        inner = inner_ref[...]
        tri = split(tri_ref[...])
        inner = inner + inner.T
        middle = product(tri, split(inner), TN)
        middle = split(product(split(middle), tri, NN) * 0.5)

        def block(at_step, carry):
            which, part = at_step // 4, at_step % 4
            here = rows(part * UNIT, UNIT)
            behind = jnp.maximum(which - 1, 0)
            own = which == 0
            vec = jnp.where(own, vec_ref[here, :], vec_row[behind, here, :])
            av = jnp.where(own, av_col[here, :], av_row[behind, here, :])
            vec = split(vec)
            w = product(split(av), tri, NN) - product(vec, middle, NN)
            vec_high[which, here, :], vec_low[which, here, :] = vec
            w_high[which, here, :], w_low[which, here, :] = split(w)

            @pl.when(own)
            def _():
                out_w[here, :] = w

            return carry

        lax.fori_loop(0, 12, block, 0)
        rest_rows = rows(HALF + row * REST, REST)
        update = product(
            (vec_high[0, rest_rows, :], vec_low[0, rest_rows, :]), (w_high[0], w_low[0]), NT
        ) + product((w_high[0, rest_rows, :], w_low[0, rest_rows, :]), (vec_high[0], vec_low[0]), NT)
        out_rest[...] = rest_ref[...] - update

    is_lower = row + 8 * position >= col
    size = halves_ref.shape[1]
    high_rows = rows(jnp.where(is_lower, 0, HALF) + chunk * size, size)
    low_at = jnp.where(is_lower, 0, 1 + position)
    high_at = jnp.where(is_lower, 1 + position, 0)
    update = product(
        (vec_high[high_at, high_rows, :], vec_low[high_at, high_rows, :]), (w_high[low_at], w_low[low_at]), NT
    ) + product((w_high[high_at, high_rows, :], w_low[high_at, high_rows, :]), (vec_high[low_at], vec_low[low_at]), NT)
    out_ref[0] = halves_ref[0] - update


def shards(halves, diag_rest, panel_vectors, tri_factor):
    vmem = pl.BlockSpec(memory_space=pltpu.VMEM)
    whole = pl.BlockSpec(memory_space=pl.ANY)
    f32 = jnp.float32
    block = (TILE, WIDTH)

    def buffer(*shape):
        return pltpu.VMEM(shape, f32)

    av_col, av_row, vec_row, inner = pl.pallas_call(
        gather_kernel,
        out_shape=[
            jax.ShapeDtypeStruct(block, f32),
            jax.ShapeDtypeStruct((2,) + block, f32),
            jax.ShapeDtypeStruct((2,) + block, f32),
            jax.ShapeDtypeStruct((WIDTH, WIDTH), f32),
        ],
        in_specs=[whole, vmem, vmem],
        out_specs=[vmem] * 4,
        scratch_shapes=[
            buffer(2, HALF, TILE),
            buffer(3, TILE, WIDTH),
            pltpu.VMEM((3, TILE, WIDTH), jnp.bfloat16),
            pltpu.VMEM((3, TILE, WIDTH), jnp.bfloat16),
            buffer(WIDTH, WIDTH),
            buffer(TILE, WIDTH),
            buffer(TILE, WIDTH),
            buffer(8, PIECE, WIDTH),
            buffer(8, PIECE, WIDTH),
            buffer(UNIT, WIDTH),
            buffer(UNIT, WIDTH),
            buffer(2, PIECE, WIDTH),
            buffer(2, PIECE, WIDTH),
            buffer(2, PIECE, WIDTH),
            buffer(128, WIDTH),
            buffer(128, WIDTH),
            buffer(32, WIDTH),
            buffer(3, 32, WIDTH),
            buffer(8, WIDTH),
            buffer(3, 8, WIDTH),
            buffer(3, 8, WIDTH),
            buffer(32, WIDTH),
            buffer(128, WIDTH),
            pltpu.SemaphoreType.DMA,
            pltpu.SemaphoreType.DMA((64,)),
            pltpu.SemaphoreType.DMA((64,)),
        ],
        compiler_params=pltpu.CompilerParams(
            collective_id=0, has_side_effects=True, vmem_limit_bytes=50 * 2**20
        ),
        name="gather",
    )(halves, diag_rest, panel_vectors)

    size = 128
    steps = HALF // size
    tile_block = pl.BlockSpec((1, size, TILE), lambda i, j: (i, j, 0))

    def fixed(*shape):
        return pl.BlockSpec(shape, lambda i, j: (0,) * len(shape))

    return pl.pallas_call(
        update_kernel,
        grid=(2, steps),
        out_shape=[
            jax.ShapeDtypeStruct(halves.shape, f32),
            jax.ShapeDtypeStruct(diag_rest.shape, f32),
            jax.ShapeDtypeStruct(panel_vectors.shape, f32),
        ],
        in_specs=[
            tile_block,
            fixed(REST, TILE),
            fixed(*block),
            fixed(2, *block),
            fixed(*block),
            fixed(2, *block),
            fixed(WIDTH, WIDTH),
            fixed(WIDTH, WIDTH),
        ],
        out_specs=[tile_block, fixed(REST, TILE), fixed(*block)],
        scratch_shapes=[pltpu.VMEM((3, TILE, WIDTH), jnp.bfloat16)] * 4,
        compiler_params=pltpu.CompilerParams(vmem_limit_bytes=50 * 2**20),
        name="update",
    )(halves, diag_rest, panel_vectors, vec_row, av_col, av_row, inner, tri_factor)


def solution(mesh):
    return jax.shard_map(
        shards,
        mesh=mesh,
        in_specs=(P(None, "row", "col"), P(("col", "row"), None), P("col", None), P()),
        out_specs=(P(None, "row", "col"), P(("col", "row"), None), P("col", None)),
        check_vma=False,
    )
```

```python
import functools

import jax
import jax.numpy as jnp
from jax import lax
from jax.experimental import pallas as pl
from jax.experimental.pallas import tpu as pltpu
from jax.sharding import PartitionSpec as P

MESH = pl.DeviceIdType.MESH
NN = (((1,), (0,)), ((), ()))
TN = (((0,), (0,)), ((), ()))
NT = (((1,), (1,)), ((), ()))
TILE = 1024
HALF = 512
WIDTH = 256
UNIT = 256
PIECE = 128
REST = 64


def split(value):
    high = value.astype(jnp.bfloat16)
    low = (value - high.astype(jnp.float32)).astype(jnp.bfloat16)
    return high, low


def product(left, right, dims):
    def dot(a, b):
        return lax.dot_general(a, b, dims, preferred_element_type=jnp.float32)

    return dot(left[0], right[0]) + (dot(left[0], right[1]) + dot(left[1], right[0]))


def rows(start, size):
    return pl.ds(pl.multiple_of(start, 8), size)


def place():
    row, col = lax.axis_index("row"), lax.axis_index("col")
    return dict(row=row, col=col, x=row // 2, lo=row % 2, z=col // 4, hi=(col // 2) % 2, core=col % 2)


def at(x, lo, z, hi, core):
    return (x * 2 + lo, z * 4 + hi * 2 + core)


def moved(me, x=0, y=0, z=0, core=0):
    y_at = (me["hi"] * 2 + me["lo"] + y) % 4
    return at((me["x"] + x) % 4, y_at % 2, (me["z"] + z) % 4, y_at // 2, (me["core"] + core) % 2)


class Copies:
    def __init__(self, send_sems, recv_sems):
        self.send_sems, self.recv_sems, self.used, self.started = send_sems, recv_sems, 0, []

    def make(self, source, target, device):
        copy = pltpu.make_async_remote_copy(
            src_ref=source,
            dst_ref=target,
            send_sem=self.send_sems.at[self.used],
            recv_sem=self.recv_sems.at[self.used],
            device_id=device,
            device_id_type=MESH,
        )
        self.used += 1
        return copy

    def start(self, source, target, device):
        copy = self.make(source, target, device)
        copy.start()
        self.started.append(copy)
        return copy

    def finish(self):
        for copy in self.started:
            copy.wait_send()


def ring_scatter(copies, source, out, relay, index, shift, plus, minus):
    def part(step, half):
        return source.at[rows(((index + step + shift) % 4) * UNIT + half * PIECE, PIECE)]

    far_plus = copies.start(part(2, 0), relay.at[0], plus)
    far_minus = copies.start(part(2, 1), relay.at[1], minus)
    near_plus = copies.start(part(1, 1), relay.at[2], plus)
    near_minus = copies.start(part(3, 0), relay.at[3], minus)
    yield
    far_plus.wait_recv()
    relay[6] = relay[0] + part(1, 0)[...]
    sum_plus = copies.start(relay.at[6], relay.at[4], plus)
    far_minus.wait_recv()
    relay[7] = relay[1] + part(3, 1)[...]
    sum_minus = copies.start(relay.at[7], relay.at[5], minus)
    yield
    near_plus.wait_recv()
    near_minus.wait_recv()
    sum_plus.wait_recv()
    sum_minus.wait_recv()
    out[0:PIECE] = part(0, 0)[...] + (relay[4] + relay[3])
    out[PIECE:UNIT] = part(0, 1)[...] + (relay[2] + relay[5])


def ring_gather(copies, block, index, shift, plus, minus, kept, partner, sibling=None):
    def piece(step, which):
        return block.at[rows(((index + step + shift) % 4) * UNIT + which * PIECE, PIECE)]

    given = 1 - kept
    shared = []

    def share(ref):
        if sibling is not None:
            shared.append(copies.start(ref, ref, sibling))

    def send(ref, device):
        return copies.start(ref, ref, device)

    own = piece(0, kept)
    pair = send(own, partner)
    own_plus, own_minus = send(own, plus), send(own, minus)
    share(own)
    yield
    pair.wait_recv()
    other = piece(0, given)
    other_plus, other_minus = send(other, plus), send(other, minus)
    share(other)
    yield
    own_plus.wait_recv()
    far_plus = send(piece(3, kept), plus)
    share(piece(3, kept))
    own_minus.wait_recv()
    share(piece(1, kept))
    yield
    other_minus.wait_recv()
    far_minus = send(piece(1, given), minus)
    share(piece(1, given))
    other_plus.wait_recv()
    share(piece(3, given))
    yield
    far_plus.wait_recv()
    share(piece(2, kept))
    far_minus.wait_recv()
    share(piece(2, given))
    yield
    for copy in shared:
        copy.wait_recv()


ORDER = (0, 4, 1, 5, 2, 6, 3, 7)


class Spread:
    def __init__(self, me, vec_ref, vec_row, send_sems, recv_sems):
        x, lo, z, hi, core = me["x"], me["lo"], me["z"], me["hi"], me["core"]
        self.vec_ref, self.vec_row, self.send_sems, self.recv_sems = vec_ref, vec_row, send_sems, recv_sems
        self.lead = core == lo
        line = hi == x % 2
        end = z % 2 == x // 2
        self.source = jnp.logical_and(jnp.logical_and(self.lead, line), end)
        self.cross = jnp.logical_and(jnp.logical_and(jnp.logical_not(self.lead), line), end)
        self.target = jnp.logical_and(jnp.logical_and(self.lead, jnp.logical_not(line)), end)
        self.ends = jnp.logical_and(self.lead, end)
        self.middle = jnp.logical_and(self.lead, jnp.logical_not(end))
        self.follow = jnp.logical_not(self.lead)
        self.plus, self.minus, self.sibling = moved(me, z=1), moved(me, z=3), moved(me, core=1)
        self.over = at(x, core, z, 1 - hi, core)
        self.own = z // 2
        self.from_minus = ((z + 3) % 4) // 2

    def chunk(self, block, c):
        return self.vec_row.at[block, pl.ds(c * PIECE, PIECE)]

    def copy(self, slot, source, target, device):
        return pltpu.make_async_remote_copy(
            src_ref=source,
            dst_ref=target,
            send_sem=self.send_sems.at[slot],
            recv_sem=self.recv_sems.at[slot],
            device_id=device,
            device_id_type=MESH,
        )

    def mine(self, c):
        return self.vec_ref.at[pl.ds(c * PIECE, PIECE)]

    def along(self, c, block, source=None):
        here = self.chunk(block, c)
        return self.copy(c, here if source is None else source, here, self.plus)

    def back(self, c, block, source=None):
        here = self.chunk(block, c)
        return self.copy(8 + c, here if source is None else source, here, self.minus)

    def across(self, c):
        return self.copy(16 + c, self.mine(c), self.chunk(self.own, c), self.over)

    def share(self, c, block, which, source=None):
        here = self.chunk(block, c)
        return self.copy(24 + 8 * which + c, here if source is None else source, here, self.sibling)

    def begin(self):
        @pl.when(self.source)
        def _():
            for c in ORDER:
                self.along(c, self.own, self.mine(c)).start()
                self.back(c, self.own, self.mine(c)).start()
                self.share(c, self.own, 0, self.mine(c)).start()
            self.vec_row[self.own] = self.vec_ref[...]

        @pl.when(self.cross)
        def _():
            for c in ORDER:
                self.across(c).start()

    def serve(self, step):
        c = ORDER[step]

        @pl.when(self.target)
        def _():
            self.across(c).wait_recv()
            self.along(c, self.own).start()
            self.back(c, self.own).start()
            self.share(c, self.own, 0).start()

        @pl.when(self.middle)
        def _():
            block = self.from_minus
            self.along(c, block).wait_recv()
            if c < 4:
                self.along(c, block).start()
            self.share(c, block, 0).start()
            self.back(c, 1 - block).wait_recv()
            if c >= 4:
                self.back(c, 1 - block).start()
            self.share(c, 1 - block, 1).start()

    def end(self):
        @pl.when(self.ends)
        def _():
            for c in ORDER:
                copy = self.along(c, 1 - self.own) if c < 4 else self.back(c, 1 - self.own)
                copy.wait_recv()
                self.share(c, 1 - self.own, 1).start()

        @pl.when(self.follow)
        def _():
            for c in ORDER:
                for which in range(2):
                    self.share(c, which, which).wait_recv()

    def finish(self):
        @pl.when(self.ends)
        def _():
            for c in ORDER:
                self.along(c, self.own).wait_send()
                self.back(c, self.own).wait_send()

        @pl.when(self.middle)
        def _():
            for c in ORDER:
                if c < 4:
                    self.along(c, 0).wait_send()
                else:
                    self.back(c, 0).wait_send()

        @pl.when(self.lead)
        def _():
            for c in ORDER:
                for which in range(2):
                    self.share(c, which, which).wait_send()

        @pl.when(self.cross)
        def _():
            for c in ORDER:
                self.across(c).wait_send()


def inner_sum(copies, me, partial, total, work):
    first, first_in, second, second_in, third, third_in, fourth_in, fifth, sixth = work
    sibling = moved(me, core=1)
    core, x, y = me["core"], me["x"], me["hi"] * 2 + me["lo"]
    copy = copies.start(partial.at[rows((1 - core) * 128, 128)], first_in, sibling)
    yield
    copy.wait_recv()
    first[...] = partial[rows(core * 128, 128), :] + first_in[...]
    sent = [
        copies.start(first.at[rows(((x + d) % 4) * 32, 32)], second_in.at[d - 1], moved(me, x=d)) for d in (1, 2, 3)
    ]
    yield
    for copy in sent:
        copy.wait_recv()
    second[...] = first[rows(x * 32, 32), :] + second_in[0] + second_in[1] + second_in[2]
    sent = [copies.start(second.at[rows(((y + d) % 4) * 8, 8)], third_in.at[d - 1], moved(me, y=d)) for d in (1, 2, 3)]
    yield
    for copy in sent:
        copy.wait_recv()
    third[...] = second[rows(y * 8, 8), :] + third_in[0] + third_in[1] + third_in[2]
    sent = [copies.start(third, fourth_in.at[d - 1], moved(me, z=d)) for d in (1, 2, 3)]
    yield
    for copy in sent:
        copy.wait_recv()
    mine = fifth.at[rows(y * 8, 8)]
    mine[...] = third[...] + fourth_in[0] + fourth_in[1] + fourth_in[2]
    sent = [copies.start(mine, mine, moved(me, y=d)) for d in (1, 2, 3)]
    yield
    for copy in sent:
        copy.wait_recv()
    mine = sixth.at[rows(x * 32, 32)]
    mine[...] = fifth[...]
    sent = [copies.start(mine, mine, moved(me, x=d)) for d in (1, 2, 3)]
    yield
    for copy in sent:
        copy.wait_recv()
    mine = total.at[rows(core * 128, 128)]
    mine[...] = sixth[...]
    copy = copies.start(mine, mine, sibling)
    yield
    copy.wait_recv()


def step_all(running):
    still = []
    for item in running:
        if next(item, "done") != "done":
            still.append(item)
    return still


def gather_kernel(
    halves_ref, rest_ref, vec_ref, av_col, av_row, vec_row, inner_ref,
    tiles, tile_high, tile_low, parts, rest_part, vec_high, vec_low, partial, row_sum, sibling_in, row_relay, col_relay,
    row_unit, col_unit, pair_in, swap_out, swap_in,
    first, first_in, second, second_in, third, third_in, fourth_in, fifth, sixth,
    load_sem, send_sems, recv_sems, vec_send_sems, vec_recv_sems,
):
    me = place()
    row, col, core = me["row"], me["col"], me["core"]
    x, lo, z, hi = me["x"], me["lo"], me["z"], me["hi"]
    sibling = moved(me, core=1)

    row_shift = (x - (x // 2 + 2 * core) + 4) % 4
    row_half = (lo + hi + x) % 2
    as_row = (((z + row_shift) % 4) * 2 + row_half, row + 8 * core)
    row_of = col % 8
    as_col = at(row_of // 2, row_of % 2, (x - row_of // 2 + z + 4) % 4, (lo + row_of + hi) % 2, col // 8)
    alone = jnp.logical_and(as_row[0] == row, as_row[1] == col)

    load = pltpu.make_async_copy(halves_ref, tiles, load_sem)
    load.start()

    barrier = pltpu.get_barrier_semaphore()
    near = [moved(me, x=d) for d in (1, 2, 3)] + [moved(me, y=d) for d in (1, 2, 3)]
    near += [moved(me, z=d) for d in (1, 2, 3)] + [sibling]
    for device in near:
        pl.semaphore_signal(barrier, inc=1, device_id=device, device_id_type=MESH)

    @pl.when(jnp.logical_not(alone))
    def _():
        for device in (as_row, as_col):
            pl.semaphore_signal(barrier, inc=1, device_id=device, device_id_type=MESH)

    pl.semaphore_wait(barrier, len(near) + jnp.where(alone, 0, 2).astype(jnp.int32))

    copies = Copies(send_sems, recv_sems)
    z_ring = (z, row_shift, moved(me, z=1), moved(me, z=3))
    x_ring = (x, 0, moved(me, x=1), moved(me, x=3))
    spread = Spread(me, vec_ref, vec_row, vec_send_sems, vec_recv_sems)
    spread.begin()
    vec_high[0], vec_low[0] = split(vec_ref[...])
    load.wait()

    def facts(position):
        block_row = row + 8 * position
        return block_row >= col, jnp.where(block_row == col, 0.5, 1.0).astype(jnp.float32)

    def upper(which):
        return vec_high[which, 0:HALF], vec_low[which, 0:HALF]

    def lower(which):
        return vec_high[which, HALF:TILE], vec_low[which, HALF:TILE]

    def whole(which):
        return vec_high[which], vec_low[which]

    def row_part(position):
        is_lower, weight = facts(position)
        tile_high[position], tile_low[position] = split(tiles[position])
        tile = tile_high.at[position], tile_low.at[position]

        @pl.when(is_lower)
        def _():
            parts[1 + position, 0:HALF] = product((tile[0][...], tile[1][...]), whole(0), NN) * weight
            parts[1 + position, HALF:TILE] = jnp.zeros((HALF, WIDTH), jnp.float32)

        @pl.when(jnp.logical_not(is_lower))
        def _():
            parts[1 + position] = product((tile[0][...], tile[1][...]), lower(0), TN)

    def col_part(position):
        is_lower, weight = facts(position)
        tile = tile_high.at[position], tile_low.at[position]

        @pl.when(is_lower)
        def _():
            parts[0] += product((tile[0][...], tile[1][...]), upper(1 + position), TN) * weight

        @pl.when(jnp.logical_not(is_lower))
        def _():
            parts[0, HALF:TILE] += product((tile[0][...], tile[1][...]), whole(1 + position), NN)

    row_part(1 - core)
    pair = copies.start(parts.at[2 - core], sibling_in, sibling)
    spread.serve(0)
    row_part(core)
    spread.serve(1)
    spread.serve(2)
    rest_rows = rows(HALF + row * REST, REST)
    block = split(rest_ref[...])
    rest_part[...] = product(block, whole(0), NN) * 0.5
    parts[0] = product(block, (vec_high[0, rest_rows, :], vec_low[0, rest_rows, :]), TN) * 0.5
    spread.serve(3)
    spread.serve(4)
    pair.wait_recv()
    row_sum[...] = parts[1 + core] + sibling_in[...]
    for step in (5, 6, 7):
        spread.serve(step)
    row_scatter = ring_scatter(copies, row_sum, row_unit, row_relay, *z_ring)
    next(row_scatter)
    spread.end()
    for position in range(2):
        vec_high[1 + position], vec_low[1 + position] = split(vec_row[position])
    col_part(0)
    next(row_scatter)
    col_part(1)
    partial[...] = product(whole(0), split(parts[0]), TN)
    parts[0, rest_rows, :] += rest_part[...]
    columns = ring_scatter(copies, parts.at[0], col_unit, col_relay, *x_ring)
    next(columns)
    inner = inner_sum(
        copies, me, partial, inner_ref, (first, first_in, second, second_in, third, third_in, fourth_in, fifth, sixth)
    )
    next(inner)
    step_all([row_scatter])

    keep_row, keep_col = rows(row_half * PIECE, PIECE), rows(lo * PIECE, PIECE)
    give_row, give_col = rows((1 - row_half) * PIECE, PIECE), rows((1 - lo) * PIECE, PIECE)
    row_partner = moved(me, y=2)
    col_partner = at(x, 1 - lo, z, hi, core)
    row_copy = copies.start(row_unit.at[give_row], pair_in.at[0], row_partner)
    next(inner)
    next(columns)
    row_copy.wait_recv()
    swap_out[...] = row_unit[keep_row, :] + pair_in[0]
    row_copy = copies.make(swap_out, swap_in, as_row)

    @pl.when(jnp.logical_not(alone))
    def _():
        row_copy.start()

    @pl.when(alone)
    def _():
        swap_in[...] = swap_out[...]

    next(inner)
    step_all([columns])
    col_copy = copies.start(col_unit.at[give_col], pair_in.at[1], col_partner)
    next(inner)
    col_copy.wait_recv()

    @pl.when(jnp.logical_not(alone))
    def _():
        row_copy.wait()

    col_rows = rows(x * UNIT + lo * PIECE, PIECE)
    col_piece = av_col.at[col_rows]
    col_piece[...] = col_unit[keep_col, :] + pair_in[1] + swap_in[...]
    row_copy = copies.make(col_piece, av_row.at[col // 8, col_rows], as_col)

    @pl.when(jnp.logical_not(alone))
    def _():
        row_copy.start()

    @pl.when(alone)
    def _():
        av_row[col // 8, col_rows, :] = col_piece[...]

    columns = ring_gather(copies, av_col, *x_ring, lo, col_partner)
    next(columns)
    next(inner)

    @pl.when(jnp.logical_not(alone))
    def _():
        row_copy.wait()

    rows_in = ring_gather(copies, av_row.at[core], *z_ring, row_half, row_partner, sibling)
    next(rows_in)
    running = [columns, rows_in, inner]
    while running:
        running = step_all(running)
    copies.finish()
    spread.finish()


def update_kernel(
    halves_ref, rest_ref, vec_ref, vec_row, av_col, av_row, inner_ref, tri_ref,
    out_ref, out_rest, out_w, vec_high, vec_low, w_high, w_low,
):
    row, col = lax.axis_index("row"), lax.axis_index("col")
    position, chunk = pl.program_id(0), pl.program_id(1)

    @pl.when(jnp.logical_and(position == 0, chunk == 0))
    def _():
        inner = inner_ref[...]
        tri = split(tri_ref[...])
        inner = inner + inner.T
        middle = product(tri, split(inner), TN)
        middle = split(product(split(middle), tri, NN) * 0.5)

        def block(at_step, carry):
            which, part = at_step // 2, at_step % 2
            here = rows(part * HALF, HALF)
            behind = jnp.maximum(which - 1, 0)
            own = which == 0
            vec = jnp.where(own, vec_ref[here, :], vec_row[behind, here, :])
            av = jnp.where(own, av_col[here, :], av_row[behind, here, :])
            vec = split(vec)
            w = product(split(av), tri, NN) - product(vec, middle, NN)
            vec_high[which, here, :], vec_low[which, here, :] = vec
            w_high[which, here, :], w_low[which, here, :] = split(w)

            @pl.when(own)
            def _():
                out_w[here, :] = w

            return carry

        lax.fori_loop(0, 6, block, 0)
        rest_rows = rows(HALF + row * REST, REST)
        update = product(
            (vec_high[0, rest_rows, :], vec_low[0, rest_rows, :]), (w_high[0], w_low[0]), NT
        ) + product((w_high[0, rest_rows, :], w_low[0, rest_rows, :]), (vec_high[0], vec_low[0]), NT)
        out_rest[...] = rest_ref[...] - update

    is_lower = row + 8 * position >= col
    size = halves_ref.shape[2]
    high_rows, low_rows = rows(jnp.where(is_lower, 0, HALF), HALF), rows(chunk * size, size)
    low_at = jnp.where(is_lower, 0, 1 + position)
    high_at = jnp.where(is_lower, 1 + position, 0)
    update = product(
        (vec_high[high_at, high_rows, :], vec_low[high_at, high_rows, :]),
        (w_high[low_at, low_rows, :], w_low[low_at, low_rows, :]),
        NT,
    ) + product(
        (w_high[high_at, high_rows, :], w_low[high_at, high_rows, :]),
        (vec_high[low_at, low_rows, :], vec_low[low_at, low_rows, :]),
        NT,
    )
    out_ref[0] = halves_ref[0] - update


def shards(halves, diag_rest, panel_vectors, tri_factor):
    vmem = pl.BlockSpec(memory_space=pltpu.VMEM)
    whole = pl.BlockSpec(memory_space=pl.ANY)
    f32 = jnp.float32
    block = (TILE, WIDTH)

    def buffer(*shape):
        return pltpu.VMEM(shape, f32)

    av_col, av_row, vec_row, inner = pl.pallas_call(
        gather_kernel,
        out_shape=[
            jax.ShapeDtypeStruct(block, f32),
            jax.ShapeDtypeStruct((2,) + block, f32),
            jax.ShapeDtypeStruct((2,) + block, f32),
            jax.ShapeDtypeStruct((WIDTH, WIDTH), f32),
        ],
        in_specs=[whole, vmem, vmem],
        out_specs=[vmem] * 4,
        scratch_shapes=[
            buffer(2, HALF, TILE),
            pltpu.VMEM((2, HALF, TILE), jnp.bfloat16),
            pltpu.VMEM((2, HALF, TILE), jnp.bfloat16),
            buffer(3, TILE, WIDTH),
            buffer(REST, WIDTH),
            pltpu.VMEM((3, TILE, WIDTH), jnp.bfloat16),
            pltpu.VMEM((3, TILE, WIDTH), jnp.bfloat16),
            buffer(WIDTH, WIDTH),
            buffer(TILE, WIDTH),
            buffer(TILE, WIDTH),
            buffer(8, PIECE, WIDTH),
            buffer(8, PIECE, WIDTH),
            buffer(UNIT, WIDTH),
            buffer(UNIT, WIDTH),
            buffer(2, PIECE, WIDTH),
            buffer(PIECE, WIDTH),
            buffer(PIECE, WIDTH),
            buffer(128, WIDTH),
            buffer(128, WIDTH),
            buffer(32, WIDTH),
            buffer(3, 32, WIDTH),
            buffer(8, WIDTH),
            buffer(3, 8, WIDTH),
            buffer(3, 8, WIDTH),
            buffer(32, WIDTH),
            buffer(128, WIDTH),
            pltpu.SemaphoreType.DMA,
            pltpu.SemaphoreType.DMA((80,)),
            pltpu.SemaphoreType.DMA((80,)),
            pltpu.SemaphoreType.DMA((40,)),
            pltpu.SemaphoreType.DMA((40,)),
        ],
        compiler_params=pltpu.CompilerParams(
            collective_id=0, has_side_effects=True, vmem_limit_bytes=50 * 2**20
        ),
        name="gather",
    )(halves, diag_rest, panel_vectors)

    size = 256
    steps = TILE // size
    tile_block = pl.BlockSpec((1, HALF, size), lambda i, j: (i, 0, j))

    def fixed(*shape):
        return pl.BlockSpec(shape, lambda i, j: (0,) * len(shape))

    return pl.pallas_call(
        update_kernel,
        grid=(2, steps),
        out_shape=[
            jax.ShapeDtypeStruct(halves.shape, f32),
            jax.ShapeDtypeStruct(diag_rest.shape, f32),
            jax.ShapeDtypeStruct(panel_vectors.shape, f32),
        ],
        in_specs=[
            tile_block,
            fixed(REST, TILE),
            fixed(*block),
            fixed(2, *block),
            fixed(*block),
            fixed(2, *block),
            fixed(WIDTH, WIDTH),
            fixed(WIDTH, WIDTH),
        ],
        out_specs=[tile_block, fixed(REST, TILE), fixed(*block)],
        scratch_shapes=[pltpu.VMEM((3, TILE, WIDTH), jnp.bfloat16)] * 4,
        compiler_params=pltpu.CompilerParams(vmem_limit_bytes=50 * 2**20),
        name="update",
    )(halves, diag_rest, panel_vectors, vec_row, av_col, av_row, inner, tri_factor)


def solution(mesh):
    return jax.shard_map(
        shards,
        mesh=mesh,
        in_specs=(P(None, "row", "col"), P(("col", "row"), None), P("col", None), P()),
        out_specs=(P(None, "row", "col"), P(("col", "row"), None), P("col", None)),
        check_vma=False,
    )
```

```python
import functools

import jax
import jax.numpy as jnp
from jax import lax
from jax.experimental import pallas as pl
from jax.experimental.pallas import tpu as pltpu
from jax.sharding import PartitionSpec as P

MESH = pl.DeviceIdType.MESH
NN = (((1,), (0,)), ((), ()))
TN = (((0,), (0,)), ((), ()))
NT = (((1,), (1,)), ((), ()))
TILE = 1024
HALF = 512
WIDTH = 256
UNIT = 256
PIECE = 128
REST = 64


def split(value):
    high = value.astype(jnp.bfloat16)
    low = (value - high.astype(jnp.float32)).astype(jnp.bfloat16)
    return high, low


def product(left, right, dims):
    def dot(a, b):
        return lax.dot_general(a, b, dims, preferred_element_type=jnp.float32)

    return dot(left[0], right[0]) + (dot(left[0], right[1]) + dot(left[1], right[0]))


def rows(start, size):
    return pl.ds(pl.multiple_of(start, 8), size)


def place():
    row, col = lax.axis_index("row"), lax.axis_index("col")
    return dict(row=row, col=col, x=row // 2, lo=row % 2, z=col // 4, hi=(col // 2) % 2, core=col % 2)


def at(x, lo, z, hi, core):
    return (x * 2 + lo, z * 4 + hi * 2 + core)


def moved(me, x=0, y=0, z=0, core=0):
    y_at = (me["hi"] * 2 + me["lo"] + y) % 4
    return at((me["x"] + x) % 4, y_at % 2, (me["z"] + z) % 4, y_at // 2, (me["core"] + core) % 2)


class Copies:
    def __init__(self, send_sems, recv_sems):
        self.send_sems, self.recv_sems, self.used, self.started = send_sems, recv_sems, 0, []

    def make(self, source, target, device):
        copy = pltpu.make_async_remote_copy(
            src_ref=source,
            dst_ref=target,
            send_sem=self.send_sems.at[self.used],
            recv_sem=self.recv_sems.at[self.used],
            device_id=device,
            device_id_type=MESH,
        )
        self.used += 1
        return copy

    def start(self, source, target, device):
        copy = self.make(source, target, device)
        copy.start()
        self.started.append(copy)
        return copy

    def finish(self):
        for copy in self.started:
            copy.wait_send()


def ring_scatter(copies, source, out, relay, index, shift, plus, minus):
    def part(step, half):
        return source.at[rows(((index + step + shift) % 4) * UNIT + half * PIECE, PIECE)]

    far_plus = copies.start(part(2, 0), relay.at[0], plus)
    far_minus = copies.start(part(2, 1), relay.at[1], minus)
    near_plus = copies.start(part(1, 1), relay.at[2], plus)
    near_minus = copies.start(part(3, 0), relay.at[3], minus)
    yield
    far_plus.wait_recv()
    relay[6] = relay[0] + part(1, 0)[...]
    sum_plus = copies.start(relay.at[6], relay.at[4], plus)
    far_minus.wait_recv()
    relay[7] = relay[1] + part(3, 1)[...]
    sum_minus = copies.start(relay.at[7], relay.at[5], minus)
    yield
    near_plus.wait_recv()
    near_minus.wait_recv()
    sum_plus.wait_recv()
    sum_minus.wait_recv()
    out[0:PIECE] = part(0, 0)[...] + (relay[4] + relay[3])
    out[PIECE:UNIT] = part(0, 1)[...] + (relay[2] + relay[5])


def ring_gather(copies, block, index, shift, plus, minus, kept, partner, sibling=None):
    def piece(step, which):
        return block.at[rows(((index + step + shift) % 4) * UNIT + which * PIECE, PIECE)]

    given = 1 - kept
    shared = []

    def share(ref):
        if sibling is not None:
            shared.append(copies.start(ref, ref, sibling))

    def send(ref, device):
        return copies.start(ref, ref, device)

    own = piece(0, kept)
    pair = send(own, partner)
    own_plus, own_minus = send(own, plus), send(own, minus)
    share(own)
    yield
    pair.wait_recv()
    other = piece(0, given)
    other_plus, other_minus = send(other, plus), send(other, minus)
    share(other)
    yield
    own_plus.wait_recv()
    far_plus = send(piece(3, kept), plus)
    share(piece(3, kept))
    own_minus.wait_recv()
    share(piece(1, kept))
    yield
    other_minus.wait_recv()
    far_minus = send(piece(1, given), minus)
    share(piece(1, given))
    other_plus.wait_recv()
    share(piece(3, given))
    yield
    far_plus.wait_recv()
    share(piece(2, kept))
    far_minus.wait_recv()
    share(piece(2, given))
    yield
    for copy in shared:
        copy.wait_recv()


ORDER = (0, 4, 1, 5, 2, 6, 3, 7)


class Spread:
    def __init__(self, me, vec_ref, vec_row, send_sems, recv_sems):
        x, lo, z, hi, core = me["x"], me["lo"], me["z"], me["hi"], me["core"]
        self.vec_ref, self.vec_row, self.send_sems, self.recv_sems = vec_ref, vec_row, send_sems, recv_sems
        self.lead = core == lo
        line = hi == x % 2
        end = z % 2 == x // 2
        self.source = jnp.logical_and(jnp.logical_and(self.lead, line), end)
        self.cross = jnp.logical_and(jnp.logical_and(jnp.logical_not(self.lead), line), end)
        self.target = jnp.logical_and(jnp.logical_and(self.lead, jnp.logical_not(line)), end)
        self.ends = jnp.logical_and(self.lead, end)
        self.middle = jnp.logical_and(self.lead, jnp.logical_not(end))
        self.follow = jnp.logical_not(self.lead)
        self.plus, self.minus, self.sibling = moved(me, z=1), moved(me, z=3), moved(me, core=1)
        self.over = at(x, core, z, 1 - hi, core)
        self.own = z // 2
        self.from_minus = ((z + 3) % 4) // 2

    def chunk(self, block, c):
        return self.vec_row.at[block, pl.ds(c * PIECE, PIECE)]

    def copy(self, slot, source, target, device):
        return pltpu.make_async_remote_copy(
            src_ref=source,
            dst_ref=target,
            send_sem=self.send_sems.at[slot],
            recv_sem=self.recv_sems.at[slot],
            device_id=device,
            device_id_type=MESH,
        )

    def mine(self, c):
        return self.vec_ref.at[pl.ds(c * PIECE, PIECE)]

    def along(self, c, block, source=None):
        here = self.chunk(block, c)
        return self.copy(c, here if source is None else source, here, self.plus)

    def back(self, c, block, source=None):
        here = self.chunk(block, c)
        return self.copy(8 + c, here if source is None else source, here, self.minus)

    def across(self, c):
        return self.copy(16 + c, self.mine(c), self.chunk(self.own, c), self.over)

    def share(self, c, block, which, source=None):
        here = self.chunk(block, c)
        return self.copy(24 + 8 * which + c, here if source is None else source, here, self.sibling)

    def begin(self):
        @pl.when(self.source)
        def _():
            for c in ORDER:
                self.along(c, self.own, self.mine(c)).start()
                self.back(c, self.own, self.mine(c)).start()
                self.share(c, self.own, 0, self.mine(c)).start()
            self.vec_row[self.own] = self.vec_ref[...]

        @pl.when(self.cross)
        def _():
            for c in ORDER:
                self.across(c).start()

    def serve(self, step):
        c = ORDER[step]

        @pl.when(self.target)
        def _():
            self.across(c).wait_recv()
            self.along(c, self.own).start()
            self.back(c, self.own).start()
            self.share(c, self.own, 0).start()

        @pl.when(self.middle)
        def _():
            block = self.from_minus
            self.along(c, block).wait_recv()
            if c < 4:
                self.along(c, block).start()
            self.share(c, block, 0).start()
            self.back(c, 1 - block).wait_recv()
            if c >= 4:
                self.back(c, 1 - block).start()
            self.share(c, 1 - block, 1).start()

    def end(self):
        @pl.when(self.ends)
        def _():
            for c in ORDER:
                copy = self.along(c, 1 - self.own) if c < 4 else self.back(c, 1 - self.own)
                copy.wait_recv()
                self.share(c, 1 - self.own, 1).start()

        @pl.when(self.follow)
        def _():
            for c in ORDER:
                for which in range(2):
                    self.share(c, which, which).wait_recv()

    def finish(self):
        @pl.when(self.ends)
        def _():
            for c in ORDER:
                self.along(c, self.own).wait_send()
                self.back(c, self.own).wait_send()

        @pl.when(self.middle)
        def _():
            for c in ORDER:
                if c < 4:
                    self.along(c, 0).wait_send()
                else:
                    self.back(c, 0).wait_send()

        @pl.when(self.lead)
        def _():
            for c in ORDER:
                for which in range(2):
                    self.share(c, which, which).wait_send()

        @pl.when(self.cross)
        def _():
            for c in ORDER:
                self.across(c).wait_send()


def inner_sum(copies, me, partial, total, work):
    first, first_in, second, second_in, third, third_in, fourth_in, fifth, sixth = work
    sibling = moved(me, core=1)
    core, x, y = me["core"], me["x"], me["hi"] * 2 + me["lo"]
    copy = copies.start(partial.at[rows((1 - core) * 128, 128)], first_in, sibling)
    yield
    copy.wait_recv()
    first[...] = partial[rows(core * 128, 128), :] + first_in[...]
    sent = [
        copies.start(first.at[rows(((x + d) % 4) * 32, 32)], second_in.at[d - 1], moved(me, x=d)) for d in (1, 2, 3)
    ]
    yield
    for copy in sent:
        copy.wait_recv()
    second[...] = first[rows(x * 32, 32), :] + second_in[0] + second_in[1] + second_in[2]
    sent = [copies.start(second.at[rows(((y + d) % 4) * 8, 8)], third_in.at[d - 1], moved(me, y=d)) for d in (1, 2, 3)]
    yield
    for copy in sent:
        copy.wait_recv()
    third[...] = second[rows(y * 8, 8), :] + third_in[0] + third_in[1] + third_in[2]
    sent = [copies.start(third, fourth_in.at[d - 1], moved(me, z=d)) for d in (1, 2, 3)]
    yield
    for copy in sent:
        copy.wait_recv()
    mine = fifth.at[rows(y * 8, 8)]
    mine[...] = third[...] + fourth_in[0] + fourth_in[1] + fourth_in[2]
    sent = [copies.start(mine, mine, moved(me, y=d)) for d in (1, 2, 3)]
    yield
    for copy in sent:
        copy.wait_recv()
    mine = sixth.at[rows(x * 32, 32)]
    mine[...] = fifth[...]
    sent = [copies.start(mine, mine, moved(me, x=d)) for d in (1, 2, 3)]
    yield
    for copy in sent:
        copy.wait_recv()
    mine = total.at[rows(core * 128, 128)]
    mine[...] = sixth[...]
    copy = copies.start(mine, mine, sibling)
    yield
    copy.wait_recv()


def step_all(running):
    still = []
    for item in running:
        if next(item, "done") != "done":
            still.append(item)
    return still


def gather_kernel(
    halves_ref, rest_hbm, vec_hbm, tri_hbm, vec_high, vec_low, w_high, w_low, w_ref,
    vec_ref, rest_ref, tri_ref, av_col, av_row, vec_row, inner_ref, vec_middle,
    tiles, tile_high, tile_low, parts, rest_part, partial, row_sum, sibling_in, row_relay, col_relay,
    row_unit, col_unit, pair_in, swap_out, swap_in,
    first, first_in, second, second_in, third, third_in, fourth_in, fifth, sixth,
    load_sems, send_sems, recv_sems, vec_send_sems, vec_recv_sems,
):
    me = place()
    row, col, core = me["row"], me["col"], me["core"]
    x, lo, z, hi = me["x"], me["lo"], me["z"], me["hi"]
    sibling = moved(me, core=1)

    row_shift = (x - (x // 2 + 2 * core) + 4) % 4
    row_half = (lo + hi + x) % 2
    as_row = (((z + row_shift) % 4) * 2 + row_half, row + 8 * core)
    row_of = col % 8
    as_col = at(row_of // 2, row_of % 2, (x - row_of // 2 + z + 4) % 4, (lo + row_of + hi) % 2, col // 8)
    alone = jnp.logical_and(as_row[0] == row, as_row[1] == col)

    loads = [
        pltpu.make_async_copy(source, target, load_sems.at[i])
        for i, (source, target) in enumerate(
            ((vec_hbm, vec_ref), (halves_ref, tiles), (rest_hbm, rest_ref), (tri_hbm, tri_ref))
        )
    ]
    for load in loads:
        load.start()

    barrier = pltpu.get_barrier_semaphore()
    near = [moved(me, x=d) for d in (1, 2, 3)] + [moved(me, y=d) for d in (1, 2, 3)]
    near += [moved(me, z=d) for d in (1, 2, 3)] + [sibling]
    for device in near:
        pl.semaphore_signal(barrier, inc=1, device_id=device, device_id_type=MESH)

    @pl.when(jnp.logical_not(alone))
    def _():
        for device in (as_row, as_col):
            pl.semaphore_signal(barrier, inc=1, device_id=device, device_id_type=MESH)

    pl.semaphore_wait(barrier, len(near) + jnp.where(alone, 0, 2).astype(jnp.int32))

    copies = Copies(send_sems, recv_sems)
    z_ring = (z, row_shift, moved(me, z=1), moved(me, z=3))
    x_ring = (x, 0, moved(me, x=1), moved(me, x=3))
    spread = Spread(me, vec_ref, vec_row, vec_send_sems, vec_recv_sems)
    loads[0].wait()
    spread.begin()
    vec_high[0], vec_low[0] = split(vec_ref[...])
    loads[1].wait()

    def facts(position):
        block_row = row + 8 * position
        return block_row >= col, jnp.where(block_row == col, 0.5, 1.0).astype(jnp.float32)

    def upper(which):
        return vec_high[which, 0:HALF], vec_low[which, 0:HALF]

    def lower(which):
        return vec_high[which, HALF:TILE], vec_low[which, HALF:TILE]

    def whole(which):
        return vec_high[which], vec_low[which]

    def row_part(position):
        is_lower, weight = facts(position)
        tile_high[position], tile_low[position] = split(tiles[position])
        tile = tile_high.at[position], tile_low.at[position]

        @pl.when(is_lower)
        def _():
            parts[1 + position, 0:HALF] = product((tile[0][...], tile[1][...]), whole(0), NN) * weight
            parts[1 + position, HALF:TILE] = jnp.zeros((HALF, WIDTH), jnp.float32)

        @pl.when(jnp.logical_not(is_lower))
        def _():
            parts[1 + position] = product((tile[0][...], tile[1][...]), lower(0), TN)

    def col_part(position):
        is_lower, weight = facts(position)
        tile = tile_high.at[position], tile_low.at[position]

        @pl.when(is_lower)
        def _():
            parts[0] += product((tile[0][...], tile[1][...]), upper(1 + position), TN) * weight

        @pl.when(jnp.logical_not(is_lower))
        def _():
            parts[0, HALF:TILE] += product((tile[0][...], tile[1][...]), whole(1 + position), NN)

    row_part(1 - core)
    pair = copies.start(parts.at[2 - core], sibling_in, sibling)
    spread.serve(0)
    row_part(core)
    spread.serve(1)
    spread.serve(2)
    rest_rows = rows(HALF + row * REST, REST)
    loads[2].wait()
    block = split(rest_ref[...])
    rest_part[...] = product(block, whole(0), NN) * 0.5
    parts[0] = product(block, (vec_high[0, rest_rows, :], vec_low[0, rest_rows, :]), TN) * 0.5
    spread.serve(3)
    spread.serve(4)
    pair.wait_recv()
    row_sum[...] = parts[1 + core] + sibling_in[...]
    for step in (5, 6, 7):
        spread.serve(step)
    row_scatter = ring_scatter(copies, row_sum, row_unit, row_relay, *z_ring)
    next(row_scatter)
    spread.end()
    for position in range(2):
        vec_high[1 + position], vec_low[1 + position] = split(vec_row[position])
    col_part(0)
    next(row_scatter)
    col_part(1)
    partial[...] = product(whole(0), split(parts[0]), TN)
    parts[0, rest_rows, :] += rest_part[...]
    columns = ring_scatter(copies, parts.at[0], col_unit, col_relay, *x_ring)
    next(columns)
    inner = inner_sum(
        copies, me, partial, inner_ref, (first, first_in, second, second_in, third, third_in, fourth_in, fifth, sixth)
    )
    next(inner)
    step_all([row_scatter])

    keep_row, keep_col = rows(row_half * PIECE, PIECE), rows(lo * PIECE, PIECE)
    give_row, give_col = rows((1 - row_half) * PIECE, PIECE), rows((1 - lo) * PIECE, PIECE)
    row_partner = moved(me, y=2)
    col_partner = at(x, 1 - lo, z, hi, core)
    row_copy = copies.start(row_unit.at[give_row], pair_in.at[0], row_partner)
    next(inner)
    next(columns)
    row_copy.wait_recv()
    swap_out[...] = row_unit[keep_row, :] + pair_in[0]
    row_copy = copies.make(swap_out, swap_in, as_row)

    @pl.when(jnp.logical_not(alone))
    def _():
        row_copy.start()

    @pl.when(alone)
    def _():
        swap_in[...] = swap_out[...]

    next(inner)
    step_all([columns])
    col_copy = copies.start(col_unit.at[give_col], pair_in.at[1], col_partner)
    next(inner)
    col_copy.wait_recv()

    @pl.when(jnp.logical_not(alone))
    def _():
        row_copy.wait()

    loads[3].wait()
    tri = split(tri_ref[...])
    col_rows = rows(x * UNIT + lo * PIECE, PIECE)
    col_piece = av_col.at[col_rows]
    col_piece[...] = product(split(col_unit[keep_col, :] + pair_in[1] + swap_in[...]), tri, NN)
    row_copy = copies.make(col_piece, av_row.at[col // 8, col_rows], as_col)

    @pl.when(jnp.logical_not(alone))
    def _():
        row_copy.start()

    @pl.when(alone)
    def _():
        av_row[col // 8, col_rows, :] = col_piece[...]

    columns = ring_gather(copies, av_col, *x_ring, lo, col_partner)
    next(columns)
    next(inner)
    next(columns)
    next(inner)

    @pl.when(jnp.logical_not(alone))
    def _():
        row_copy.wait()

    rows_in = ring_gather(copies, av_row.at[core], *z_ring, row_half, row_partner, sibling)
    next(rows_in)
    next(inner)
    next(columns)
    next(rows_in)
    step_all([inner])
    whole_inner = inner_ref[...] + inner_ref[...].T
    middle = split(product(split(product(tri, split(whole_inner), TN)), tri, NN) * 0.5)
    next(columns)
    next(rows_in)
    vec_middle[0] = product(whole(0), middle, NN)
    next(columns)
    next(rows_in)
    vec_middle[1] = product(whole(1), middle, NN)
    step_all([columns])
    w = av_col[...] - vec_middle[0]
    w_ref[...] = w
    w_high[0], w_low[0] = split(w)
    vec_middle[2] = product(whole(2), middle, NN)
    next(rows_in)
    step_all([rows_in])
    for position in range(2):
        w_high[1 + position], w_low[1 + position] = split(av_row[position] - vec_middle[1 + position])
    copies.finish()
    spread.finish()


def update_kernel(
    halves_ref, rest_ref, vec_high, vec_low, w_high, w_low, w_ref, out_ref, out_rest, out_w,
    tiles, rest, load_sems, store_sems, side_sems,
):
    row, col = lax.axis_index("row"), lax.axis_index("col")
    count, _, size = tiles.shape
    each = TILE // size

    def place_of(ref, at_step):
        return ref.at[at_step // each, :, pl.ds(pl.multiple_of((at_step % each) * size, size), size)]

    def load(at_step):
        return pltpu.make_async_copy(place_of(halves_ref, at_step), tiles.at[at_step], load_sems.at[at_step])

    def store(at_step):
        return pltpu.make_async_copy(tiles.at[at_step], place_of(out_ref, at_step), store_sems.at[at_step])

    w_copy = pltpu.make_async_copy(w_ref, out_w, side_sems.at[0])
    rest_in = pltpu.make_async_copy(rest_ref, rest, side_sems.at[1])
    rest_out = pltpu.make_async_copy(rest, out_rest, side_sems.at[2])
    for at_step in range(count):
        load(at_step).start()
    rest_in.start()
    w_copy.start()

    def one(at_step, carry):
        position = at_step // each
        is_lower = row + 8 * position >= col
        high_rows = rows(jnp.where(is_lower, 0, HALF), HALF)
        low_rows = rows((at_step % each) * size, size)
        low_at = jnp.where(is_lower, 0, 1 + position)
        high_at = jnp.where(is_lower, 1 + position, 0)
        update = product(
            (vec_high[high_at, high_rows, :], vec_low[high_at, high_rows, :]),
            (w_high[low_at, low_rows, :], w_low[low_at, low_rows, :]),
            NT,
        ) + product(
            (w_high[high_at, high_rows, :], w_low[high_at, high_rows, :]),
            (vec_high[low_at, low_rows, :], vec_low[low_at, low_rows, :]),
            NT,
        )
        load(at_step).wait()
        tiles[at_step] = tiles[at_step] - update
        store(at_step).start()
        return carry

    lax.fori_loop(0, count, one, 0)
    rest_rows = rows(HALF + row * REST, REST)
    update = product(
        (vec_high[0, rest_rows, :], vec_low[0, rest_rows, :]), (w_high[0], w_low[0]), NT
    ) + product((w_high[0, rest_rows, :], w_low[0, rest_rows, :]), (vec_high[0], vec_low[0]), NT)
    rest_in.wait()
    rest[...] = rest[...] - update
    rest_out.start()
    for at_step in range(count):
        store(at_step).wait()
    w_copy.wait()
    rest_out.wait()


def shards(halves, diag_rest, panel_vectors, tri_factor):
    vmem = pl.BlockSpec(memory_space=pltpu.VMEM)
    outside = pl.BlockSpec(memory_space=pltpu.HBM)
    f32 = jnp.float32
    block = (TILE, WIDTH)

    def buffer(*shape):
        return pltpu.VMEM(shape, f32)

    terms = jax.ShapeDtypeStruct((3,) + block, jnp.bfloat16)
    handed = pl.pallas_call(
        gather_kernel,
        out_shape=[terms, terms, terms, terms, jax.ShapeDtypeStruct(block, f32)],
        in_specs=[outside] * 4,
        out_specs=[vmem] * 5,
        scratch_shapes=[
            buffer(*block),
            buffer(REST, TILE),
            buffer(WIDTH, WIDTH),
            buffer(*block),
            buffer(2, *block),
            buffer(2, *block),
            buffer(WIDTH, WIDTH),
            buffer(3, *block),
            buffer(2, HALF, TILE),
            pltpu.VMEM((2, HALF, TILE), jnp.bfloat16),
            pltpu.VMEM((2, HALF, TILE), jnp.bfloat16),
            buffer(3, *block),
            buffer(REST, WIDTH),
            buffer(WIDTH, WIDTH),
            buffer(*block),
            buffer(*block),
            buffer(8, PIECE, WIDTH),
            buffer(8, PIECE, WIDTH),
            buffer(UNIT, WIDTH),
            buffer(UNIT, WIDTH),
            buffer(2, PIECE, WIDTH),
            buffer(PIECE, WIDTH),
            buffer(PIECE, WIDTH),
            buffer(128, WIDTH),
            buffer(128, WIDTH),
            buffer(32, WIDTH),
            buffer(3, 32, WIDTH),
            buffer(8, WIDTH),
            buffer(3, 8, WIDTH),
            buffer(3, 8, WIDTH),
            buffer(32, WIDTH),
            buffer(128, WIDTH),
            pltpu.SemaphoreType.DMA((4,)),
            pltpu.SemaphoreType.DMA((80,)),
            pltpu.SemaphoreType.DMA((80,)),
            pltpu.SemaphoreType.DMA((40,)),
            pltpu.SemaphoreType.DMA((40,)),
        ],
        compiler_params=pltpu.CompilerParams(
            collective_id=0, has_side_effects=True, vmem_limit_bytes=44 * 2**20
        ),
        name="gather",
    )(halves, diag_rest, panel_vectors, tri_factor)

    size = 256
    count = 2 * TILE // size
    return pl.pallas_call(
        update_kernel,
        out_shape=[
            jax.ShapeDtypeStruct(halves.shape, f32),
            jax.ShapeDtypeStruct(diag_rest.shape, f32),
            jax.ShapeDtypeStruct(panel_vectors.shape, f32),
        ],
        in_specs=[outside] * 2 + [vmem] * 5,
        out_specs=[outside] * 3,
        scratch_shapes=[
            buffer(count, HALF, size),
            buffer(REST, TILE),
            pltpu.SemaphoreType.DMA((count,)),
            pltpu.SemaphoreType.DMA((count,)),
            pltpu.SemaphoreType.DMA((3,)),
        ],
        compiler_params=pltpu.CompilerParams(vmem_limit_bytes=24 * 2**20),
        name="update",
    )(halves, diag_rest, *handed)


def solution(mesh):
    return jax.shard_map(
        shards,
        mesh=mesh,
        in_specs=(P(None, "row", "col"), P(("col", "row"), None), P("col", None), P()),
        out_specs=(P(None, "row", "col"), P(("col", "row"), None), P("col", None)),
        check_vma=False,
    )
```

```python
import functools

import jax
import jax.numpy as jnp
from jax import lax
from jax.experimental import pallas as pl
from jax.experimental.pallas import tpu as pltpu
from jax.sharding import PartitionSpec as P

MESH = pl.DeviceIdType.MESH
NN = (((1,), (0,)), ((), ()))
TN = (((0,), (0,)), ((), ()))
NT = (((1,), (1,)), ((), ()))
TILE = 1024
HALF = 512
WIDTH = 256
UNIT = 256
PIECE = 128
REST = 64


def split(value):
    high = value.astype(jnp.bfloat16)
    low = (value - high.astype(jnp.float32)).astype(jnp.bfloat16)
    return high, low


def product(left, right, dims):
    def dot(a, b):
        return lax.dot_general(a, b, dims, preferred_element_type=jnp.float32)

    return dot(left[0], right[0]) + (dot(left[0], right[1]) + dot(left[1], right[0]))


def rows(start, size):
    return pl.ds(pl.multiple_of(start, 8), size)


def place():
    row, col = lax.axis_index("row"), lax.axis_index("col")
    return dict(row=row, col=col, x=row // 2, lo=row % 2, z=col // 4, hi=(col // 2) % 2, core=col % 2)


def at(x, lo, z, hi, core):
    return (x * 2 + lo, z * 4 + hi * 2 + core)


def moved(me, x=0, y=0, z=0, core=0):
    y_at = (me["hi"] * 2 + me["lo"] + y) % 4
    return at((me["x"] + x) % 4, y_at % 2, (me["z"] + z) % 4, y_at // 2, (me["core"] + core) % 2)


class Copies:
    def __init__(self, send_sems, recv_sems):
        self.send_sems, self.recv_sems, self.used, self.started = send_sems, recv_sems, 0, []

    def make(self, source, target, device):
        copy = pltpu.make_async_remote_copy(
            src_ref=source,
            dst_ref=target,
            send_sem=self.send_sems.at[self.used],
            recv_sem=self.recv_sems.at[self.used],
            device_id=device,
            device_id_type=MESH,
        )
        self.used += 1
        return copy

    def start(self, source, target, device):
        copy = self.make(source, target, device)
        copy.start()
        self.started.append(copy)
        return copy

    def finish(self):
        for copy in self.started:
            copy.wait_send()


def ring_scatter(copies, source, out, relay, index, shift, plus, minus):
    def part(step, half):
        return source.at[rows(((index + step + shift) % 4) * UNIT + half * PIECE, PIECE)]

    far_plus = copies.start(part(2, 0), relay.at[0], plus)
    far_minus = copies.start(part(2, 1), relay.at[1], minus)
    near_plus = copies.start(part(1, 1), relay.at[2], plus)
    near_minus = copies.start(part(3, 0), relay.at[3], minus)
    yield
    far_plus.wait_recv()
    relay[6] = relay[0] + part(1, 0)[...]
    sum_plus = copies.start(relay.at[6], relay.at[4], plus)
    far_minus.wait_recv()
    relay[7] = relay[1] + part(3, 1)[...]
    sum_minus = copies.start(relay.at[7], relay.at[5], minus)
    yield
    near_plus.wait_recv()
    near_minus.wait_recv()
    sum_plus.wait_recv()
    sum_minus.wait_recv()
    out[0:PIECE] = part(0, 0)[...] + (relay[4] + relay[3])
    out[PIECE:UNIT] = part(0, 1)[...] + (relay[2] + relay[5])


def ring_gather(copies, block, index, shift, plus, minus, kept, partner, sibling=None):
    def piece(step, which):
        return block.at[rows(((index + step + shift) % 4) * UNIT + which * PIECE, PIECE)]

    given = 1 - kept
    shared = []

    def share(ref):
        if sibling is not None:
            shared.append(copies.start(ref, ref, sibling))

    def send(ref, device):
        return copies.start(ref, ref, device)

    own = piece(0, kept)
    pair = send(own, partner)
    own_plus, own_minus = send(own, plus), send(own, minus)
    share(own)
    yield
    pair.wait_recv()
    other = piece(0, given)
    other_plus, other_minus = send(other, plus), send(other, minus)
    share(other)
    yield
    own_plus.wait_recv()
    far_plus = send(piece(3, kept), plus)
    share(piece(3, kept))
    own_minus.wait_recv()
    share(piece(1, kept))
    yield
    other_minus.wait_recv()
    far_minus = send(piece(1, given), minus)
    share(piece(1, given))
    other_plus.wait_recv()
    share(piece(3, given))
    yield
    far_plus.wait_recv()
    share(piece(2, kept))
    far_minus.wait_recv()
    share(piece(2, given))
    yield
    for copy in shared:
        copy.wait_recv()


ORDER = (0, 4, 1, 5, 2, 6, 3, 7)


class Spread:
    def __init__(self, me, vec_ref, vec_row, send_sems, recv_sems):
        x, lo, z, hi, core = me["x"], me["lo"], me["z"], me["hi"], me["core"]
        self.vec_ref, self.vec_row, self.send_sems, self.recv_sems = vec_ref, vec_row, send_sems, recv_sems
        self.lead = core == lo
        line = hi == x % 2
        end = z % 2 == x // 2
        self.source = jnp.logical_and(jnp.logical_and(self.lead, line), end)
        self.cross = jnp.logical_and(jnp.logical_and(jnp.logical_not(self.lead), line), end)
        self.target = jnp.logical_and(jnp.logical_and(self.lead, jnp.logical_not(line)), end)
        self.ends = jnp.logical_and(self.lead, end)
        self.middle = jnp.logical_and(self.lead, jnp.logical_not(end))
        self.follow = jnp.logical_not(self.lead)
        self.plus, self.minus, self.sibling = moved(me, z=1), moved(me, z=3), moved(me, core=1)
        self.over = at(x, core, z, 1 - hi, core)
        self.own = z // 2
        self.from_minus = ((z + 3) % 4) // 2

    def chunk(self, block, c):
        return self.vec_row.at[block, pl.ds(c * PIECE, PIECE)]

    def copy(self, slot, source, target, device):
        return pltpu.make_async_remote_copy(
            src_ref=source,
            dst_ref=target,
            send_sem=self.send_sems.at[slot],
            recv_sem=self.recv_sems.at[slot],
            device_id=device,
            device_id_type=MESH,
        )

    def mine(self, c):
        return self.vec_ref.at[pl.ds(c * PIECE, PIECE)]

    def along(self, c, block, source=None):
        here = self.chunk(block, c)
        return self.copy(c, here if source is None else source, here, self.plus)

    def back(self, c, block, source=None):
        here = self.chunk(block, c)
        return self.copy(8 + c, here if source is None else source, here, self.minus)

    def across(self, c):
        return self.copy(16 + c, self.mine(c), self.chunk(self.own, c), self.over)

    def share(self, c, block, which, source=None):
        here = self.chunk(block, c)
        return self.copy(24 + 8 * which + c, here if source is None else source, here, self.sibling)

    def begin(self):
        @pl.when(self.source)
        def _():
            for c in ORDER:
                self.along(c, self.own, self.mine(c)).start()
                self.back(c, self.own, self.mine(c)).start()
                self.share(c, self.own, 0, self.mine(c)).start()
            self.vec_row[self.own] = self.vec_ref[...]

        @pl.when(self.cross)
        def _():
            for c in ORDER:
                self.across(c).start()

    def serve(self, step):
        c = ORDER[step]

        @pl.when(self.target)
        def _():
            self.across(c).wait_recv()
            self.along(c, self.own).start()
            self.back(c, self.own).start()
            self.share(c, self.own, 0).start()

        @pl.when(self.middle)
        def _():
            block = self.from_minus
            self.along(c, block).wait_recv()
            if c < 4:
                self.along(c, block).start()
            self.share(c, block, 0).start()
            self.back(c, 1 - block).wait_recv()
            if c >= 4:
                self.back(c, 1 - block).start()
            self.share(c, 1 - block, 1).start()

    def end(self):
        @pl.when(self.ends)
        def _():
            for c in ORDER:
                copy = self.along(c, 1 - self.own) if c < 4 else self.back(c, 1 - self.own)
                copy.wait_recv()
                self.share(c, 1 - self.own, 1).start()

        @pl.when(self.follow)
        def _():
            for c in ORDER:
                for which in range(2):
                    self.share(c, which, which).wait_recv()

    def finish(self):
        @pl.when(self.ends)
        def _():
            for c in ORDER:
                self.along(c, self.own).wait_send()
                self.back(c, self.own).wait_send()

        @pl.when(self.middle)
        def _():
            for c in ORDER:
                if c < 4:
                    self.along(c, 0).wait_send()
                else:
                    self.back(c, 0).wait_send()

        @pl.when(self.lead)
        def _():
            for c in ORDER:
                for which in range(2):
                    self.share(c, which, which).wait_send()

        @pl.when(self.cross)
        def _():
            for c in ORDER:
                self.across(c).wait_send()


def inner_sum(copies, me, partial, total, work):
    first, first_in, second, second_in, third, third_in, fourth_in, fifth, sixth = work
    sibling = moved(me, core=1)
    core, x, y = me["core"], me["x"], me["hi"] * 2 + me["lo"]
    copy = copies.start(partial.at[rows((1 - core) * 128, 128)], first_in, sibling)
    yield
    copy.wait_recv()
    first[...] = partial[rows(core * 128, 128), :] + first_in[...]
    sent = [
        copies.start(first.at[rows(((x + d) % 4) * 32, 32)], second_in.at[d - 1], moved(me, x=d)) for d in (1, 2, 3)
    ]
    yield
    for copy in sent:
        copy.wait_recv()
    second[...] = first[rows(x * 32, 32), :] + second_in[0] + second_in[1] + second_in[2]
    sent = [copies.start(second.at[rows(((y + d) % 4) * 8, 8)], third_in.at[d - 1], moved(me, y=d)) for d in (1, 2, 3)]
    yield
    for copy in sent:
        copy.wait_recv()
    third[...] = second[rows(y * 8, 8), :] + third_in[0] + third_in[1] + third_in[2]
    sent = [copies.start(third, fourth_in.at[d - 1], moved(me, z=d)) for d in (1, 2, 3)]
    yield
    for copy in sent:
        copy.wait_recv()
    mine = fifth.at[rows(y * 8, 8)]
    mine[...] = third[...] + fourth_in[0] + fourth_in[1] + fourth_in[2]
    sent = [copies.start(mine, mine, moved(me, y=d)) for d in (1, 2, 3)]
    yield
    for copy in sent:
        copy.wait_recv()
    mine = sixth.at[rows(x * 32, 32)]
    mine[...] = fifth[...]
    sent = [copies.start(mine, mine, moved(me, x=d)) for d in (1, 2, 3)]
    yield
    for copy in sent:
        copy.wait_recv()
    mine = total.at[rows(core * 128, 128)]
    mine[...] = sixth[...]
    copy = copies.start(mine, mine, sibling)
    yield
    copy.wait_recv()


def step_all(running):
    still = []
    for item in running:
        if next(item, "done") != "done":
            still.append(item)
    return still


def gather_kernel(
    halves_ref, rest_hbm, vec_hbm, tri_hbm, vec_high, vec_low, w_high, w_low, w_ref,
    vec_ref, rest_ref, tri_ref, av_col, av_row, vec_row, inner_ref, vec_middle,
    tiles, tile_high, tile_low, parts, rest_part, partial, row_sum, sibling_in, row_relay, col_relay,
    row_unit, col_unit, pair_in, swap_out, swap_in,
    first, first_in, second, second_in, third, third_in, fourth_in, fifth, sixth,
    load_sems, send_sems, recv_sems, vec_send_sems, vec_recv_sems,
):
    me = place()
    row, col, core = me["row"], me["col"], me["core"]
    x, lo, z, hi = me["x"], me["lo"], me["z"], me["hi"]
    sibling = moved(me, core=1)

    row_shift = (x - (x // 2 + 2 * core) + 4) % 4
    row_half = (lo + hi + x) % 2
    as_row = (((z + row_shift) % 4) * 2 + row_half, row + 8 * core)
    row_of = col % 8
    as_col = at(row_of // 2, row_of % 2, (x - row_of // 2 + z + 4) % 4, (lo + row_of + hi) % 2, col // 8)
    alone = jnp.logical_and(as_row[0] == row, as_row[1] == col)

    loads = [
        pltpu.make_async_copy(source, target, load_sems.at[i])
        for i, (source, target) in enumerate(
            ((vec_hbm, vec_ref), (halves_ref, tiles), (rest_hbm, rest_ref), (tri_hbm, tri_ref))
        )
    ]
    for load in loads:
        load.start()

    barrier = pltpu.get_barrier_semaphore()
    near = [moved(me, x=d) for d in (1, 2, 3)] + [moved(me, y=d) for d in (1, 2, 3)]
    near += [moved(me, z=d) for d in (1, 2, 3)] + [sibling]
    for device in near:
        pl.semaphore_signal(barrier, inc=1, device_id=device, device_id_type=MESH)

    @pl.when(jnp.logical_not(alone))
    def _():
        for device in (as_row, as_col):
            pl.semaphore_signal(barrier, inc=1, device_id=device, device_id_type=MESH)

    pl.semaphore_wait(barrier, len(near) + jnp.where(alone, 0, 2).astype(jnp.int32))

    copies = Copies(send_sems, recv_sems)
    z_ring = (z, row_shift, moved(me, z=1), moved(me, z=3))
    x_ring = (x, 0, moved(me, x=1), moved(me, x=3))
    spread = Spread(me, vec_ref, vec_row, vec_send_sems, vec_recv_sems)
    loads[0].wait()
    spread.begin()
    vec_high[0], vec_low[0] = split(vec_ref[...])
    loads[1].wait()

    def facts(position):
        block_row = row + 8 * position
        return block_row >= col, jnp.where(block_row == col, 0.5, 1.0).astype(jnp.float32)

    def upper(which):
        return vec_high[which, 0:HALF], vec_low[which, 0:HALF]

    def lower(which):
        return vec_high[which, HALF:TILE], vec_low[which, HALF:TILE]

    def whole(which):
        return vec_high[which], vec_low[which]

    def row_part(position):
        is_lower, weight = facts(position)
        tile_high[position], tile_low[position] = split(tiles[position])
        tile = tile_high.at[position], tile_low.at[position]

        @pl.when(is_lower)
        def _():
            parts[1 + position, 0:HALF] = product((tile[0][...], tile[1][...]), whole(0), NN) * weight
            parts[1 + position, HALF:TILE] = jnp.zeros((HALF, WIDTH), jnp.float32)

        @pl.when(jnp.logical_not(is_lower))
        def _():
            parts[1 + position] = product((tile[0][...], tile[1][...]), lower(0), TN)

    def col_part(position):
        is_lower, weight = facts(position)
        tile = tile_high.at[position], tile_low.at[position]

        @pl.when(is_lower)
        def _():
            parts[0] += product((tile[0][...], tile[1][...]), upper(1 + position), TN) * weight

        @pl.when(jnp.logical_not(is_lower))
        def _():
            parts[0, HALF:TILE] += product((tile[0][...], tile[1][...]), whole(1 + position), NN)

    row_part(1 - core)
    pair = copies.start(parts.at[2 - core], sibling_in, sibling)
    spread.serve(0)
    row_part(core)
    spread.serve(1)
    spread.serve(2)
    rest_rows = rows(HALF + row * REST, REST)
    loads[2].wait()
    block = split(rest_ref[...])
    rest_part[...] = product(block, whole(0), NN) * 0.5
    parts[0] = product(block, (vec_high[0, rest_rows, :], vec_low[0, rest_rows, :]), TN) * 0.5
    spread.serve(3)
    spread.serve(4)
    pair.wait_recv()
    row_sum[...] = parts[1 + core] + sibling_in[...]
    spread.serve(5)
    row_scatter = ring_scatter(copies, row_sum, row_unit, row_relay, *z_ring)
    next(row_scatter)
    spread.serve(6)
    spread.serve(7)
    spread.end()
    vec_high[1], vec_low[1] = split(vec_row[0])
    col_part(0)
    vec_high[2], vec_low[2] = split(vec_row[1])
    col_part(1)
    partial[...] = product(whole(0), split(parts[0]), TN)
    parts[0, rest_rows, :] += rest_part[...]
    columns = ring_scatter(copies, parts.at[0], col_unit, col_relay, *x_ring)
    next(columns)
    inner = inner_sum(
        copies, me, partial, inner_ref, (first, first_in, second, second_in, third, third_in, fourth_in, fifth, sixth)
    )
    next(inner)
    loads[3].wait()
    tri = split(tri_ref[...])
    next(row_scatter)
    next(inner)
    next(columns)
    step_all([row_scatter])

    keep_row, keep_col = rows(row_half * PIECE, PIECE), rows(lo * PIECE, PIECE)
    give_row, give_col = rows((1 - row_half) * PIECE, PIECE), rows((1 - lo) * PIECE, PIECE)
    row_partner = moved(me, y=2)
    col_partner = at(x, 1 - lo, z, hi, core)
    row_copy = copies.start(row_unit.at[give_row], pair_in.at[0], row_partner)
    next(inner)
    step_all([columns])
    col_copy = copies.start(col_unit.at[give_col], pair_in.at[1], col_partner)
    row_copy.wait_recv()
    swap_out[0] = product(split(row_unit[keep_row, :] + pair_in[0]), tri, NN)
    row_copy = copies.make(swap_out.at[0], swap_in.at[0], as_row)

    @pl.when(jnp.logical_not(alone))
    def _():
        row_copy.start()

    next(inner)
    col_copy.wait_recv()
    swap_out[1] = product(split(col_unit[keep_col, :] + pair_in[1]), tri, NN)
    col_copy = copies.make(swap_out.at[1], swap_in.at[1], as_col)

    @pl.when(jnp.logical_not(alone))
    def _():
        col_copy.start()

    @pl.when(alone)
    def _():
        swap_in[...] = swap_out[...]

    next(inner)

    @pl.when(jnp.logical_not(alone))
    def _():
        row_copy.wait()

    av_col[rows(x * UNIT + lo * PIECE, PIECE), :] = swap_out[1] + swap_in[0]
    columns = ring_gather(copies, av_col, *x_ring, lo, col_partner)
    next(columns)
    next(inner)

    @pl.when(jnp.logical_not(alone))
    def _():
        col_copy.wait()

    av_row[core, rows(((z + row_shift) % 4) * UNIT + row_half * PIECE, PIECE), :] = swap_out[0] + swap_in[1]
    rows_in = ring_gather(copies, av_row.at[core], *z_ring, row_half, row_partner, sibling)
    next(rows_in)
    next(columns)
    next(inner)
    next(rows_in)
    next(columns)
    step_all([inner])
    whole_inner = inner_ref[...] + inner_ref[...].T
    middle = split(product(split(product(tri, split(whole_inner), TN)), tri, NN) * 0.5)
    vec_middle[0] = product(whole(0), middle, NN)
    next(rows_in)
    next(columns)
    vec_middle[1] = product(whole(1), middle, NN)
    next(rows_in)
    next(columns)
    vec_middle[2] = product(whole(2), middle, NN)
    step_all([columns])
    w = av_col[...] - vec_middle[0]
    w_ref[...] = w
    w_high[0], w_low[0] = split(w)
    next(rows_in)
    step_all([rows_in])
    for position in range(2):
        w_high[1 + position], w_low[1 + position] = split(av_row[position] - vec_middle[1 + position])
    copies.finish()
    spread.finish()


def update_kernel(
    halves_ref, rest_ref, vec_high, vec_low, w_high, w_low, w_ref, out_ref, out_rest, out_w,
    tiles, rest, load_sems, store_sems, side_sems,
):
    row, col = lax.axis_index("row"), lax.axis_index("col")
    count, _, size = tiles.shape
    each = TILE // size

    def place_of(ref, at_step):
        return ref.at[at_step // each, :, pl.ds(pl.multiple_of((at_step % each) * size, size), size)]

    def load(at_step):
        return pltpu.make_async_copy(place_of(halves_ref, at_step), tiles.at[at_step], load_sems.at[at_step])

    def store(at_step):
        return pltpu.make_async_copy(tiles.at[at_step], place_of(out_ref, at_step), store_sems.at[at_step])

    w_copy = pltpu.make_async_copy(w_ref, out_w, side_sems.at[0])
    rest_in = pltpu.make_async_copy(rest_ref, rest, side_sems.at[1])
    rest_out = pltpu.make_async_copy(rest, out_rest, side_sems.at[2])
    for at_step in range(count):
        load(at_step).start()
    rest_in.start()
    w_copy.start()

    def one(at_step, carry):
        position = at_step // each
        is_lower = row + 8 * position >= col
        high_rows = rows(jnp.where(is_lower, 0, HALF), HALF)
        low_rows = rows((at_step % each) * size, size)
        low_at = jnp.where(is_lower, 0, 1 + position)
        high_at = jnp.where(is_lower, 1 + position, 0)
        update = product(
            (vec_high[high_at, high_rows, :], vec_low[high_at, high_rows, :]),
            (w_high[low_at, low_rows, :], w_low[low_at, low_rows, :]),
            NT,
        ) + product(
            (w_high[high_at, high_rows, :], w_low[high_at, high_rows, :]),
            (vec_high[low_at, low_rows, :], vec_low[low_at, low_rows, :]),
            NT,
        )
        load(at_step).wait()
        tiles[at_step] = tiles[at_step] - update
        store(at_step).start()
        return carry

    lax.fori_loop(0, count, one, 0)
    rest_rows = rows(HALF + row * REST, REST)
    update = product(
        (vec_high[0, rest_rows, :], vec_low[0, rest_rows, :]), (w_high[0], w_low[0]), NT
    ) + product((w_high[0, rest_rows, :], w_low[0, rest_rows, :]), (vec_high[0], vec_low[0]), NT)
    rest_in.wait()
    rest[...] = rest[...] - update
    rest_out.start()
    for at_step in range(count):
        store(at_step).wait()
    w_copy.wait()
    rest_out.wait()


def shards(halves, diag_rest, panel_vectors, tri_factor):
    vmem = pl.BlockSpec(memory_space=pltpu.VMEM)
    outside = pl.BlockSpec(memory_space=pltpu.HBM)
    f32 = jnp.float32
    block = (TILE, WIDTH)

    def buffer(*shape):
        return pltpu.VMEM(shape, f32)

    terms = jax.ShapeDtypeStruct((3,) + block, jnp.bfloat16)
    handed = pl.pallas_call(
        gather_kernel,
        out_shape=[terms, terms, terms, terms, jax.ShapeDtypeStruct(block, f32)],
        in_specs=[outside] * 4,
        out_specs=[vmem] * 5,
        scratch_shapes=[
            buffer(*block),
            buffer(REST, TILE),
            buffer(WIDTH, WIDTH),
            buffer(*block),
            buffer(2, *block),
            buffer(2, *block),
            buffer(WIDTH, WIDTH),
            buffer(3, *block),
            buffer(2, HALF, TILE),
            pltpu.VMEM((2, HALF, TILE), jnp.bfloat16),
            pltpu.VMEM((2, HALF, TILE), jnp.bfloat16),
            buffer(3, *block),
            buffer(REST, WIDTH),
            buffer(WIDTH, WIDTH),
            buffer(*block),
            buffer(*block),
            buffer(8, PIECE, WIDTH),
            buffer(8, PIECE, WIDTH),
            buffer(UNIT, WIDTH),
            buffer(UNIT, WIDTH),
            buffer(2, PIECE, WIDTH),
            buffer(2, PIECE, WIDTH),
            buffer(2, PIECE, WIDTH),
            buffer(128, WIDTH),
            buffer(128, WIDTH),
            buffer(32, WIDTH),
            buffer(3, 32, WIDTH),
            buffer(8, WIDTH),
            buffer(3, 8, WIDTH),
            buffer(3, 8, WIDTH),
            buffer(32, WIDTH),
            buffer(128, WIDTH),
            pltpu.SemaphoreType.DMA((4,)),
            pltpu.SemaphoreType.DMA((80,)),
            pltpu.SemaphoreType.DMA((80,)),
            pltpu.SemaphoreType.DMA((40,)),
            pltpu.SemaphoreType.DMA((40,)),
        ],
        compiler_params=pltpu.CompilerParams(
            collective_id=0, has_side_effects=True, vmem_limit_bytes=44 * 2**20
        ),
        name="gather",
    )(halves, diag_rest, panel_vectors, tri_factor)

    size = 256
    count = 2 * TILE // size
    return pl.pallas_call(
        update_kernel,
        out_shape=[
            jax.ShapeDtypeStruct(halves.shape, f32),
            jax.ShapeDtypeStruct(diag_rest.shape, f32),
            jax.ShapeDtypeStruct(panel_vectors.shape, f32),
        ],
        in_specs=[outside] * 2 + [vmem] * 5,
        out_specs=[outside] * 3,
        scratch_shapes=[
            buffer(count, HALF, size),
            buffer(REST, TILE),
            pltpu.SemaphoreType.DMA((count,)),
            pltpu.SemaphoreType.DMA((count,)),
            pltpu.SemaphoreType.DMA((3,)),
        ],
        compiler_params=pltpu.CompilerParams(vmem_limit_bytes=24 * 2**20),
        name="update",
    )(halves, diag_rest, *handed)


def solution(mesh):
    return jax.shard_map(
        shards,
        mesh=mesh,
        in_specs=(P(None, "row", "col"), P(("col", "row"), None), P("col", None), P()),
        out_specs=(P(None, "row", "col"), P(("col", "row"), None), P("col", None)),
        check_vma=False,
    )
```

```python
import functools

import jax
import jax.numpy as jnp
from jax import lax
from jax.experimental import pallas as pl
from jax.experimental.pallas import tpu as pltpu
from jax.sharding import PartitionSpec as P

MESH = pl.DeviceIdType.MESH
NN = (((1,), (0,)), ((), ()))
TN = (((0,), (0,)), ((), ()))
NT = (((1,), (1,)), ((), ()))
TILE = 1024
HALF = 512
WIDTH = 256
UNIT = 256
PIECE = 128
REST = 64


def split(value):
    high = value.astype(jnp.bfloat16)
    low = (value - high.astype(jnp.float32)).astype(jnp.bfloat16)
    return high, low


def product(left, right, dims):
    def dot(a, b):
        return lax.dot_general(a, b, dims, preferred_element_type=jnp.float32)

    return dot(left[0], right[0]) + (dot(left[0], right[1]) + dot(left[1], right[0]))


def rows(start, size):
    return pl.ds(pl.multiple_of(start, 8), size)


def place():
    row, col = lax.axis_index("row"), lax.axis_index("col")
    return dict(row=row, col=col, x=row // 2, lo=row % 2, z=col // 4, hi=(col // 2) % 2, core=col % 2)


def at(x, lo, z, hi, core):
    return (x * 2 + lo, z * 4 + hi * 2 + core)


def moved(me, x=0, y=0, z=0, core=0):
    y_at = (me["hi"] * 2 + me["lo"] + y) % 4
    return at((me["x"] + x) % 4, y_at % 2, (me["z"] + z) % 4, y_at // 2, (me["core"] + core) % 2)


class Copies:
    def __init__(self, send_sems, recv_sems):
        self.send_sems, self.recv_sems, self.used, self.started = send_sems, recv_sems, 0, []

    def make(self, source, target, device):
        copy = pltpu.make_async_remote_copy(
            src_ref=source,
            dst_ref=target,
            send_sem=self.send_sems.at[self.used],
            recv_sem=self.recv_sems.at[self.used],
            device_id=device,
            device_id_type=MESH,
        )
        self.used += 1
        return copy

    def start(self, source, target, device):
        copy = self.make(source, target, device)
        copy.start()
        self.started.append(copy)
        return copy

    def finish(self):
        for copy in self.started:
            copy.wait_send()


def ring_scatter(copies, source, out, relay, index, shift, plus, minus):
    def part(step, half):
        return source.at[rows(((index + step + shift) % 4) * UNIT + half * PIECE, PIECE)]

    far_plus = copies.start(part(2, 0), relay.at[0], plus)
    far_minus = copies.start(part(2, 1), relay.at[1], minus)
    near_plus = copies.start(part(1, 1), relay.at[2], plus)
    near_minus = copies.start(part(3, 0), relay.at[3], minus)
    yield
    far_plus.wait_recv()
    relay[6] = relay[0] + part(1, 0)[...]
    sum_plus = copies.start(relay.at[6], relay.at[4], plus)
    far_minus.wait_recv()
    relay[7] = relay[1] + part(3, 1)[...]
    sum_minus = copies.start(relay.at[7], relay.at[5], minus)
    yield
    near_plus.wait_recv()
    near_minus.wait_recv()
    sum_plus.wait_recv()
    sum_minus.wait_recv()
    out[0:PIECE] = part(0, 0)[...] + (relay[4] + relay[3])
    out[PIECE:UNIT] = part(0, 1)[...] + (relay[2] + relay[5])


def ring_gather(copies, block, index, shift, plus, minus, kept, partner, sibling=None):
    def piece(step, which):
        return block.at[rows(((index + step + shift) % 4) * UNIT + which * PIECE, PIECE)]

    given = 1 - kept
    shared = []

    def share(ref):
        if sibling is not None:
            shared.append(copies.start(ref, ref, sibling))

    def send(ref, device):
        return copies.start(ref, ref, device)

    own = piece(0, kept)
    pair = send(own, partner)
    own_plus, own_minus = send(own, plus), send(own, minus)
    share(own)
    yield
    pair.wait_recv()
    other = piece(0, given)
    other_plus, other_minus = send(other, plus), send(other, minus)
    share(other)
    yield
    own_plus.wait_recv()
    far_plus = send(piece(3, kept), plus)
    share(piece(3, kept))
    own_minus.wait_recv()
    share(piece(1, kept))
    yield
    other_minus.wait_recv()
    far_minus = send(piece(1, given), minus)
    share(piece(1, given))
    other_plus.wait_recv()
    share(piece(3, given))
    yield
    far_plus.wait_recv()
    share(piece(2, kept))
    far_minus.wait_recv()
    share(piece(2, given))
    yield
    for copy in shared:
        copy.wait_recv()


ORDER = (0, 4, 1, 5, 2, 6, 3, 7)


class Spread:
    def __init__(self, me, vec_ref, vec_row, send_sems, recv_sems):
        x, lo, z, hi, core = me["x"], me["lo"], me["z"], me["hi"], me["core"]
        self.vec_ref, self.vec_row, self.send_sems, self.recv_sems = vec_ref, vec_row, send_sems, recv_sems
        self.lead = core == lo
        line = hi == x % 2
        end = z % 2 == x // 2
        self.source = jnp.logical_and(jnp.logical_and(self.lead, line), end)
        self.cross = jnp.logical_and(jnp.logical_and(jnp.logical_not(self.lead), line), end)
        self.target = jnp.logical_and(jnp.logical_and(self.lead, jnp.logical_not(line)), end)
        self.ends = jnp.logical_and(self.lead, end)
        self.middle = jnp.logical_and(self.lead, jnp.logical_not(end))
        self.follow = jnp.logical_not(self.lead)
        self.plus, self.minus, self.sibling = moved(me, z=1), moved(me, z=3), moved(me, core=1)
        self.over = at(x, core, z, 1 - hi, core)
        self.own = z // 2
        self.from_minus = ((z + 3) % 4) // 2

    def chunk(self, block, c):
        return self.vec_row.at[block, pl.ds(c * PIECE, PIECE)]

    def copy(self, slot, source, target, device):
        return pltpu.make_async_remote_copy(
            src_ref=source,
            dst_ref=target,
            send_sem=self.send_sems.at[slot],
            recv_sem=self.recv_sems.at[slot],
            device_id=device,
            device_id_type=MESH,
        )

    def mine(self, c):
        return self.vec_ref.at[pl.ds(c * PIECE, PIECE)]

    def along(self, c, block, source=None):
        here = self.chunk(block, c)
        return self.copy(c, here if source is None else source, here, self.plus)

    def back(self, c, block, source=None):
        here = self.chunk(block, c)
        return self.copy(8 + c, here if source is None else source, here, self.minus)

    def across(self, c):
        return self.copy(16 + c, self.mine(c), self.chunk(self.own, c), self.over)

    def share(self, c, block, which, source=None):
        here = self.chunk(block, c)
        return self.copy(24 + 8 * which + c, here if source is None else source, here, self.sibling)

    def begin(self):
        @pl.when(self.source)
        def _():
            for c in ORDER:
                self.along(c, self.own, self.mine(c)).start()
                self.back(c, self.own, self.mine(c)).start()
                self.share(c, self.own, 0, self.mine(c)).start()
            self.vec_row[self.own] = self.vec_ref[...]

        @pl.when(self.cross)
        def _():
            for c in ORDER:
                self.across(c).start()

    def serve(self, step):
        c = ORDER[step]

        @pl.when(self.target)
        def _():
            self.across(c).wait_recv()
            self.along(c, self.own).start()
            self.back(c, self.own).start()
            self.share(c, self.own, 0).start()

        @pl.when(self.middle)
        def _():
            block = self.from_minus
            self.along(c, block).wait_recv()
            if c < 4:
                self.along(c, block).start()
            self.share(c, block, 0).start()
            self.back(c, 1 - block).wait_recv()
            if c >= 4:
                self.back(c, 1 - block).start()
            self.share(c, 1 - block, 1).start()

    def end(self):
        @pl.when(self.ends)
        def _():
            for c in ORDER:
                copy = self.along(c, 1 - self.own) if c < 4 else self.back(c, 1 - self.own)
                copy.wait_recv()
                self.share(c, 1 - self.own, 1).start()

        @pl.when(self.follow)
        def _():
            for c in ORDER:
                for which in range(2):
                    self.share(c, which, which).wait_recv()

    def finish(self):
        @pl.when(self.ends)
        def _():
            for c in ORDER:
                self.along(c, self.own).wait_send()
                self.back(c, self.own).wait_send()

        @pl.when(self.middle)
        def _():
            for c in ORDER:
                if c < 4:
                    self.along(c, 0).wait_send()
                else:
                    self.back(c, 0).wait_send()

        @pl.when(self.lead)
        def _():
            for c in ORDER:
                for which in range(2):
                    self.share(c, which, which).wait_send()

        @pl.when(self.cross)
        def _():
            for c in ORDER:
                self.across(c).wait_send()


def inner_sum(copies, me, partial, total, work):
    first, first_in, second_in, third_in, fourth_in = work
    sibling = moved(me, core=1)
    core, x, y, z = me["core"], me["x"], me["hi"] * 2 + me["lo"], me["z"]
    copy = copies.start(partial.at[rows((1 - core) * 128, 128)], first_in, sibling)
    yield
    copy.wait_recv()
    first[...] = partial[rows(core * 128, 128), :] + first_in[...]
    sent = [
        copies.start(first.at[rows(((y + d) % 4) * 32, 32)], second_in.at[d - 1], moved(me, y=d)) for d in (1, 2, 3)
    ]
    yield
    for copy in sent:
        copy.wait_recv()
    mine = third_in.at[z]
    mine[...] = first[rows(y * 32, 32), :] + second_in[0] + second_in[1] + second_in[2]
    sent = [copies.start(mine, mine, moved(me, z=d)) for d in (1, 2, 3)]
    yield
    for copy in sent:
        copy.wait_recv()
    mine = fourth_in.at[x]
    mine[...] = third_in[0] + third_in[1] + third_in[2] + third_in[3]
    sent = [copies.start(mine, mine, moved(me, x=d)) for d in (1, 2, 3)]
    yield
    for copy in sent:
        copy.wait_recv()
    mine = total.at[rows(core * 128 + y * 32, 32)]
    mine[...] = fourth_in[0] + fourth_in[1] + fourth_in[2] + fourth_in[3]
    sent = [copies.start(mine, mine, moved(me, y=d)) for d in (1, 2, 3)]
    yield
    for copy in sent:
        copy.wait_recv()
    mine = total.at[rows(core * 128, 128)]
    copy = copies.start(mine, mine, sibling)
    yield
    copy.wait_recv()


def step_all(running):
    still = []
    for item in running:
        if next(item, "done") != "done":
            still.append(item)
    return still


def gather_kernel(
    halves_ref, rest_hbm, vec_hbm, tri_hbm, vec_high, vec_low, w_high, w_low, w_ref,
    vec_ref, rest_ref, tri_ref, av_col, av_row, vec_row, inner_ref, vec_middle,
    tiles, tile_high, tile_low, parts, rest_part, partial, row_sum, sibling_in, row_relay, col_relay,
    row_unit, col_unit, pair_in, swap_out, swap_in,
    first, first_in, second_in, third_in, fourth_in,
    load_sems, send_sems, recv_sems, vec_send_sems, vec_recv_sems,
):
    me = place()
    row, col, core = me["row"], me["col"], me["core"]
    x, lo, z, hi = me["x"], me["lo"], me["z"], me["hi"]
    sibling = moved(me, core=1)

    row_shift = (x - (x // 2 + 2 * core) + 4) % 4
    row_half = (lo + hi + x) % 2
    as_row = (((z + row_shift) % 4) * 2 + row_half, row + 8 * core)
    row_of = col % 8
    as_col = at(row_of // 2, row_of % 2, (x - row_of // 2 + z + 4) % 4, (lo + row_of + hi) % 2, col // 8)
    alone = jnp.logical_and(as_row[0] == row, as_row[1] == col)

    loads = [
        pltpu.make_async_copy(source, target, load_sems.at[i])
        for i, (source, target) in enumerate(
            ((vec_hbm, vec_ref), (halves_ref, tiles), (rest_hbm, rest_ref), (tri_hbm, tri_ref))
        )
    ]
    for load in loads:
        load.start()

    barrier = pltpu.get_barrier_semaphore()
    near = [moved(me, x=d) for d in (1, 2, 3)] + [moved(me, y=d) for d in (1, 2, 3)]
    near += [moved(me, z=d) for d in (1, 2, 3)] + [sibling]
    for device in near:
        pl.semaphore_signal(barrier, inc=1, device_id=device, device_id_type=MESH)

    @pl.when(jnp.logical_not(alone))
    def _():
        for device in (as_row, as_col):
            pl.semaphore_signal(barrier, inc=1, device_id=device, device_id_type=MESH)

    pl.semaphore_wait(barrier, len(near) + jnp.where(alone, 0, 2).astype(jnp.int32))

    copies = Copies(send_sems, recv_sems)
    z_ring = (z, row_shift, moved(me, z=1), moved(me, z=3))
    x_ring = (x, 0, moved(me, x=1), moved(me, x=3))
    spread = Spread(me, vec_ref, vec_row, vec_send_sems, vec_recv_sems)
    loads[0].wait()
    spread.begin()
    vec_high[0], vec_low[0] = split(vec_ref[...])
    loads[1].wait()

    def facts(position):
        block_row = row + 8 * position
        return block_row >= col, jnp.where(block_row == col, 0.5, 1.0).astype(jnp.float32)

    def upper(which):
        return vec_high[which, 0:HALF], vec_low[which, 0:HALF]

    def lower(which):
        return vec_high[which, HALF:TILE], vec_low[which, HALF:TILE]

    def whole(which):
        return vec_high[which], vec_low[which]

    def row_part(position):
        is_lower, weight = facts(position)
        tile_high[position], tile_low[position] = split(tiles[position])
        tile = tile_high.at[position], tile_low.at[position]

        @pl.when(is_lower)
        def _():
            parts[1 + position, 0:HALF] = product((tile[0][...], tile[1][...]), whole(0), NN) * weight
            parts[1 + position, HALF:TILE] = jnp.zeros((HALF, WIDTH), jnp.float32)

        @pl.when(jnp.logical_not(is_lower))
        def _():
            parts[1 + position] = product((tile[0][...], tile[1][...]), lower(0), TN)

    def col_part(position):
        is_lower, weight = facts(position)
        tile = tile_high.at[position], tile_low.at[position]

        @pl.when(is_lower)
        def _():
            parts[0] += product((tile[0][...], tile[1][...]), upper(1 + position), TN) * weight

        @pl.when(jnp.logical_not(is_lower))
        def _():
            parts[0, HALF:TILE] += product((tile[0][...], tile[1][...]), whole(1 + position), NN)

    row_part(1 - core)
    pair = copies.start(parts.at[2 - core], sibling_in, sibling)
    spread.serve(0)
    row_part(core)
    spread.serve(1)
    spread.serve(2)
    rest_rows = rows(HALF + row * REST, REST)
    loads[2].wait()
    block = split(rest_ref[...])
    rest_part[...] = product(block, whole(0), NN) * 0.5
    parts[0] = product(block, (vec_high[0, rest_rows, :], vec_low[0, rest_rows, :]), TN) * 0.5
    spread.serve(3)
    spread.serve(4)
    pair.wait_recv()
    row_sum[...] = parts[1 + core] + sibling_in[...]
    spread.serve(5)
    row_scatter = ring_scatter(copies, row_sum, row_unit, row_relay, *z_ring)
    next(row_scatter)
    spread.serve(6)
    spread.serve(7)
    spread.end()
    vec_high[1], vec_low[1] = split(vec_row[0])
    col_part(0)
    vec_high[2], vec_low[2] = split(vec_row[1])
    col_part(1)
    partial[...] = product(whole(0), split(parts[0]), TN)
    parts[0, rest_rows, :] += rest_part[...]
    columns = ring_scatter(copies, parts.at[0], col_unit, col_relay, *x_ring)
    next(columns)
    inner = inner_sum(
        copies, me, partial, inner_ref, (first, first_in, second_in, third_in, fourth_in)
    )
    next(inner)
    loads[3].wait()
    tri = split(tri_ref[...])
    next(row_scatter)
    next(inner)
    next(columns)
    step_all([row_scatter])

    keep_row, keep_col = rows(row_half * PIECE, PIECE), rows(lo * PIECE, PIECE)
    give_row, give_col = rows((1 - row_half) * PIECE, PIECE), rows((1 - lo) * PIECE, PIECE)
    row_partner = moved(me, y=2)
    col_partner = at(x, 1 - lo, z, hi, core)
    next(inner)
    row_copy = copies.start(row_unit.at[give_row], pair_in.at[0], row_partner)
    step_all([columns])
    col_copy = copies.start(col_unit.at[give_col], pair_in.at[1], col_partner)
    next(inner)
    row_copy.wait_recv()
    swap_out[0] = product(split(row_unit[keep_row, :] + pair_in[0]), tri, NN)
    row_copy = copies.make(swap_out.at[0], swap_in.at[0], as_row)

    @pl.when(jnp.logical_not(alone))
    def _():
        row_copy.start()

    col_copy.wait_recv()
    swap_out[1] = product(split(col_unit[keep_col, :] + pair_in[1]), tri, NN)
    col_copy = copies.make(swap_out.at[1], swap_in.at[1], as_col)

    @pl.when(jnp.logical_not(alone))
    def _():
        col_copy.start()

    @pl.when(alone)
    def _():
        swap_in[...] = swap_out[...]

    next(inner)

    @pl.when(jnp.logical_not(alone))
    def _():
        row_copy.wait()

    av_col[rows(x * UNIT + lo * PIECE, PIECE), :] = swap_out[1] + swap_in[0]
    columns = ring_gather(copies, av_col, *x_ring, lo, col_partner)
    next(columns)
    next(inner)

    @pl.when(jnp.logical_not(alone))
    def _():
        col_copy.wait()

    av_row[core, rows(((z + row_shift) % 4) * UNIT + row_half * PIECE, PIECE), :] = swap_out[0] + swap_in[1]
    rows_in = ring_gather(copies, av_row.at[core], *z_ring, row_half, row_partner, sibling)
    next(rows_in)
    next(columns)
    step_all([inner])
    next(rows_in)
    next(columns)
    whole_inner = inner_ref[...] + inner_ref[...].T
    middle = split(product(split(product(tri, split(whole_inner), TN)), tri, NN) * 0.5)
    vec_middle[0] = product(whole(0), middle, NN)
    next(rows_in)
    next(columns)
    vec_middle[1] = product(whole(1), middle, NN)
    next(rows_in)
    next(columns)
    vec_middle[2] = product(whole(2), middle, NN)
    step_all([columns])
    w = av_col[...] - vec_middle[0]
    w_ref[...] = w
    w_high[0], w_low[0] = split(w)
    next(rows_in)
    step_all([rows_in])
    for position in range(2):
        w_high[1 + position], w_low[1 + position] = split(av_row[position] - vec_middle[1 + position])
    copies.finish()
    spread.finish()


def update_kernel(
    halves_ref, rest_ref, vec_high, vec_low, w_high, w_low, w_ref, out_ref, out_rest, out_w,
    tiles, rest, load_sems, store_sems, side_sems,
):
    row, col = lax.axis_index("row"), lax.axis_index("col")
    count, _, size = tiles.shape
    each = TILE // size

    def place_of(ref, at_step):
        return ref.at[at_step // each, :, pl.ds(pl.multiple_of((at_step % each) * size, size), size)]

    def load(at_step):
        return pltpu.make_async_copy(place_of(halves_ref, at_step), tiles.at[at_step], load_sems.at[at_step])

    def store(at_step):
        return pltpu.make_async_copy(tiles.at[at_step], place_of(out_ref, at_step), store_sems.at[at_step])

    w_copy = pltpu.make_async_copy(w_ref, out_w, side_sems.at[0])
    rest_in = pltpu.make_async_copy(rest_ref, rest, side_sems.at[1])
    rest_out = pltpu.make_async_copy(rest, out_rest, side_sems.at[2])
    for at_step in range(count):
        load(at_step).start()
    rest_in.start()
    w_copy.start()

    def one(at_step, carry):
        position = at_step // each
        is_lower = row + 8 * position >= col
        high_rows = rows(jnp.where(is_lower, 0, HALF), HALF)
        low_rows = rows((at_step % each) * size, size)
        low_at = jnp.where(is_lower, 0, 1 + position)
        high_at = jnp.where(is_lower, 1 + position, 0)
        update = product(
            (vec_high[high_at, high_rows, :], vec_low[high_at, high_rows, :]),
            (w_high[low_at, low_rows, :], w_low[low_at, low_rows, :]),
            NT,
        ) + product(
            (w_high[high_at, high_rows, :], w_low[high_at, high_rows, :]),
            (vec_high[low_at, low_rows, :], vec_low[low_at, low_rows, :]),
            NT,
        )
        load(at_step).wait()
        tiles[at_step] = tiles[at_step] - update
        store(at_step).start()
        return carry

    lax.fori_loop(0, count, one, 0)
    rest_rows = rows(HALF + row * REST, REST)
    update = product(
        (vec_high[0, rest_rows, :], vec_low[0, rest_rows, :]), (w_high[0], w_low[0]), NT
    ) + product((w_high[0, rest_rows, :], w_low[0, rest_rows, :]), (vec_high[0], vec_low[0]), NT)
    rest_in.wait()
    rest[...] = rest[...] - update
    rest_out.start()
    for at_step in range(count):
        store(at_step).wait()
    w_copy.wait()
    rest_out.wait()


def shards(halves, diag_rest, panel_vectors, tri_factor):
    vmem = pl.BlockSpec(memory_space=pltpu.VMEM)
    outside = pl.BlockSpec(memory_space=pltpu.HBM)
    f32 = jnp.float32
    block = (TILE, WIDTH)

    def buffer(*shape):
        return pltpu.VMEM(shape, f32)

    held = pltpu.with_memory_space_constraint
    diag_rest, panel_vectors, tri_factor = (held(value, pltpu.HBM) for value in (diag_rest, panel_vectors, tri_factor))
    terms = jax.ShapeDtypeStruct((3,) + block, jnp.bfloat16)
    handed = pl.pallas_call(
        gather_kernel,
        out_shape=[terms, terms, terms, terms, jax.ShapeDtypeStruct(block, f32)],
        in_specs=[outside] * 4,
        out_specs=[vmem] * 5,
        scratch_shapes=[
            buffer(*block),
            buffer(REST, TILE),
            buffer(WIDTH, WIDTH),
            buffer(*block),
            buffer(2, *block),
            buffer(2, *block),
            buffer(WIDTH, WIDTH),
            buffer(3, *block),
            buffer(2, HALF, TILE),
            pltpu.VMEM((2, HALF, TILE), jnp.bfloat16),
            pltpu.VMEM((2, HALF, TILE), jnp.bfloat16),
            buffer(3, *block),
            buffer(REST, WIDTH),
            buffer(WIDTH, WIDTH),
            buffer(*block),
            buffer(*block),
            buffer(8, PIECE, WIDTH),
            buffer(8, PIECE, WIDTH),
            buffer(UNIT, WIDTH),
            buffer(UNIT, WIDTH),
            buffer(2, PIECE, WIDTH),
            buffer(2, PIECE, WIDTH),
            buffer(2, PIECE, WIDTH),
            buffer(128, WIDTH),
            buffer(128, WIDTH),
            buffer(3, 32, WIDTH),
            buffer(4, 32, WIDTH),
            buffer(4, 32, WIDTH),
            pltpu.SemaphoreType.DMA((4,)),
            pltpu.SemaphoreType.DMA((80,)),
            pltpu.SemaphoreType.DMA((80,)),
            pltpu.SemaphoreType.DMA((40,)),
            pltpu.SemaphoreType.DMA((40,)),
        ],
        compiler_params=pltpu.CompilerParams(
            collective_id=0, has_side_effects=True, vmem_limit_bytes=44 * 2**20
        ),
        name="gather",
    )(halves, diag_rest, panel_vectors, tri_factor)

    size = 256
    count = 2 * TILE // size
    return pl.pallas_call(
        update_kernel,
        out_shape=[
            jax.ShapeDtypeStruct(halves.shape, f32),
            jax.ShapeDtypeStruct(diag_rest.shape, f32),
            jax.ShapeDtypeStruct(panel_vectors.shape, f32),
        ],
        in_specs=[outside] * 2 + [vmem] * 5,
        out_specs=[outside] * 3,
        scratch_shapes=[
            buffer(count, HALF, size),
            buffer(REST, TILE),
            pltpu.SemaphoreType.DMA((count,)),
            pltpu.SemaphoreType.DMA((count,)),
            pltpu.SemaphoreType.DMA((3,)),
        ],
        compiler_params=pltpu.CompilerParams(vmem_limit_bytes=24 * 2**20),
        name="update",
    )(halves, diag_rest, *handed)


def solution(mesh):
    return jax.shard_map(
        shards,
        mesh=mesh,
        in_specs=(P(None, "row", "col"), P(("col", "row"), None), P("col", None), P()),
        out_specs=(P(None, "row", "col"), P(("col", "row"), None), P("col", None)),
        check_vma=False,
    )
```

```python
import functools

import jax
import jax.numpy as jnp
from jax import lax
from jax.experimental import pallas as pl
from jax.experimental.pallas import tpu as pltpu
from jax.sharding import PartitionSpec as P

MESH = pl.DeviceIdType.MESH
NN = (((1,), (0,)), ((), ()))
TN = (((0,), (0,)), ((), ()))
NT = (((1,), (1,)), ((), ()))
TILE = 1024
HALF = 512
WIDTH = 256
UNIT = 256
PIECE = 128
REST = 64


def split(value):
    high = value.astype(jnp.bfloat16)
    low = (value - high.astype(jnp.float32)).astype(jnp.bfloat16)
    return high, low


def product(left, right, dims):
    def dot(a, b):
        return lax.dot_general(a, b, dims, preferred_element_type=jnp.float32)

    return dot(left[0], right[0]) + (dot(left[0], right[1]) + dot(left[1], right[0]))


def rows(start, size):
    return pl.ds(pl.multiple_of(start, 8), size)


def place():
    row, col = lax.axis_index("row"), lax.axis_index("col")
    return dict(row=row, col=col, x=row // 2, lo=row % 2, z=col // 4, hi=(col // 2) % 2, core=col % 2)


def at(x, lo, z, hi, core):
    return (x * 2 + lo, z * 4 + hi * 2 + core)


def moved(me, x=0, y=0, z=0, core=0):
    y_at = (me["hi"] * 2 + me["lo"] + y) % 4
    return at((me["x"] + x) % 4, y_at % 2, (me["z"] + z) % 4, y_at // 2, (me["core"] + core) % 2)


class Copies:
    def __init__(self, send_sems, recv_sems):
        self.send_sems, self.recv_sems, self.used, self.started = send_sems, recv_sems, 0, []

    def make(self, source, target, device):
        copy = pltpu.make_async_remote_copy(
            src_ref=source,
            dst_ref=target,
            send_sem=self.send_sems.at[self.used],
            recv_sem=self.recv_sems.at[self.used],
            device_id=device,
            device_id_type=MESH,
        )
        self.used += 1
        return copy

    def start(self, source, target, device):
        copy = self.make(source, target, device)
        copy.start()
        self.started.append(copy)
        return copy

    def finish(self):
        for copy in self.started:
            copy.wait_send()


def ring_scatter(copies, source, out, relay, index, shift, plus, minus):
    def part(step, half):
        return source.at[rows(((index + step + shift) % 4) * UNIT + half * PIECE, PIECE)]

    far_plus = copies.start(part(2, 0), relay.at[0], plus)
    far_minus = copies.start(part(2, 1), relay.at[1], minus)
    near_plus = copies.start(part(1, 1), relay.at[2], plus)
    near_minus = copies.start(part(3, 0), relay.at[3], minus)
    yield
    far_plus.wait_recv()
    relay[6] = relay[0] + part(1, 0)[...]
    sum_plus = copies.start(relay.at[6], relay.at[4], plus)
    far_minus.wait_recv()
    relay[7] = relay[1] + part(3, 1)[...]
    sum_minus = copies.start(relay.at[7], relay.at[5], minus)
    yield
    near_plus.wait_recv()
    near_minus.wait_recv()
    sum_plus.wait_recv()
    sum_minus.wait_recv()
    out[0:PIECE] = part(0, 0)[...] + (relay[4] + relay[3])
    out[PIECE:UNIT] = part(0, 1)[...] + (relay[2] + relay[5])


def ring_gather(copies, block, index, shift, plus, minus, kept, partner, sibling=None):
    def piece(step, which):
        return block.at[rows(((index + step + shift) % 4) * UNIT + which * PIECE, PIECE)]

    given = 1 - kept
    shared = []

    def part(step, which, at_half):
        start = ((index + step + shift) % 4) * UNIT + which * PIECE + at_half * (PIECE // 2)
        return block.at[rows(start, PIECE // 2)]

    def share(ref):
        if sibling is not None:
            shared.append(copies.start(ref, ref, sibling))

    def send(ref, device):
        return copies.start(ref, ref, device)

    own = piece(0, kept)
    pair = [send(part(0, kept, half), partner) for half in (0, 1)]
    own_plus, own_minus = send(own, plus), send(own, minus)
    share(own)
    yield
    other_plus, other_minus = [], []
    for half in (0, 1):
        pair[half].wait_recv()
        other_minus.append(send(part(0, given, half), minus))
        other_plus.append(send(part(0, given, half), plus))
    share(piece(0, given))
    yield
    own_plus.wait_recv()
    far_plus = send(piece(3, kept), plus)
    share(piece(3, kept))
    own_minus.wait_recv()
    share(piece(1, kept))
    yield
    far_minus = []
    for half in (0, 1):
        other_minus[half].wait_recv()
        far_minus.append(send(part(1, given, half), minus))
    share(piece(1, given))
    for copy in other_plus:
        copy.wait_recv()
    share(piece(3, given))
    yield
    far_plus.wait_recv()
    share(piece(2, kept))
    for half in (0, 1):
        far_minus[half].wait_recv()
        share(part(2, given, half))
    yield
    for copy in shared:
        copy.wait_recv()


CHUNKS = 16
CHUNK = TILE // CHUNKS
ORDER = [half + c for c in range(CHUNKS // 2) for half in (0, CHUNKS // 2)]


class Spread:
    def __init__(self, me, vec_ref, vec_row, send_sems, recv_sems):
        x, lo, z, hi, core = me["x"], me["lo"], me["z"], me["hi"], me["core"]
        self.vec_ref, self.vec_row, self.send_sems, self.recv_sems = vec_ref, vec_row, send_sems, recv_sems
        self.lead = core == lo
        line = hi == x % 2
        end = z % 2 == x // 2
        self.source = jnp.logical_and(jnp.logical_and(self.lead, line), end)
        self.cross = jnp.logical_and(jnp.logical_and(jnp.logical_not(self.lead), line), end)
        self.target = jnp.logical_and(jnp.logical_and(self.lead, jnp.logical_not(line)), end)
        self.ends = jnp.logical_and(self.lead, end)
        self.middle = jnp.logical_and(self.lead, jnp.logical_not(end))
        self.follow = jnp.logical_not(self.lead)
        self.plus, self.minus, self.sibling = moved(me, z=1), moved(me, z=3), moved(me, core=1)
        self.over = at(x, core, z, 1 - hi, core)
        self.own = z // 2
        self.from_minus = ((z + 3) % 4) // 2

    def chunk(self, block, c):
        return self.vec_row.at[block, pl.ds(c * CHUNK, CHUNK)]

    def copy(self, slot, source, target, device):
        return pltpu.make_async_remote_copy(
            src_ref=source,
            dst_ref=target,
            send_sem=self.send_sems.at[slot],
            recv_sem=self.recv_sems.at[slot],
            device_id=device,
            device_id_type=MESH,
        )

    def mine(self, c):
        return self.vec_ref.at[pl.ds(c * CHUNK, CHUNK)]

    def along(self, c, block, source=None):
        here = self.chunk(block, c)
        return self.copy(c, here if source is None else source, here, self.plus)

    def back(self, c, block, source=None):
        here = self.chunk(block, c)
        return self.copy(CHUNKS + c, here if source is None else source, here, self.minus)

    def across(self, c):
        return self.copy(2 * CHUNKS + c, self.mine(c), self.chunk(self.own, c), self.over)

    def share(self, c, block, which, source=None):
        here = self.chunk(block, c)
        return self.copy((3 + which) * CHUNKS + c, here if source is None else source, here, self.sibling)

    def begin(self):
        @pl.when(self.source)
        def _():
            for c in ORDER:
                self.along(c, self.own, self.mine(c)).start()
                self.back(c, self.own, self.mine(c)).start()
                self.share(c, self.own, 0, self.mine(c)).start()
            self.vec_row[self.own] = self.vec_ref[...]

        @pl.when(self.cross)
        def _():
            for c in ORDER:
                self.across(c).start()

    def serve(self, *steps):
        for step in steps:
            self.pass_on(ORDER[2 * step])
            self.pass_on(ORDER[2 * step + 1])

    def pass_on(self, c):
        @pl.when(self.target)
        def _():
            self.across(c).wait_recv()
            self.along(c, self.own).start()
            self.back(c, self.own).start()
            self.share(c, self.own, 0).start()

        @pl.when(self.middle)
        def _():
            block = self.from_minus
            self.along(c, block).wait_recv()
            if c < CHUNKS // 2:
                self.along(c, block).start()
            self.share(c, block, 0).start()
            self.back(c, 1 - block).wait_recv()
            if c >= CHUNKS // 2:
                self.back(c, 1 - block).start()
            self.share(c, 1 - block, 1).start()

    def end(self):
        @pl.when(self.ends)
        def _():
            for c in ORDER:
                copy = self.along(c, 1 - self.own) if c < CHUNKS // 2 else self.back(c, 1 - self.own)
                copy.wait_recv()
                self.share(c, 1 - self.own, 1).start()

        @pl.when(self.follow)
        def _():
            for c in ORDER:
                for which in range(2):
                    self.share(c, which, which).wait_recv()

    def finish(self):
        @pl.when(self.ends)
        def _():
            for c in ORDER:
                self.along(c, self.own).wait_send()
                self.back(c, self.own).wait_send()

        @pl.when(self.middle)
        def _():
            for c in ORDER:
                if c < CHUNKS // 2:
                    self.along(c, 0).wait_send()
                else:
                    self.back(c, 0).wait_send()

        @pl.when(self.lead)
        def _():
            for c in ORDER:
                for which in range(2):
                    self.share(c, which, which).wait_send()

        @pl.when(self.cross)
        def _():
            for c in ORDER:
                self.across(c).wait_send()


def inner_sum(copies, me, partial, total, work):
    first, first_in, second_in, third_in, fourth_in = work
    sibling = moved(me, core=1)
    core, x, y, z = me["core"], me["x"], me["hi"] * 2 + me["lo"], me["z"]
    copy = copies.start(partial.at[rows((1 - core) * 128, 128)], first_in, sibling)
    yield
    copy.wait_recv()
    first[...] = partial[rows(core * 128, 128), :] + first_in[...]
    sent = [
        copies.start(first.at[rows(((y + d) % 4) * 32, 32)], second_in.at[d - 1], moved(me, y=d)) for d in (1, 2, 3)
    ]
    yield
    for copy in sent:
        copy.wait_recv()
    mine = third_in.at[z]
    mine[...] = first[rows(y * 32, 32), :] + second_in[0] + second_in[1] + second_in[2]
    sent = [copies.start(mine, mine, moved(me, z=d)) for d in (1, 2, 3)]
    yield
    for copy in sent:
        copy.wait_recv()
    mine = fourth_in.at[x]
    mine[...] = third_in[0] + third_in[1] + third_in[2] + third_in[3]
    sent = [copies.start(mine, mine, moved(me, x=d)) for d in (1, 2, 3)]
    yield
    for copy in sent:
        copy.wait_recv()
    mine = total.at[rows(core * 128 + y * 32, 32)]
    mine[...] = fourth_in[0] + fourth_in[1] + fourth_in[2] + fourth_in[3]
    sent = [copies.start(mine, mine, moved(me, y=d)) for d in (1, 2, 3)]
    yield
    for copy in sent:
        copy.wait_recv()
    mine = total.at[rows(core * 128, 128)]
    copy = copies.start(mine, mine, sibling)
    yield
    copy.wait_recv()


def step_all(running):
    still = []
    for item in running:
        if next(item, "done") != "done":
            still.append(item)
    return still


def gather_kernel(
    halves_ref, rest_hbm, vec_hbm, tri_hbm, vec_high, vec_low, w_high, w_low, w_ref,
    vec_ref, rest_ref, tri_ref, av_col, av_row, vec_row, inner_ref, vec_middle,
    tiles, tile_high, tile_low, col_high, col_low, parts, rest_part, partial, row_sum, sibling_in, row_relay, col_relay,
    row_unit, col_unit, pair_in, swap_out, swap_in,
    first, first_in, second_in, third_in, fourth_in,
    load_sems, send_sems, recv_sems, vec_send_sems, vec_recv_sems,
):
    me = place()
    row, col, core = me["row"], me["col"], me["core"]
    x, lo, z, hi = me["x"], me["lo"], me["z"], me["hi"]
    sibling = moved(me, core=1)

    row_shift = (x - (x // 2 + 2 * core) + 4) % 4
    row_half = (lo + hi + x) % 2
    as_row = (((z + row_shift) % 4) * 2 + row_half, row + 8 * core)
    row_of = col % 8
    as_col = at(row_of // 2, row_of % 2, (x - row_of // 2 + z + 4) % 4, (lo + row_of + hi) % 2, col // 8)
    alone = jnp.logical_and(as_row[0] == row, as_row[1] == col)

    loads = [
        pltpu.make_async_copy(source, target, load_sems.at[i])
        for i, (source, target) in enumerate(
            ((vec_hbm, vec_ref), (halves_ref, tiles), (rest_hbm, rest_ref), (tri_hbm, tri_ref))
        )
    ]
    for load in loads:
        load.start()

    barrier = pltpu.get_barrier_semaphore()
    near = [moved(me, x=d) for d in (1, 2, 3)] + [moved(me, y=d) for d in (1, 2, 3)]
    near += [moved(me, z=d) for d in (1, 2, 3)] + [sibling]
    for device in near:
        pl.semaphore_signal(barrier, inc=1, device_id=device, device_id_type=MESH)

    @pl.when(jnp.logical_not(alone))
    def _():
        for device in (as_row, as_col):
            pl.semaphore_signal(barrier, inc=1, device_id=device, device_id_type=MESH)

    pl.semaphore_wait(barrier, len(near) + jnp.where(alone, 0, 2).astype(jnp.int32))

    copies = Copies(send_sems, recv_sems)
    z_ring = (z, row_shift, moved(me, z=1), moved(me, z=3))
    x_ring = (x, 0, moved(me, x=1), moved(me, x=3))
    spread = Spread(me, vec_ref, vec_row, vec_send_sems, vec_recv_sems)
    loads[0].wait()
    spread.begin()
    vec_high[0], vec_low[0] = split(vec_ref[...])
    loads[1].wait()

    def facts(position):
        block_row = row + 8 * position
        return block_row >= col, jnp.where(block_row == col, 0.5, 1.0).astype(jnp.float32)

    def upper(which):
        return vec_high[which, 0:HALF], vec_low[which, 0:HALF]

    def lower(which):
        return vec_high[which, HALF:TILE], vec_low[which, HALF:TILE]

    def whole(which):
        return vec_high[which], vec_low[which]

    def row_part(position):
        is_lower, weight = facts(position)
        tile_high[position], tile_low[position] = split(tiles[position])
        tile = tile_high.at[position], tile_low.at[position]

        @pl.when(is_lower)
        def _():
            parts[1 + position, 0:HALF] = product((tile[0][...], tile[1][...]), whole(0), NN) * weight
            parts[1 + position, HALF:TILE] = jnp.zeros((HALF, WIDTH), jnp.float32)

        @pl.when(jnp.logical_not(is_lower))
        def _():
            parts[1 + position] = product((tile[0][...], tile[1][...]), lower(0), TN)

    def col_part(position):
        is_lower, weight = facts(position)
        tile = tile_high.at[position], tile_low.at[position]

        @pl.when(is_lower)
        def _():
            parts[0] += product((tile[0][...], tile[1][...]), upper(1 + position), TN) * weight

        @pl.when(jnp.logical_not(is_lower))
        def _():
            parts[0, HALF:TILE] += product((tile[0][...], tile[1][...]), whole(1 + position), NN)

    row_part(1 - core)
    pair = copies.start(parts.at[2 - core], sibling_in, sibling)
    spread.serve(0)
    row_part(core)
    spread.serve(1)
    spread.serve(2)
    rest_rows = rows(HALF + row * REST, REST)
    loads[2].wait()
    block = split(rest_ref[...])
    rest_part[...] = product(block, whole(0), NN) * 0.5
    parts[0] = product(block, (vec_high[0, rest_rows, :], vec_low[0, rest_rows, :]), TN) * 0.5
    spread.serve(3)
    spread.serve(4)
    pair.wait_recv()
    row_sum[...] = parts[1 + core] + sibling_in[...]
    spread.serve(5)
    row_scatter = ring_scatter(copies, row_sum, row_unit, row_relay, *z_ring)
    next(row_scatter)
    spread.serve(6)
    spread.serve(7)
    spread.end()
    vec_high[1], vec_low[1] = split(vec_row[0])
    col_part(0)
    vec_high[2], vec_low[2] = split(vec_row[1])
    col_part(1)
    col_high[...], col_low[...] = split(parts[0])
    parts[0, rest_rows, :] += rest_part[...]
    columns = ring_scatter(copies, parts.at[0], col_unit, col_relay, *x_ring)
    next(columns)
    partial[...] = product(whole(0), (col_high[...], col_low[...]), TN)
    inner = inner_sum(
        copies, me, partial, inner_ref, (first, first_in, second_in, third_in, fourth_in)
    )
    next(inner)
    loads[3].wait()
    tri = split(tri_ref[...])
    next(row_scatter)
    next(inner)
    next(columns)
    step_all([row_scatter])

    keep_row, keep_col = rows(row_half * PIECE, PIECE), rows(lo * PIECE, PIECE)
    give_row, give_col = rows((1 - row_half) * PIECE, PIECE), rows((1 - lo) * PIECE, PIECE)
    row_partner = moved(me, y=2)
    col_partner = at(x, 1 - lo, z, hi, core)
    next(inner)
    row_copy = copies.start(row_unit.at[give_row], pair_in.at[0], row_partner)
    step_all([columns])
    col_copy = copies.start(col_unit.at[give_col], pair_in.at[1], col_partner)
    next(inner)
    row_copy.wait_recv()
    swap_out[0] = product(split(row_unit[keep_row, :] + pair_in[0]), tri, NN)
    row_copy = copies.make(swap_out.at[0], swap_in.at[0], as_row)

    @pl.when(jnp.logical_not(alone))
    def _():
        row_copy.start()

    col_copy.wait_recv()
    swap_out[1] = product(split(col_unit[keep_col, :] + pair_in[1]), tri, NN)
    col_copy = copies.make(swap_out.at[1], swap_in.at[1], as_col)

    @pl.when(jnp.logical_not(alone))
    def _():
        col_copy.start()

    @pl.when(alone)
    def _():
        swap_in[...] = swap_out[...]

    next(inner)

    @pl.when(jnp.logical_not(alone))
    def _():
        row_copy.wait()

    av_col[rows(x * UNIT + lo * PIECE, PIECE), :] = swap_out[1] + swap_in[0]
    columns = ring_gather(copies, av_col, *x_ring, lo, col_partner)
    next(columns)
    next(inner)

    @pl.when(jnp.logical_not(alone))
    def _():
        col_copy.wait()

    av_row[core, rows(((z + row_shift) % 4) * UNIT + row_half * PIECE, PIECE), :] = swap_out[0] + swap_in[1]
    rows_in = ring_gather(copies, av_row.at[core], *z_ring, row_half, row_partner, sibling)
    next(rows_in)
    next(columns)
    step_all([inner])
    next(rows_in)
    next(columns)
    whole_inner = inner_ref[...] + inner_ref[...].T
    middle = split(product(split(product(tri, split(whole_inner), TN)), tri, NN) * 0.5)
    vec_middle[0] = product(whole(0), middle, NN)
    next(rows_in)
    next(columns)
    vec_middle[1] = product(whole(1), middle, NN)
    next(rows_in)
    next(columns)
    vec_middle[2] = product(whole(2), middle, NN)
    step_all([columns])
    w = av_col[...] - vec_middle[0]
    w_ref[...] = w
    w_high[0], w_low[0] = split(w)
    next(rows_in)
    step_all([rows_in])
    for position in range(2):
        w_high[1 + position], w_low[1 + position] = split(av_row[position] - vec_middle[1 + position])
    copies.finish()
    spread.finish()


def update_kernel(
    halves_ref, rest_ref, vec_high, vec_low, w_high, w_low, w_ref, out_ref, out_rest, out_w,
    tiles, rest, load_sems, store_sems, side_sems,
):
    row, col = lax.axis_index("row"), lax.axis_index("col")
    count, _, size = tiles.shape
    each = TILE // size

    def place_of(ref, at_step):
        return ref.at[at_step // each, :, pl.ds(pl.multiple_of((at_step % each) * size, size), size)]

    def load(at_step):
        return pltpu.make_async_copy(place_of(halves_ref, at_step), tiles.at[at_step], load_sems.at[at_step])

    def store(at_step):
        return pltpu.make_async_copy(tiles.at[at_step], place_of(out_ref, at_step), store_sems.at[at_step])

    w_copy = pltpu.make_async_copy(w_ref, out_w, side_sems.at[0])
    rest_in = pltpu.make_async_copy(rest_ref, rest, side_sems.at[1])
    rest_out = pltpu.make_async_copy(rest, out_rest, side_sems.at[2])
    for at_step in range(count):
        load(at_step).start()
    rest_in.start()
    w_copy.start()

    def one(at_step, carry):
        position = at_step // each
        is_lower = row + 8 * position >= col
        high_rows = rows(jnp.where(is_lower, 0, HALF), HALF)
        low_rows = rows((at_step % each) * size, size)
        low_at = jnp.where(is_lower, 0, 1 + position)
        high_at = jnp.where(is_lower, 1 + position, 0)
        update = product(
            (vec_high[high_at, high_rows, :], vec_low[high_at, high_rows, :]),
            (w_high[low_at, low_rows, :], w_low[low_at, low_rows, :]),
            NT,
        ) + product(
            (w_high[high_at, high_rows, :], w_low[high_at, high_rows, :]),
            (vec_high[low_at, low_rows, :], vec_low[low_at, low_rows, :]),
            NT,
        )
        load(at_step).wait()
        tiles[at_step] = tiles[at_step] - update
        store(at_step).start()
        return carry

    lax.fori_loop(0, count, one, 0)
    rest_rows = rows(HALF + row * REST, REST)
    update = product(
        (vec_high[0, rest_rows, :], vec_low[0, rest_rows, :]), (w_high[0], w_low[0]), NT
    ) + product((w_high[0, rest_rows, :], w_low[0, rest_rows, :]), (vec_high[0], vec_low[0]), NT)
    rest_in.wait()
    rest[...] = rest[...] - update
    rest_out.start()
    for at_step in range(count):
        store(at_step).wait()
    w_copy.wait()
    rest_out.wait()


def shards(halves, diag_rest, panel_vectors, tri_factor):
    vmem = pl.BlockSpec(memory_space=pltpu.VMEM)
    outside = pl.BlockSpec(memory_space=pltpu.HBM)
    f32 = jnp.float32
    block = (TILE, WIDTH)

    def buffer(*shape):
        return pltpu.VMEM(shape, f32)

    held = pltpu.with_memory_space_constraint
    diag_rest, panel_vectors, tri_factor = (held(value, pltpu.HBM) for value in (diag_rest, panel_vectors, tri_factor))
    terms = jax.ShapeDtypeStruct((3,) + block, jnp.bfloat16)
    handed = pl.pallas_call(
        gather_kernel,
        out_shape=[terms, terms, terms, terms, jax.ShapeDtypeStruct(block, f32)],
        in_specs=[outside] * 4,
        out_specs=[vmem] * 5,
        scratch_shapes=[
            buffer(*block),
            buffer(REST, TILE),
            buffer(WIDTH, WIDTH),
            buffer(*block),
            buffer(2, *block),
            buffer(2, *block),
            buffer(WIDTH, WIDTH),
            buffer(3, *block),
            buffer(2, HALF, TILE),
            pltpu.VMEM((2, HALF, TILE), jnp.bfloat16),
            pltpu.VMEM((2, HALF, TILE), jnp.bfloat16),
            pltpu.VMEM(block, jnp.bfloat16),
            pltpu.VMEM(block, jnp.bfloat16),
            buffer(3, *block),
            buffer(REST, WIDTH),
            buffer(WIDTH, WIDTH),
            buffer(*block),
            buffer(*block),
            buffer(8, PIECE, WIDTH),
            buffer(8, PIECE, WIDTH),
            buffer(UNIT, WIDTH),
            buffer(UNIT, WIDTH),
            buffer(2, PIECE, WIDTH),
            buffer(2, PIECE, WIDTH),
            buffer(2, PIECE, WIDTH),
            buffer(128, WIDTH),
            buffer(128, WIDTH),
            buffer(3, 32, WIDTH),
            buffer(4, 32, WIDTH),
            buffer(4, 32, WIDTH),
            pltpu.SemaphoreType.DMA((4,)),
            pltpu.SemaphoreType.DMA((80,)),
            pltpu.SemaphoreType.DMA((80,)),
            pltpu.SemaphoreType.DMA((5 * CHUNKS,)),
            pltpu.SemaphoreType.DMA((5 * CHUNKS,)),
        ],
        compiler_params=pltpu.CompilerParams(
            collective_id=0, has_side_effects=True, vmem_limit_bytes=44 * 2**20
        ),
        name="gather",
    )(halves, diag_rest, panel_vectors, tri_factor)

    size = 256
    count = 2 * TILE // size
    return pl.pallas_call(
        update_kernel,
        out_shape=[
            jax.ShapeDtypeStruct(halves.shape, f32),
            jax.ShapeDtypeStruct(diag_rest.shape, f32),
            jax.ShapeDtypeStruct(panel_vectors.shape, f32),
        ],
        in_specs=[outside] * 2 + [vmem] * 5,
        out_specs=[outside] * 3,
        scratch_shapes=[
            buffer(count, HALF, size),
            buffer(REST, TILE),
            pltpu.SemaphoreType.DMA((count,)),
            pltpu.SemaphoreType.DMA((count,)),
            pltpu.SemaphoreType.DMA((3,)),
        ],
        compiler_params=pltpu.CompilerParams(vmem_limit_bytes=24 * 2**20),
        name="update",
    )(halves, diag_rest, *handed)


def solution(mesh):
    return jax.shard_map(
        shards,
        mesh=mesh,
        in_specs=(P(None, "row", "col"), P(("col", "row"), None), P("col", None), P()),
        out_specs=(P(None, "row", "col"), P(("col", "row"), None), P("col", None)),
        check_vma=False,
    )
```

```python
import functools

import jax
import jax.numpy as jnp
from jax import lax
from jax.experimental import pallas as pl
from jax.experimental.pallas import tpu as pltpu
from jax.sharding import PartitionSpec as P

MESH = pl.DeviceIdType.MESH
NN = (((1,), (0,)), ((), ()))
TN = (((0,), (0,)), ((), ()))
NT = (((1,), (1,)), ((), ()))
TILE = 1024
HALF = 512
WIDTH = 256
UNIT = 256
PIECE = 128
REST = 64


def split(value):
    high = value.astype(jnp.bfloat16)
    low = (value - high.astype(jnp.float32)).astype(jnp.bfloat16)
    return high, low


def product(left, right, dims):
    def dot(a, b):
        return lax.dot_general(a, b, dims, preferred_element_type=jnp.float32)

    return dot(left[0], right[0]) + (dot(left[0], right[1]) + dot(left[1], right[0]))


def rows(start, size):
    return pl.ds(pl.multiple_of(start, 8), size)


def place():
    row, col = lax.axis_index("row"), lax.axis_index("col")
    return dict(row=row, col=col, x=row // 2, lo=row % 2, z=col // 4, hi=(col // 2) % 2, core=col % 2)


def at(x, lo, z, hi, core):
    return (x * 2 + lo, z * 4 + hi * 2 + core)


def moved(me, x=0, y=0, z=0, core=0):
    y_at = (me["hi"] * 2 + me["lo"] + y) % 4
    return at((me["x"] + x) % 4, y_at % 2, (me["z"] + z) % 4, y_at // 2, (me["core"] + core) % 2)


class Copies:
    def __init__(self, send_sems, recv_sems):
        self.send_sems, self.recv_sems, self.used, self.started = send_sems, recv_sems, 0, []

    def make(self, source, target, device):
        copy = pltpu.make_async_remote_copy(
            src_ref=source,
            dst_ref=target,
            send_sem=self.send_sems.at[self.used],
            recv_sem=self.recv_sems.at[self.used],
            device_id=device,
            device_id_type=MESH,
        )
        self.used += 1
        return copy

    def start(self, source, target, device):
        copy = self.make(source, target, device)
        copy.start()
        self.started.append(copy)
        return copy

    def finish(self):
        for copy in self.started:
            copy.wait_send()


def ring_scatter(copies, source, out, relay, index, shift, plus, minus, kept, partner, pair_in):
    size = PIECE // 2
    given = 1 - kept

    def part(step, which, at_half):
        return source.at[rows(((index + step + shift) % 4) * UNIT + which * PIECE + at_half * size, size)]

    def far(base, which):
        return (
            copies.start(part(2, which, 0), relay.at[base], plus),
            copies.start(part(2, which, 1), relay.at[base + 1], minus),
        )

    def near(base, which):
        return (
            copies.start(part(1, which, 1), relay.at[base + 2], plus),
            copies.start(part(3, which, 0), relay.at[base + 3], minus),
        )

    def passed(base, which, arriving):
        arriving[0].wait_recv()
        relay[base + 6] = relay[base] + part(1, which, 0)[...]
        to_plus = copies.start(relay.at[base + 6], relay.at[base + 4], plus)
        arriving[1].wait_recv()
        relay[base + 7] = relay[base + 1] + part(3, which, 1)[...]
        return to_plus, copies.start(relay.at[base + 7], relay.at[base + 5], minus)

    def total(base, which, arriving):
        for copy in arriving:
            copy.wait_recv()
        out[rows(which * PIECE, size), :] = part(0, which, 0)[...] + (relay[base + 4] + relay[base + 3])
        out[rows(which * PIECE + size, size), :] = part(0, which, 1)[...] + (relay[base + 2] + relay[base + 5])

    far_given = far(0, given)
    near_given = near(0, given)
    far_kept = far(8, kept)
    yield
    sum_given = passed(0, given, far_given)
    near_kept = near(8, kept)
    yield
    sum_kept = passed(8, kept, far_kept)
    yield
    total(0, given, near_given + sum_given)
    pair = copies.start(out.at[rows(given * PIECE, PIECE)], pair_in, partner)
    yield
    total(8, kept, near_kept + sum_kept)
    yield
    pair.wait_recv()


def ring_gather(copies, block, index, shift, plus, minus, kept, partner, sibling=None):
    def piece(step, which):
        return block.at[rows(((index + step + shift) % 4) * UNIT + which * PIECE, PIECE)]

    given = 1 - kept
    shared = []

    def part(step, which, at_half):
        start = ((index + step + shift) % 4) * UNIT + which * PIECE + at_half * (PIECE // 2)
        return block.at[rows(start, PIECE // 2)]

    def share(ref):
        if sibling is not None:
            shared.append(copies.start(ref, ref, sibling))

    def send(ref, device):
        return copies.start(ref, ref, device)

    own = piece(0, kept)
    pair = [send(part(0, kept, half), partner) for half in (0, 1)]
    own_plus, own_minus = send(own, plus), send(own, minus)
    share(own)
    yield
    other_plus, other_minus = [], []
    for half in (0, 1):
        pair[half].wait_recv()
        other_minus.append(send(part(0, given, half), minus))
        other_plus.append(send(part(0, given, half), plus))
    share(piece(0, given))
    yield
    own_plus.wait_recv()
    far_plus = send(piece(3, kept), plus)
    share(piece(3, kept))
    own_minus.wait_recv()
    share(piece(1, kept))
    yield
    far_minus = []
    for half in (0, 1):
        other_minus[half].wait_recv()
        far_minus.append(send(part(1, given, half), minus))
    share(piece(1, given))
    for copy in other_plus:
        copy.wait_recv()
    share(piece(3, given))
    yield
    far_plus.wait_recv()
    share(piece(2, kept))
    for half in (0, 1):
        far_minus[half].wait_recv()
        share(part(2, given, half))
    yield
    for copy in shared:
        copy.wait_recv()


CHUNKS = 16
CHUNK = TILE // CHUNKS
ORDER = [half + c for c in range(CHUNKS // 2) for half in (0, CHUNKS // 2)]


class Spread:
    def __init__(self, me, vec_ref, vec_row, send_sems, recv_sems):
        x, lo, z, hi, core = me["x"], me["lo"], me["z"], me["hi"], me["core"]
        self.vec_ref, self.vec_row, self.send_sems, self.recv_sems = vec_ref, vec_row, send_sems, recv_sems
        self.lead = core == lo
        line = hi == x % 2
        end = z % 2 == x // 2
        self.source = jnp.logical_and(jnp.logical_and(self.lead, line), end)
        self.cross = jnp.logical_and(jnp.logical_and(jnp.logical_not(self.lead), line), end)
        self.target = jnp.logical_and(jnp.logical_and(self.lead, jnp.logical_not(line)), end)
        self.ends = jnp.logical_and(self.lead, end)
        self.middle = jnp.logical_and(self.lead, jnp.logical_not(end))
        self.follow = jnp.logical_not(self.lead)
        self.plus, self.minus, self.sibling = moved(me, z=1), moved(me, z=3), moved(me, core=1)
        self.over = at(x, core, z, 1 - hi, core)
        self.own = z // 2
        self.from_minus = ((z + 3) % 4) // 2

    def chunk(self, block, c):
        return self.vec_row.at[block, pl.ds(c * CHUNK, CHUNK)]

    def copy(self, slot, source, target, device):
        return pltpu.make_async_remote_copy(
            src_ref=source,
            dst_ref=target,
            send_sem=self.send_sems.at[slot],
            recv_sem=self.recv_sems.at[slot],
            device_id=device,
            device_id_type=MESH,
        )

    def mine(self, c):
        return self.vec_ref.at[pl.ds(c * CHUNK, CHUNK)]

    def along(self, c, block, source=None):
        here = self.chunk(block, c)
        return self.copy(c, here if source is None else source, here, self.plus)

    def back(self, c, block, source=None):
        here = self.chunk(block, c)
        return self.copy(CHUNKS + c, here if source is None else source, here, self.minus)

    def across(self, c):
        return self.copy(2 * CHUNKS + c, self.mine(c), self.chunk(self.own, c), self.over)

    def share(self, c, block, which, source=None):
        here = self.chunk(block, c)
        return self.copy((3 + which) * CHUNKS + c, here if source is None else source, here, self.sibling)

    def begin(self):
        @pl.when(self.source)
        def _():
            for c in ORDER:
                self.along(c, self.own, self.mine(c)).start()
                self.back(c, self.own, self.mine(c)).start()
                self.share(c, self.own, 0, self.mine(c)).start()
            self.vec_row[self.own] = self.vec_ref[...]

        @pl.when(self.cross)
        def _():
            for c in ORDER:
                self.across(c).start()

    def serve(self, *steps):
        for step in steps:
            self.pass_on(ORDER[2 * step])
            self.pass_on(ORDER[2 * step + 1])

    def pass_on(self, c):
        @pl.when(self.target)
        def _():
            self.across(c).wait_recv()
            self.along(c, self.own).start()
            self.back(c, self.own).start()
            self.share(c, self.own, 0).start()

        @pl.when(self.middle)
        def _():
            block = self.from_minus
            self.along(c, block).wait_recv()
            if c < CHUNKS // 2:
                self.along(c, block).start()
            self.share(c, block, 0).start()
            self.back(c, 1 - block).wait_recv()
            if c >= CHUNKS // 2:
                self.back(c, 1 - block).start()
            self.share(c, 1 - block, 1).start()

    def end(self):
        @pl.when(self.ends)
        def _():
            for c in ORDER:
                copy = self.along(c, 1 - self.own) if c < CHUNKS // 2 else self.back(c, 1 - self.own)
                copy.wait_recv()
                self.share(c, 1 - self.own, 1).start()

        @pl.when(self.follow)
        def _():
            for c in ORDER:
                for which in range(2):
                    self.share(c, which, which).wait_recv()

    def finish(self):
        @pl.when(self.ends)
        def _():
            for c in ORDER:
                self.along(c, self.own).wait_send()
                self.back(c, self.own).wait_send()

        @pl.when(self.middle)
        def _():
            for c in ORDER:
                if c < CHUNKS // 2:
                    self.along(c, 0).wait_send()
                else:
                    self.back(c, 0).wait_send()

        @pl.when(self.lead)
        def _():
            for c in ORDER:
                for which in range(2):
                    self.share(c, which, which).wait_send()

        @pl.when(self.cross)
        def _():
            for c in ORDER:
                self.across(c).wait_send()


def inner_sum(copies, me, partial, total, work):
    first, first_in, second_in, third_in, fourth_in = work
    sibling = moved(me, core=1)
    core, x, y, z = me["core"], me["x"], me["hi"] * 2 + me["lo"], me["z"]
    copy = copies.start(partial.at[rows((1 - core) * 128, 128)], first_in, sibling)
    yield
    copy.wait_recv()
    first[...] = partial[rows(core * 128, 128), :] + first_in[...]
    sent = [
        copies.start(first.at[rows(((y + d) % 4) * 32, 32)], second_in.at[d - 1], moved(me, y=d)) for d in (1, 2, 3)
    ]
    yield
    for copy in sent:
        copy.wait_recv()
    mine = third_in.at[z]
    mine[...] = first[rows(y * 32, 32), :] + second_in[0] + second_in[1] + second_in[2]
    sent = [copies.start(mine, mine, moved(me, z=d)) for d in (1, 2, 3)]
    yield
    for copy in sent:
        copy.wait_recv()
    mine = fourth_in.at[x]
    mine[...] = third_in[0] + third_in[1] + third_in[2] + third_in[3]
    sent = [copies.start(mine, mine, moved(me, x=d)) for d in (1, 2, 3)]
    yield
    for copy in sent:
        copy.wait_recv()
    mine = total.at[rows(core * 128 + y * 32, 32)]
    mine[...] = fourth_in[0] + fourth_in[1] + fourth_in[2] + fourth_in[3]
    sent = [copies.start(mine, mine, moved(me, y=d)) for d in (1, 2, 3)]
    yield
    for copy in sent:
        copy.wait_recv()
    mine = total.at[rows(core * 128, 128)]
    copy = copies.start(mine, mine, sibling)
    yield
    copy.wait_recv()


def step_all(running):
    still = []
    for item in running:
        if next(item, "done") != "done":
            still.append(item)
    return still


def gather_kernel(
    halves_ref, rest_hbm, vec_hbm, tri_hbm, vec_high, vec_low, w_high, w_low, w_ref,
    vec_ref, rest_ref, tri_ref, av_col, av_row, vec_row, inner_ref, vec_middle,
    tiles, tile_high, tile_low, col_high, col_low, parts, rest_part, partial, row_sum, sibling_in, row_relay, col_relay,
    row_unit, col_unit, pair_in, swap_out, swap_in,
    first, first_in, second_in, third_in, fourth_in,
    load_sems, send_sems, recv_sems, vec_send_sems, vec_recv_sems,
):
    me = place()
    row, col, core = me["row"], me["col"], me["core"]
    x, lo, z, hi = me["x"], me["lo"], me["z"], me["hi"]
    sibling = moved(me, core=1)

    row_shift = (x - (x // 2 + 2 * core) + 4) % 4
    row_half = (lo + hi + x) % 2
    as_row = (((z + row_shift) % 4) * 2 + row_half, row + 8 * core)
    row_of = col % 8
    as_col = at(row_of // 2, row_of % 2, (x - row_of // 2 + z + 4) % 4, (lo + row_of + hi) % 2, col // 8)
    alone = jnp.logical_and(as_row[0] == row, as_row[1] == col)

    loads = [
        pltpu.make_async_copy(source, target, load_sems.at[i])
        for i, (source, target) in enumerate(
            ((vec_hbm, vec_ref), (halves_ref, tiles), (rest_hbm, rest_ref), (tri_hbm, tri_ref))
        )
    ]
    for load in loads:
        load.start()

    barrier = pltpu.get_barrier_semaphore()
    near = [moved(me, x=d) for d in (1, 2, 3)] + [moved(me, y=d) for d in (1, 2, 3)]
    near += [moved(me, z=d) for d in (1, 2, 3)] + [sibling]
    for device in near:
        pl.semaphore_signal(barrier, inc=1, device_id=device, device_id_type=MESH)

    @pl.when(jnp.logical_not(alone))
    def _():
        for device in (as_row, as_col):
            pl.semaphore_signal(barrier, inc=1, device_id=device, device_id_type=MESH)

    pl.semaphore_wait(barrier, len(near) + jnp.where(alone, 0, 2).astype(jnp.int32))

    copies = Copies(send_sems, recv_sems)
    z_ring = (z, row_shift, moved(me, z=1), moved(me, z=3))
    x_ring = (x, 0, moved(me, x=1), moved(me, x=3))
    spread = Spread(me, vec_ref, vec_row, vec_send_sems, vec_recv_sems)
    loads[0].wait()
    spread.begin()
    vec_high[0], vec_low[0] = split(vec_ref[...])
    loads[1].wait()

    def facts(position):
        block_row = row + 8 * position
        return block_row >= col, jnp.where(block_row == col, 0.5, 1.0).astype(jnp.float32)

    def upper(which):
        return vec_high[which, 0:HALF], vec_low[which, 0:HALF]

    def lower(which):
        return vec_high[which, HALF:TILE], vec_low[which, HALF:TILE]

    def whole(which):
        return vec_high[which], vec_low[which]

    def row_part(position):
        is_lower, weight = facts(position)
        tile_high[position], tile_low[position] = split(tiles[position])
        tile = tile_high.at[position], tile_low.at[position]

        @pl.when(is_lower)
        def _():
            parts[1 + position, 0:HALF] = product((tile[0][...], tile[1][...]), whole(0), NN) * weight
            parts[1 + position, HALF:TILE] = jnp.zeros((HALF, WIDTH), jnp.float32)

        @pl.when(jnp.logical_not(is_lower))
        def _():
            parts[1 + position] = product((tile[0][...], tile[1][...]), lower(0), TN)

    def col_part(position):
        is_lower, weight = facts(position)
        tile = tile_high.at[position], tile_low.at[position]

        @pl.when(is_lower)
        def _():
            parts[0] += product((tile[0][...], tile[1][...]), upper(1 + position), TN) * weight

        @pl.when(jnp.logical_not(is_lower))
        def _():
            parts[0, HALF:TILE] += product((tile[0][...], tile[1][...]), whole(1 + position), NN)

    row_partner = moved(me, y=2)
    col_partner = at(x, 1 - lo, z, hi, core)
    row_part(1 - core)
    pair = copies.start(parts.at[2 - core], sibling_in, sibling)
    spread.serve(0)
    row_part(core)
    spread.serve(1)
    spread.serve(2)
    rest_rows = rows(HALF + row * REST, REST)
    loads[2].wait()
    block = split(rest_ref[...])
    rest_part[...] = product(block, whole(0), NN) * 0.5
    parts[0] = product(block, (vec_high[0, rest_rows, :], vec_low[0, rest_rows, :]), TN) * 0.5
    spread.serve(3)
    spread.serve(4)
    pair.wait_recv()
    row_sum[...] = parts[1 + core] + sibling_in[...]
    spread.serve(5)
    row_scatter = ring_scatter(copies, row_sum, row_unit, row_relay, *z_ring, row_half, row_partner, pair_in.at[0])
    next(row_scatter)
    spread.serve(6)
    spread.serve(7)
    spread.end()
    vec_high[1], vec_low[1] = split(vec_row[0])
    col_part(0)
    vec_high[2], vec_low[2] = split(vec_row[1])
    col_part(1)
    col_high[...], col_low[...] = split(parts[0])
    parts[0, rest_rows, :] += rest_part[...]
    columns = ring_scatter(copies, parts.at[0], col_unit, col_relay, *x_ring, lo, col_partner, pair_in.at[1])
    next(columns)
    partial[...] = product(whole(0), (col_high[...], col_low[...]), TN)
    inner = inner_sum(
        copies, me, partial, inner_ref, (first, first_in, second_in, third_in, fourth_in)
    )
    next(inner)
    loads[3].wait()
    tri = split(tri_ref[...])
    next(row_scatter)
    next(inner)
    next(row_scatter)
    next(columns)
    next(row_scatter)
    next(columns)
    next(row_scatter)
    next(inner)
    next(columns)
    step_all([row_scatter])
    keep_row, keep_col = rows(row_half * PIECE, PIECE), rows(lo * PIECE, PIECE)
    swap_out[0] = product(split(row_unit[keep_row, :] + pair_in[0]), tri, NN)
    row_copy = copies.make(swap_out.at[0], swap_in.at[0], as_row)

    @pl.when(jnp.logical_not(alone))
    def _():
        row_copy.start()

    next(columns)
    next(inner)
    step_all([columns])
    swap_out[1] = product(split(col_unit[keep_col, :] + pair_in[1]), tri, NN)
    col_copy = copies.make(swap_out.at[1], swap_in.at[1], as_col)

    @pl.when(jnp.logical_not(alone))
    def _():
        col_copy.start()

    @pl.when(alone)
    def _():
        swap_in[...] = swap_out[...]

    next(inner)

    @pl.when(jnp.logical_not(alone))
    def _():
        row_copy.wait()

    av_col[rows(x * UNIT + lo * PIECE, PIECE), :] = swap_out[1] + swap_in[0]
    columns = ring_gather(copies, av_col, *x_ring, lo, col_partner)
    next(columns)
    next(inner)

    @pl.when(jnp.logical_not(alone))
    def _():
        col_copy.wait()

    av_row[core, rows(((z + row_shift) % 4) * UNIT + row_half * PIECE, PIECE), :] = swap_out[0] + swap_in[1]
    rows_in = ring_gather(copies, av_row.at[core], *z_ring, row_half, row_partner, sibling)
    next(rows_in)
    next(columns)
    step_all([inner])
    next(rows_in)
    next(columns)
    whole_inner = inner_ref[...] + inner_ref[...].T
    middle = split(product(split(product(tri, split(whole_inner), TN)), tri, NN) * 0.5)
    vec_middle[0] = product(whole(0), middle, NN)
    next(rows_in)
    next(columns)
    vec_middle[1] = product(whole(1), middle, NN)
    next(rows_in)
    next(columns)
    vec_middle[2] = product(whole(2), middle, NN)
    step_all([columns])
    w = av_col[...] - vec_middle[0]
    w_ref[...] = w
    w_high[0], w_low[0] = split(w)
    next(rows_in)
    step_all([rows_in])
    for position in range(2):
        w_high[1 + position], w_low[1 + position] = split(av_row[position] - vec_middle[1 + position])
    copies.finish()
    spread.finish()


def update_kernel(
    halves_ref, rest_ref, vec_high, vec_low, w_high, w_low, w_ref, out_ref, out_rest, out_w,
    tiles, rest, store_sems, side_sems,
):
    row, col = lax.axis_index("row"), lax.axis_index("col")
    count, _, size = tiles.shape
    each = TILE // size

    def place_of(ref, at_step):
        return ref.at[at_step // each, :, pl.ds(pl.multiple_of((at_step % each) * size, size), size)]

    def store(at_step):
        return pltpu.make_async_copy(tiles.at[at_step], place_of(out_ref, at_step), store_sems.at[at_step])

    w_copy = pltpu.make_async_copy(w_ref, out_w, side_sems.at[0])
    rest_in = pltpu.make_async_copy(rest_ref, rest, side_sems.at[1])
    rest_out = pltpu.make_async_copy(rest, out_rest, side_sems.at[2])
    rest_in.start()
    w_copy.start()
    rest_rows = rows(HALF + row * REST, REST)
    update = product(
        (vec_high[0, rest_rows, :], vec_low[0, rest_rows, :]), (w_high[0], w_low[0]), NT
    ) + product((w_high[0, rest_rows, :], w_low[0, rest_rows, :]), (vec_high[0], vec_low[0]), NT)
    rest_in.wait()
    rest[...] = rest[...] - update
    rest_out.start()

    def one(at_step, carry):
        position = at_step // each
        is_lower = row + 8 * position >= col
        high_rows = rows(jnp.where(is_lower, 0, HALF), HALF)
        low_rows = rows((at_step % each) * size, size)
        low_at = jnp.where(is_lower, 0, 1 + position)
        high_at = jnp.where(is_lower, 1 + position, 0)
        update = product(
            (vec_high[high_at, high_rows, :], vec_low[high_at, high_rows, :]),
            (w_high[low_at, low_rows, :], w_low[low_at, low_rows, :]),
            NT,
        ) + product(
            (w_high[high_at, high_rows, :], w_low[high_at, high_rows, :]),
            (vec_high[low_at, low_rows, :], vec_low[low_at, low_rows, :]),
            NT,
        )
        tiles[at_step] = place_of(halves_ref, at_step)[...] - update
        store(at_step).start()
        return carry

    lax.fori_loop(0, count, one, 0)
    for at_step in range(count):
        store(at_step).wait()
    w_copy.wait()
    rest_out.wait()


def shards(halves, diag_rest, panel_vectors, tri_factor):
    vmem = pl.BlockSpec(memory_space=pltpu.VMEM)
    outside = pl.BlockSpec(memory_space=pltpu.HBM)
    f32 = jnp.float32
    block = (TILE, WIDTH)

    def buffer(*shape):
        return pltpu.VMEM(shape, f32)

    held = pltpu.with_memory_space_constraint
    diag_rest, panel_vectors, tri_factor = (held(value, pltpu.HBM) for value in (diag_rest, panel_vectors, tri_factor))
    terms = jax.ShapeDtypeStruct((3,) + block, jnp.bfloat16)
    handed = pl.pallas_call(
        gather_kernel,
        out_shape=[terms, terms, terms, terms, jax.ShapeDtypeStruct(block, f32)],
        in_specs=[outside] * 4,
        out_specs=[vmem] * 5,
        scratch_shapes=[
            buffer(*block),
            buffer(REST, TILE),
            buffer(WIDTH, WIDTH),
            buffer(*block),
            buffer(2, *block),
            buffer(2, *block),
            buffer(WIDTH, WIDTH),
            buffer(3, *block),
            buffer(2, HALF, TILE),
            pltpu.VMEM((2, HALF, TILE), jnp.bfloat16),
            pltpu.VMEM((2, HALF, TILE), jnp.bfloat16),
            pltpu.VMEM(block, jnp.bfloat16),
            pltpu.VMEM(block, jnp.bfloat16),
            buffer(3, *block),
            buffer(REST, WIDTH),
            buffer(WIDTH, WIDTH),
            buffer(*block),
            buffer(*block),
            buffer(16, PIECE // 2, WIDTH),
            buffer(16, PIECE // 2, WIDTH),
            buffer(UNIT, WIDTH),
            buffer(UNIT, WIDTH),
            buffer(2, PIECE, WIDTH),
            buffer(2, PIECE, WIDTH),
            buffer(2, PIECE, WIDTH),
            buffer(128, WIDTH),
            buffer(128, WIDTH),
            buffer(3, 32, WIDTH),
            buffer(4, 32, WIDTH),
            buffer(4, 32, WIDTH),
            pltpu.SemaphoreType.DMA((4,)),
            pltpu.SemaphoreType.DMA((96,)),
            pltpu.SemaphoreType.DMA((96,)),
            pltpu.SemaphoreType.DMA((5 * CHUNKS,)),
            pltpu.SemaphoreType.DMA((5 * CHUNKS,)),
        ],
        compiler_params=pltpu.CompilerParams(
            collective_id=0, has_side_effects=True, vmem_limit_bytes=44 * 2**20
        ),
        name="gather",
    )(halves, diag_rest, panel_vectors, tri_factor)

    size = 256
    count = 2 * TILE // size
    return pl.pallas_call(
        update_kernel,
        out_shape=[
            jax.ShapeDtypeStruct(halves.shape, f32),
            jax.ShapeDtypeStruct(diag_rest.shape, f32),
            jax.ShapeDtypeStruct(panel_vectors.shape, f32),
        ],
        in_specs=[vmem, outside] + [vmem] * 5,
        out_specs=[outside] * 3,
        scratch_shapes=[
            buffer(count, HALF, size),
            buffer(REST, TILE),
            pltpu.SemaphoreType.DMA((count,)),
            pltpu.SemaphoreType.DMA((3,)),
        ],
        compiler_params=pltpu.CompilerParams(vmem_limit_bytes=24 * 2**20),
        name="update",
    )(halves, diag_rest, *handed)


def solution(mesh):
    return jax.shard_map(
        shards,
        mesh=mesh,
        in_specs=(P(None, "row", "col"), P(("col", "row"), None), P("col", None), P()),
        out_specs=(P(None, "row", "col"), P(("col", "row"), None), P("col", None)),
        check_vma=False,
    )
```

```python
import functools

import jax
import jax.numpy as jnp
from jax import lax
from jax.experimental import pallas as pl
from jax.experimental.pallas import tpu as pltpu
from jax.sharding import PartitionSpec as P

MESH = pl.DeviceIdType.MESH
NN = (((1,), (0,)), ((), ()))
TN = (((0,), (0,)), ((), ()))
NT = (((1,), (1,)), ((), ()))
TILE = 1024
HALF = 512
WIDTH = 256
UNIT = 256
PIECE = 128
REST = 64


def split(value):
    high = value.astype(jnp.bfloat16)
    low = (value - high.astype(jnp.float32)).astype(jnp.bfloat16)
    return high, low


def product(left, right, dims):
    def dot(a, b):
        return lax.dot_general(a, b, dims, preferred_element_type=jnp.float32)

    return dot(left[0], right[0]) + (dot(left[0], right[1]) + dot(left[1], right[0]))


def rows(start, size):
    return pl.ds(pl.multiple_of(start, 8), size)


def place():
    row, col = lax.axis_index("row"), lax.axis_index("col")
    return dict(row=row, col=col, x=row // 2, lo=row % 2, z=col // 4, hi=(col // 2) % 2, core=col % 2)


def at(x, lo, z, hi, core):
    return (x * 2 + lo, z * 4 + hi * 2 + core)


def moved(me, x=0, y=0, z=0, core=0):
    y_at = (me["hi"] * 2 + me["lo"] + y) % 4
    return at((me["x"] + x) % 4, y_at % 2, (me["z"] + z) % 4, y_at // 2, (me["core"] + core) % 2)


class Copies:
    def __init__(self, send_sems, recv_sems):
        self.send_sems, self.recv_sems, self.used, self.started = send_sems, recv_sems, 0, []

    def make(self, source, target, device):
        copy = pltpu.make_async_remote_copy(
            src_ref=source,
            dst_ref=target,
            send_sem=self.send_sems.at[self.used],
            recv_sem=self.recv_sems.at[self.used],
            device_id=device,
            device_id_type=MESH,
        )
        self.used += 1
        return copy

    def start(self, source, target, device):
        copy = self.make(source, target, device)
        copy.start()
        self.started.append(copy)
        return copy

    def finish(self):
        for copy in self.started:
            copy.wait_send()


def ring_scatter(copies, source, out, relay, index, shift, plus, minus, kept, partner, pair_in):
    size = PIECE // 2
    given = 1 - kept

    def part(step, which, at_half):
        return source.at[rows(((index + step + shift) % 4) * UNIT + which * PIECE + at_half * size, size)]

    def far(base, which):
        return (
            copies.start(part(2, which, 0), relay.at[base], plus),
            copies.start(part(2, which, 1), relay.at[base + 1], minus),
        )

    def near(base, which):
        return (
            copies.start(part(1, which, 1), relay.at[base + 2], plus),
            copies.start(part(3, which, 0), relay.at[base + 3], minus),
        )

    def passed(base, which, arriving):
        arriving[0].wait_recv()
        relay[base + 6] = relay[base] + part(1, which, 0)[...]
        to_plus = copies.start(relay.at[base + 6], relay.at[base + 4], plus)
        arriving[1].wait_recv()
        relay[base + 7] = relay[base + 1] + part(3, which, 1)[...]
        return to_plus, copies.start(relay.at[base + 7], relay.at[base + 5], minus)

    def total(base, which, arriving):
        for copy in arriving:
            copy.wait_recv()
        out[rows(which * PIECE, size), :] = part(0, which, 0)[...] + (relay[base + 4] + relay[base + 3])
        out[rows(which * PIECE + size, size), :] = part(0, which, 1)[...] + (relay[base + 2] + relay[base + 5])

    far_given = far(0, given)
    near_given = near(0, given)
    far_kept = far(8, kept)
    yield
    sum_given = passed(0, given, far_given)
    near_kept = near(8, kept)
    yield
    sum_kept = passed(8, kept, far_kept)
    yield
    total(0, given, near_given + sum_given)
    pair = copies.start(out.at[rows(given * PIECE, PIECE)], pair_in, partner)
    yield
    total(8, kept, near_kept + sum_kept)
    yield
    pair.wait_recv()


def ring_gather(copies, block, index, shift, plus, minus, kept, partner, sibling=None):
    def piece(step, which):
        return block.at[rows(((index + step + shift) % 4) * UNIT + which * PIECE, PIECE)]

    given = 1 - kept
    shared = []

    def part(step, which, at_half):
        start = ((index + step + shift) % 4) * UNIT + which * PIECE + at_half * (PIECE // 2)
        return block.at[rows(start, PIECE // 2)]

    def share(ref):
        if sibling is not None:
            shared.append(copies.start(ref, ref, sibling))

    def send(ref, device):
        return copies.start(ref, ref, device)

    own = piece(0, kept)
    pair = [send(part(0, kept, half), partner) for half in (0, 1)]
    own_plus, own_minus = send(own, plus), send(own, minus)
    share(own)
    yield
    other_plus, other_minus = [], []
    for half in (0, 1):
        pair[half].wait_recv()
        other_minus.append(send(part(0, given, half), minus))
        other_plus.append(send(part(0, given, half), plus))
    share(piece(0, given))
    yield
    own_plus.wait_recv()
    far_plus = send(piece(3, kept), plus)
    share(piece(3, kept))
    own_minus.wait_recv()
    share(piece(1, kept))
    yield
    far_minus = []
    for half in (0, 1):
        other_minus[half].wait_recv()
        far_minus.append(send(part(1, given, half), minus))
    share(piece(1, given))
    for copy in other_plus:
        copy.wait_recv()
    share(piece(3, given))
    yield
    far_plus.wait_recv()
    share(piece(2, kept))
    for half in (0, 1):
        far_minus[half].wait_recv()
        share(part(2, given, half))
    yield
    for copy in shared:
        copy.wait_recv()


CHUNKS = 16
CHUNK = TILE // CHUNKS
ORDER = [half + c for c in range(CHUNKS // 2) for half in (0, CHUNKS // 2)]


class Spread:
    def __init__(self, me, vec_ref, vec_row, send_sems, recv_sems):
        x, lo, z, hi, core = me["x"], me["lo"], me["z"], me["hi"], me["core"]
        self.vec_ref, self.vec_row, self.send_sems, self.recv_sems = vec_ref, vec_row, send_sems, recv_sems
        self.lead = core == lo
        line = hi == x % 2
        end = z % 2 == x // 2
        self.source = jnp.logical_and(jnp.logical_and(self.lead, line), end)
        self.cross = jnp.logical_and(jnp.logical_and(jnp.logical_not(self.lead), line), end)
        self.target = jnp.logical_and(jnp.logical_and(self.lead, jnp.logical_not(line)), end)
        self.ends = jnp.logical_and(self.lead, end)
        self.middle = jnp.logical_and(self.lead, jnp.logical_not(end))
        self.follow = jnp.logical_not(self.lead)
        self.plus, self.minus, self.sibling = moved(me, z=1), moved(me, z=3), moved(me, core=1)
        self.over = at(x, core, z, 1 - hi, core)
        self.own = z // 2
        self.from_minus = ((z + 3) % 4) // 2

    def chunk(self, block, c):
        return self.vec_row.at[block, pl.ds(c * CHUNK, CHUNK)]

    def copy(self, slot, source, target, device):
        return pltpu.make_async_remote_copy(
            src_ref=source,
            dst_ref=target,
            send_sem=self.send_sems.at[slot],
            recv_sem=self.recv_sems.at[slot],
            device_id=device,
            device_id_type=MESH,
        )

    def mine(self, c):
        return self.vec_ref.at[pl.ds(c * CHUNK, CHUNK)]

    def along(self, c, block, source=None):
        here = self.chunk(block, c)
        return self.copy(c, here if source is None else source, here, self.plus)

    def back(self, c, block, source=None):
        here = self.chunk(block, c)
        return self.copy(CHUNKS + c, here if source is None else source, here, self.minus)

    def across(self, c):
        return self.copy(2 * CHUNKS + c, self.mine(c), self.chunk(self.own, c), self.over)

    def share(self, c, block, which, source=None):
        here = self.chunk(block, c)
        return self.copy((3 + which) * CHUNKS + c, here if source is None else source, here, self.sibling)

    def begin(self):
        @pl.when(self.source)
        def _():
            for c in ORDER:
                self.along(c, self.own, self.mine(c)).start()
                self.back(c, self.own, self.mine(c)).start()
                self.share(c, self.own, 0, self.mine(c)).start()
            self.vec_row[self.own] = self.vec_ref[...]

        @pl.when(self.cross)
        def _():
            for c in ORDER:
                self.across(c).start()

    def serve(self, *steps):
        for step in steps:
            self.pass_on(ORDER[2 * step])
            self.pass_on(ORDER[2 * step + 1])

    def pass_on(self, c):
        @pl.when(self.target)
        def _():
            self.across(c).wait_recv()
            self.along(c, self.own).start()
            self.back(c, self.own).start()
            self.share(c, self.own, 0).start()

        @pl.when(self.middle)
        def _():
            block = self.from_minus
            self.along(c, block).wait_recv()
            if c < CHUNKS // 2:
                self.along(c, block).start()
            self.share(c, block, 0).start()
            self.back(c, 1 - block).wait_recv()
            if c >= CHUNKS // 2:
                self.back(c, 1 - block).start()
            self.share(c, 1 - block, 1).start()

    def end(self):
        @pl.when(self.ends)
        def _():
            for c in ORDER:
                copy = self.along(c, 1 - self.own) if c < CHUNKS // 2 else self.back(c, 1 - self.own)
                copy.wait_recv()
                self.share(c, 1 - self.own, 1).start()

        @pl.when(self.follow)
        def _():
            for c in ORDER:
                for which in range(2):
                    self.share(c, which, which).wait_recv()

    def finish(self):
        @pl.when(self.ends)
        def _():
            for c in ORDER:
                self.along(c, self.own).wait_send()
                self.back(c, self.own).wait_send()

        @pl.when(self.middle)
        def _():
            for c in ORDER:
                if c < CHUNKS // 2:
                    self.along(c, 0).wait_send()
                else:
                    self.back(c, 0).wait_send()

        @pl.when(self.lead)
        def _():
            for c in ORDER:
                for which in range(2):
                    self.share(c, which, which).wait_send()

        @pl.when(self.cross)
        def _():
            for c in ORDER:
                self.across(c).wait_send()


def inner_sum(copies, me, partial, total, work):
    first, first_in, second_in, third_in, fourth_in = work
    sibling = moved(me, core=1)
    core, x, y, z = me["core"], me["x"], me["hi"] * 2 + me["lo"], me["z"]
    copy = copies.start(partial.at[rows((1 - core) * 128, 128)], first_in, sibling)
    yield
    copy.wait_recv()
    first[...] = partial[rows(core * 128, 128), :] + first_in[...]
    sent = [
        copies.start(first.at[rows(((y + d) % 4) * 32, 32)], second_in.at[d - 1], moved(me, y=d)) for d in (1, 2, 3)
    ]
    yield
    for copy in sent:
        copy.wait_recv()
    mine = third_in.at[z]
    mine[...] = first[rows(y * 32, 32), :] + second_in[0] + second_in[1] + second_in[2]
    sent = [copies.start(mine, mine, moved(me, z=d)) for d in (1, 2, 3)]
    yield
    for copy in sent:
        copy.wait_recv()
    mine = fourth_in.at[x]
    mine[...] = third_in[0] + third_in[1] + third_in[2] + third_in[3]
    sent = [copies.start(mine, mine, moved(me, x=d)) for d in (1, 2, 3)]
    yield
    for copy in sent:
        copy.wait_recv()
    mine = total.at[rows(core * 128 + y * 32, 32)]
    mine[...] = fourth_in[0] + fourth_in[1] + fourth_in[2] + fourth_in[3]
    sent = [copies.start(mine, mine, moved(me, y=d)) for d in (1, 2, 3)]
    yield
    for copy in sent:
        copy.wait_recv()
    mine = total.at[rows(core * 128, 128)]
    copy = copies.start(mine, mine, sibling)
    yield
    copy.wait_recv()


def step_all(running):
    still = []
    for item in running:
        if next(item, "done") != "done":
            still.append(item)
    return still


def gather_kernel(
    halves_ref, rest_hbm, vec_hbm, tri_hbm, vec_high, vec_low, w_high, w_low, w_ref,
    vec_ref, rest_ref, tri_ref, av_col, av_row, vec_row, inner_ref, vec_middle,
    tiles, tile_high, tile_low, col_high, col_low, parts, rest_part, partial, row_sum, sibling_in, row_relay, col_relay,
    row_unit, col_unit, pair_in, swap_out, swap_in,
    first, first_in, second_in, third_in, fourth_in,
    load_sems, send_sems, recv_sems, vec_send_sems, vec_recv_sems,
):
    me = place()
    row, col, core = me["row"], me["col"], me["core"]
    x, lo, z, hi = me["x"], me["lo"], me["z"], me["hi"]
    sibling = moved(me, core=1)

    row_shift = (x - (x // 2 + 2 * core) + 4) % 4
    row_half = (lo + hi + x) % 2
    as_row = (((z + row_shift) % 4) * 2 + row_half, row + 8 * core)
    row_of = col % 8
    as_col = at(row_of // 2, row_of % 2, (x - row_of // 2 + z + 4) % 4, (lo + row_of + hi) % 2, col // 8)
    alone = jnp.logical_and(as_row[0] == row, as_row[1] == col)

    loads = [
        pltpu.make_async_copy(source, target, load_sems.at[i])
        for i, (source, target) in enumerate(
            ((vec_hbm, vec_ref), (halves_ref, tiles), (rest_hbm, rest_ref), (tri_hbm, tri_ref))
        )
    ]
    for load in loads:
        load.start()

    barrier = pltpu.get_barrier_semaphore()
    near = [moved(me, x=d) for d in (1, 2, 3)] + [moved(me, y=d) for d in (1, 2, 3)]
    near += [moved(me, z=d) for d in (1, 2, 3)] + [sibling]
    for device in near:
        pl.semaphore_signal(barrier, inc=1, device_id=device, device_id_type=MESH)

    @pl.when(jnp.logical_not(alone))
    def _():
        for device in (as_row, as_col):
            pl.semaphore_signal(barrier, inc=1, device_id=device, device_id_type=MESH)

    pl.semaphore_wait(barrier, len(near) + jnp.where(alone, 0, 2).astype(jnp.int32))

    copies = Copies(send_sems, recv_sems)
    z_ring = (z, row_shift, moved(me, z=1), moved(me, z=3))
    x_ring = (x, 0, moved(me, x=1), moved(me, x=3))
    spread = Spread(me, vec_ref, vec_row, vec_send_sems, vec_recv_sems)
    loads[0].wait()
    spread.begin()
    vec_high[0], vec_low[0] = split(vec_ref[...])
    loads[1].wait()

    def facts(position):
        block_row = row + 8 * position
        return block_row >= col, jnp.where(block_row == col, 0.5, 1.0).astype(jnp.float32)

    def upper(which):
        return vec_high[which, 0:HALF], vec_low[which, 0:HALF]

    def lower(which):
        return vec_high[which, HALF:TILE], vec_low[which, HALF:TILE]

    def whole(which):
        return vec_high[which], vec_low[which]

    def row_part(position):
        is_lower, weight = facts(position)
        tile_high[position], tile_low[position] = split(tiles[position])
        tile = tile_high.at[position], tile_low.at[position]

        @pl.when(is_lower)
        def _():
            parts[1 + position, 0:HALF] = product((tile[0][...], tile[1][...]), whole(0), NN) * weight
            parts[1 + position, HALF:TILE] = jnp.zeros((HALF, WIDTH), jnp.float32)

        @pl.when(jnp.logical_not(is_lower))
        def _():
            parts[1 + position] = product((tile[0][...], tile[1][...]), lower(0), TN)

    def col_part(position):
        is_lower, weight = facts(position)
        tile = tile_high.at[position], tile_low.at[position]

        @pl.when(is_lower)
        def _():
            parts[0] += product((tile[0][...], tile[1][...]), upper(1 + position), TN) * weight

        @pl.when(jnp.logical_not(is_lower))
        def _():
            parts[0, HALF:TILE] += product((tile[0][...], tile[1][...]), whole(1 + position), NN)

    row_partner = moved(me, y=2)
    col_partner = at(x, 1 - lo, z, hi, core)
    row_part(1 - core)
    pair = copies.start(parts.at[2 - core], sibling_in, sibling)
    spread.serve(0)
    row_part(core)
    spread.serve(1)
    spread.serve(2)
    rest_rows = rows(HALF + row * REST, REST)
    loads[2].wait()
    block = split(rest_ref[...])
    rest_part[...] = product(block, whole(0), NN) * 0.5
    parts[0] = product(block, (vec_high[0, rest_rows, :], vec_low[0, rest_rows, :]), TN) * 0.5
    spread.serve(3)
    spread.serve(4)
    pair.wait_recv()
    row_sum[...] = parts[1 + core] + sibling_in[...]
    spread.serve(5)
    spread.serve(6)
    spread.serve(7)
    spread.end()
    row_scatter = ring_scatter(copies, row_sum, row_unit, row_relay, *z_ring, row_half, row_partner, pair_in.at[0])
    next(row_scatter)
    vec_high[1], vec_low[1] = split(vec_row[0])
    col_part(0)
    vec_high[2], vec_low[2] = split(vec_row[1])
    col_part(1)
    col_high[...], col_low[...] = split(parts[0])
    parts[0, rest_rows, :] += rest_part[...]
    columns = ring_scatter(copies, parts.at[0], col_unit, col_relay, *x_ring, lo, col_partner, pair_in.at[1])
    next(columns)
    partial[...] = product(whole(0), (col_high[...], col_low[...]), TN)
    inner = inner_sum(
        copies, me, partial, inner_ref, (first, first_in, second_in, third_in, fourth_in)
    )
    next(inner)
    loads[3].wait()
    tri = split(tri_ref[...])
    next(row_scatter)
    next(inner)
    next(row_scatter)
    next(columns)
    next(row_scatter)
    next(columns)
    next(row_scatter)
    next(inner)
    next(columns)
    step_all([row_scatter])
    keep_row, keep_col = rows(row_half * PIECE, PIECE), rows(lo * PIECE, PIECE)
    swap_out[0] = product(split(row_unit[keep_row, :] + pair_in[0]), tri, NN)
    row_copy = copies.make(swap_out.at[0], swap_in.at[0], as_row)

    @pl.when(jnp.logical_not(alone))
    def _():
        row_copy.start()

    next(columns)
    next(inner)
    step_all([columns])
    swap_out[1] = product(split(col_unit[keep_col, :] + pair_in[1]), tri, NN)
    col_copy = copies.make(swap_out.at[1], swap_in.at[1], as_col)

    @pl.when(jnp.logical_not(alone))
    def _():
        col_copy.start()

    @pl.when(alone)
    def _():
        swap_in[...] = swap_out[...]

    next(inner)

    @pl.when(jnp.logical_not(alone))
    def _():
        row_copy.wait()

    av_col[rows(x * UNIT + lo * PIECE, PIECE), :] = swap_out[1] + swap_in[0]
    columns = ring_gather(copies, av_col, *x_ring, lo, col_partner)
    next(columns)
    next(inner)

    @pl.when(jnp.logical_not(alone))
    def _():
        col_copy.wait()

    av_row[core, rows(((z + row_shift) % 4) * UNIT + row_half * PIECE, PIECE), :] = swap_out[0] + swap_in[1]
    rows_in = ring_gather(copies, av_row.at[core], *z_ring, row_half, row_partner, sibling)
    next(rows_in)
    next(columns)
    step_all([inner])
    next(rows_in)
    next(columns)
    whole_inner = inner_ref[...] + inner_ref[...].T
    middle = split(product(split(product(tri, split(whole_inner), TN)), tri, NN) * 0.5)
    vec_middle[0] = product(whole(0), middle, NN)
    next(rows_in)
    next(columns)
    vec_middle[1] = product(whole(1), middle, NN)
    next(rows_in)
    next(columns)
    vec_middle[2] = product(whole(2), middle, NN)
    step_all([columns])
    w = av_col[...] - vec_middle[0]
    w_ref[...] = w
    w_high[0], w_low[0] = split(w)
    next(rows_in)
    step_all([rows_in])
    for position in range(2):
        w_high[1 + position], w_low[1 + position] = split(av_row[position] - vec_middle[1 + position])
    copies.finish()
    spread.finish()


def update_kernel(
    halves_ref, rest_ref, vec_high, vec_low, w_high, w_low, w_ref, out_ref, out_rest, out_w,
    tiles, rest, store_sems, side_sems,
):
    row, col = lax.axis_index("row"), lax.axis_index("col")
    count, _, size = tiles.shape
    each = TILE // size

    def place_of(ref, at_step):
        return ref.at[at_step // each, :, pl.ds(pl.multiple_of((at_step % each) * size, size), size)]

    def store(at_step):
        return pltpu.make_async_copy(tiles.at[at_step], place_of(out_ref, at_step), store_sems.at[at_step])

    w_copy = pltpu.make_async_copy(w_ref, out_w, side_sems.at[0])
    rest_in = pltpu.make_async_copy(rest_ref, rest, side_sems.at[1])
    rest_out = pltpu.make_async_copy(rest, out_rest, side_sems.at[2])
    rest_in.start()
    w_copy.start()
    rest_rows = rows(HALF + row * REST, REST)
    update = product(
        (vec_high[0, rest_rows, :], vec_low[0, rest_rows, :]), (w_high[0], w_low[0]), NT
    ) + product((w_high[0, rest_rows, :], w_low[0, rest_rows, :]), (vec_high[0], vec_low[0]), NT)
    rest_in.wait()
    rest[...] = rest[...] - update
    rest_out.start()

    def one(at_step, carry):
        position = at_step // each
        is_lower = row + 8 * position >= col
        high_rows = rows(jnp.where(is_lower, 0, HALF), HALF)
        low_rows = rows((at_step % each) * size, size)
        low_at = jnp.where(is_lower, 0, 1 + position)
        high_at = jnp.where(is_lower, 1 + position, 0)
        update = product(
            (vec_high[high_at, high_rows, :], vec_low[high_at, high_rows, :]),
            (w_high[low_at, low_rows, :], w_low[low_at, low_rows, :]),
            NT,
        ) + product(
            (w_high[high_at, high_rows, :], w_low[high_at, high_rows, :]),
            (vec_high[low_at, low_rows, :], vec_low[low_at, low_rows, :]),
            NT,
        )
        tiles[at_step] = place_of(halves_ref, at_step)[...] - update
        store(at_step).start()
        return carry

    lax.fori_loop(0, count, one, 0)
    for at_step in range(count):
        store(at_step).wait()
    w_copy.wait()
    rest_out.wait()


def shards(halves, diag_rest, panel_vectors, tri_factor):
    vmem = pl.BlockSpec(memory_space=pltpu.VMEM)
    outside = pl.BlockSpec(memory_space=pltpu.HBM)
    f32 = jnp.float32
    block = (TILE, WIDTH)

    def buffer(*shape):
        return pltpu.VMEM(shape, f32)

    held = pltpu.with_memory_space_constraint
    diag_rest, panel_vectors, tri_factor = (held(value, pltpu.HBM) for value in (diag_rest, panel_vectors, tri_factor))
    terms = jax.ShapeDtypeStruct((3,) + block, jnp.bfloat16)
    handed = pl.pallas_call(
        gather_kernel,
        out_shape=[terms, terms, terms, terms, jax.ShapeDtypeStruct(block, f32)],
        in_specs=[outside] * 4,
        out_specs=[vmem] * 5,
        scratch_shapes=[
            buffer(*block),
            buffer(REST, TILE),
            buffer(WIDTH, WIDTH),
            buffer(*block),
            buffer(2, *block),
            buffer(2, *block),
            buffer(WIDTH, WIDTH),
            buffer(3, *block),
            buffer(2, HALF, TILE),
            pltpu.VMEM((2, HALF, TILE), jnp.bfloat16),
            pltpu.VMEM((2, HALF, TILE), jnp.bfloat16),
            pltpu.VMEM(block, jnp.bfloat16),
            pltpu.VMEM(block, jnp.bfloat16),
            buffer(3, *block),
            buffer(REST, WIDTH),
            buffer(WIDTH, WIDTH),
            buffer(*block),
            buffer(*block),
            buffer(16, PIECE // 2, WIDTH),
            buffer(16, PIECE // 2, WIDTH),
            buffer(UNIT, WIDTH),
            buffer(UNIT, WIDTH),
            buffer(2, PIECE, WIDTH),
            buffer(2, PIECE, WIDTH),
            buffer(2, PIECE, WIDTH),
            buffer(128, WIDTH),
            buffer(128, WIDTH),
            buffer(3, 32, WIDTH),
            buffer(4, 32, WIDTH),
            buffer(4, 32, WIDTH),
            pltpu.SemaphoreType.DMA((4,)),
            pltpu.SemaphoreType.DMA((96,)),
            pltpu.SemaphoreType.DMA((96,)),
            pltpu.SemaphoreType.DMA((5 * CHUNKS,)),
            pltpu.SemaphoreType.DMA((5 * CHUNKS,)),
        ],
        compiler_params=pltpu.CompilerParams(
            collective_id=0, has_side_effects=True, vmem_limit_bytes=44 * 2**20
        ),
        name="gather",
    )(halves, diag_rest, panel_vectors, tri_factor)

    size = 256
    count = 2 * TILE // size
    return pl.pallas_call(
        update_kernel,
        out_shape=[
            jax.ShapeDtypeStruct(halves.shape, f32),
            jax.ShapeDtypeStruct(diag_rest.shape, f32),
            jax.ShapeDtypeStruct(panel_vectors.shape, f32),
        ],
        in_specs=[vmem, outside] + [vmem] * 5,
        out_specs=[outside] * 3,
        scratch_shapes=[
            buffer(count, HALF, size),
            buffer(REST, TILE),
            pltpu.SemaphoreType.DMA((count,)),
            pltpu.SemaphoreType.DMA((3,)),
        ],
        compiler_params=pltpu.CompilerParams(vmem_limit_bytes=24 * 2**20),
        name="update",
    )(halves, diag_rest, *handed)


def solution(mesh):
    return jax.shard_map(
        shards,
        mesh=mesh,
        in_specs=(P(None, "row", "col"), P(("col", "row"), None), P("col", None), P()),
        out_specs=(P(None, "row", "col"), P(("col", "row"), None), P("col", None)),
        check_vma=False,
    )
```

```python
import functools

import jax
import jax.numpy as jnp
from jax import lax
from jax.experimental import pallas as pl
from jax.experimental.pallas import tpu as pltpu
from jax.sharding import PartitionSpec as P

MESH = pl.DeviceIdType.MESH
NN = (((1,), (0,)), ((), ()))
TN = (((0,), (0,)), ((), ()))
NT = (((1,), (1,)), ((), ()))
TILE = 1024
HALF = 512
WIDTH = 256
UNIT = 256
PIECE = 128
REST = 64


def split(value):
    high = value.astype(jnp.bfloat16)
    low = (value - high.astype(jnp.float32)).astype(jnp.bfloat16)
    return high, low


def product(left, right, dims):
    def dot(a, b):
        return lax.dot_general(a, b, dims, preferred_element_type=jnp.float32)

    return dot(left[0], right[0]) + (dot(left[0], right[1]) + dot(left[1], right[0]))


def rows(start, size):
    return pl.ds(pl.multiple_of(start, 8), size)


def place():
    row, col = lax.axis_index("row"), lax.axis_index("col")
    return dict(row=row, col=col, x=row // 2, lo=row % 2, z=col // 4, hi=(col // 2) % 2, core=col % 2)


def at(x, lo, z, hi, core):
    return (x * 2 + lo, z * 4 + hi * 2 + core)


def moved(me, x=0, y=0, z=0, core=0):
    y_at = (me["hi"] * 2 + me["lo"] + y) % 4
    return at((me["x"] + x) % 4, y_at % 2, (me["z"] + z) % 4, y_at // 2, (me["core"] + core) % 2)


class Copies:
    def __init__(self, send_sems, recv_sems):
        self.send_sems, self.recv_sems, self.used, self.started = send_sems, recv_sems, 0, []

    def make(self, source, target, device):
        copy = pltpu.make_async_remote_copy(
            src_ref=source,
            dst_ref=target,
            send_sem=self.send_sems.at[self.used],
            recv_sem=self.recv_sems.at[self.used],
            device_id=device,
            device_id_type=MESH,
        )
        self.used += 1
        return copy

    def start(self, source, target, device):
        copy = self.make(source, target, device)
        copy.start()
        self.started.append(copy)
        return copy

    def finish(self):
        for copy in self.started:
            copy.wait_send()


def ring_scatter(copies, source, out, relay, index, shift, plus, minus, kept, partner, pair_in):
    size = PIECE // 2
    given = 1 - kept

    def part(step, which, at_half):
        return source.at[rows(((index + step + shift) % 4) * UNIT + which * PIECE + at_half * size, size)]

    def far(base, which):
        return (
            copies.start(part(2, which, 0), relay.at[base], plus),
            copies.start(part(2, which, 1), relay.at[base + 1], minus),
        )

    def near(base, which):
        return (
            copies.start(part(1, which, 1), relay.at[base + 2], plus),
            copies.start(part(3, which, 0), relay.at[base + 3], minus),
        )

    def passed(base, which, arriving):
        arriving[0].wait_recv()
        relay[base + 6] = relay[base] + part(1, which, 0)[...]
        to_plus = copies.start(relay.at[base + 6], relay.at[base + 4], plus)
        arriving[1].wait_recv()
        relay[base + 7] = relay[base + 1] + part(3, which, 1)[...]
        return to_plus, copies.start(relay.at[base + 7], relay.at[base + 5], minus)

    def total(base, which, arriving):
        for copy in arriving:
            copy.wait_recv()
        out[rows(which * PIECE, size), :] = part(0, which, 0)[...] + (relay[base + 4] + relay[base + 3])
        out[rows(which * PIECE + size, size), :] = part(0, which, 1)[...] + (relay[base + 2] + relay[base + 5])

    far_given = far(0, given)
    near_given = near(0, given)
    far_kept = far(8, kept)
    yield
    sum_given = passed(0, given, far_given)
    near_kept = near(8, kept)
    yield
    sum_kept = passed(8, kept, far_kept)
    yield
    total(0, given, near_given + sum_given)
    pair = copies.start(out.at[rows(given * PIECE, PIECE)], pair_in, partner)
    yield
    total(8, kept, near_kept + sum_kept)
    yield
    pair.wait_recv()


def ring_gather(copies, block, index, shift, plus, minus, kept, partner, sibling=None):
    def piece(step, which):
        return block.at[rows(((index + step + shift) % 4) * UNIT + which * PIECE, PIECE)]

    given = 1 - kept
    shared = []

    def part(step, which, at_half):
        start = ((index + step + shift) % 4) * UNIT + which * PIECE + at_half * (PIECE // 2)
        return block.at[rows(start, PIECE // 2)]

    def share(ref):
        if sibling is not None:
            shared.append(copies.start(ref, ref, sibling))

    def send(ref, device):
        return copies.start(ref, ref, device)

    own = piece(0, kept)
    pair = [send(part(0, kept, half), partner) for half in (0, 1)]
    own_plus, own_minus = send(own, plus), send(own, minus)
    share(own)
    yield
    other_plus, other_minus = [], []
    for half in (0, 1):
        pair[half].wait_recv()
        other_minus.append(send(part(0, given, half), minus))
        other_plus.append(send(part(0, given, half), plus))
    share(piece(0, given))
    yield
    own_plus.wait_recv()
    far_plus = send(piece(3, kept), plus)
    share(piece(3, kept))
    own_minus.wait_recv()
    share(piece(1, kept))
    yield
    far_minus = []
    for half in (0, 1):
        other_minus[half].wait_recv()
        far_minus.append(send(part(1, given, half), minus))
    share(piece(1, given))
    for copy in other_plus:
        copy.wait_recv()
    share(piece(3, given))
    yield
    far_plus.wait_recv()
    share(piece(2, kept))
    for half in (0, 1):
        far_minus[half].wait_recv()
        share(part(2, given, half))
    yield
    for copy in shared:
        copy.wait_recv()


CHUNKS = 16
CHUNK = TILE // CHUNKS
ORDER = [half + c for c in range(CHUNKS // 2) for half in (0, CHUNKS // 2)]


class Spread:
    def __init__(self, me, vec_ref, vec_row, send_sems, recv_sems):
        x, lo, z, hi, core = me["x"], me["lo"], me["z"], me["hi"], me["core"]
        self.vec_ref, self.vec_row, self.send_sems, self.recv_sems = vec_ref, vec_row, send_sems, recv_sems
        self.lead = core == lo
        line = hi == x % 2
        end = z % 2 == x // 2
        self.source = jnp.logical_and(jnp.logical_and(self.lead, line), end)
        self.cross = jnp.logical_and(jnp.logical_and(jnp.logical_not(self.lead), line), end)
        self.target = jnp.logical_and(jnp.logical_and(self.lead, jnp.logical_not(line)), end)
        self.ends = jnp.logical_and(self.lead, end)
        self.middle = jnp.logical_and(self.lead, jnp.logical_not(end))
        self.follow = jnp.logical_not(self.lead)
        self.plus, self.minus, self.sibling = moved(me, z=1), moved(me, z=3), moved(me, core=1)
        self.over = at(x, core, z, 1 - hi, core)
        self.own = z // 2
        self.from_minus = ((z + 3) % 4) // 2
        self.early = jnp.where(end, self.own, self.from_minus)

    def chunk(self, block, c):
        return self.vec_row.at[block, pl.ds(c * CHUNK, CHUNK)]

    def copy(self, slot, source, target, device):
        return pltpu.make_async_remote_copy(
            src_ref=source,
            dst_ref=target,
            send_sem=self.send_sems.at[slot],
            recv_sem=self.recv_sems.at[slot],
            device_id=device,
            device_id_type=MESH,
        )

    def mine(self, c):
        return self.vec_ref.at[pl.ds(c * CHUNK, CHUNK)]

    def along(self, c, block, source=None):
        here = self.chunk(block, c)
        return self.copy(c, here if source is None else source, here, self.plus)

    def back(self, c, block, source=None):
        here = self.chunk(block, c)
        return self.copy(CHUNKS + c, here if source is None else source, here, self.minus)

    def across(self, c):
        return self.copy(2 * CHUNKS + c, self.mine(c), self.chunk(self.own, c), self.over)

    def share(self, c, block, which, source=None):
        here = self.chunk(block, c)
        return self.copy((3 + which) * CHUNKS + c, here if source is None else source, here, self.sibling)

    def begin(self):
        @pl.when(self.source)
        def _():
            for c in ORDER:
                self.along(c, self.own, self.mine(c)).start()
                self.back(c, self.own, self.mine(c)).start()
                self.share(c, self.own, 0, self.mine(c)).start()
            self.vec_row[self.own] = self.vec_ref[...]

        @pl.when(self.cross)
        def _():
            for c in ORDER:
                self.across(c).start()

    def serve(self, *steps):
        for step in steps:
            self.pass_on(ORDER[2 * step])
            self.pass_on(ORDER[2 * step + 1])

    def pass_on(self, c):
        @pl.when(self.target)
        def _():
            self.across(c).wait_recv()
            self.along(c, self.own).start()
            self.back(c, self.own).start()
            self.share(c, self.own, 0).start()

        @pl.when(self.middle)
        def _():
            block = self.from_minus
            self.along(c, block).wait_recv()
            if c < CHUNKS // 2:
                self.along(c, block).start()
            self.share(c, block, 0).start()
            self.back(c, 1 - block).wait_recv()
            if c >= CHUNKS // 2:
                self.back(c, 1 - block).start()
            self.share(c, 1 - block, 1).start()

    def half_end(self):
        @pl.when(self.follow)
        def _():
            for c in ORDER:
                self.share(c, 0, 0).wait_recv()

    def end(self):
        @pl.when(self.ends)
        def _():
            for c in ORDER:
                copy = self.along(c, 1 - self.own) if c < CHUNKS // 2 else self.back(c, 1 - self.own)
                copy.wait_recv()
                self.share(c, 1 - self.own, 1).start()

        @pl.when(self.follow)
        def _():
            for c in ORDER:
                self.share(c, 1, 1).wait_recv()

    def finish(self):
        @pl.when(self.ends)
        def _():
            for c in ORDER:
                self.along(c, self.own).wait_send()
                self.back(c, self.own).wait_send()

        @pl.when(self.middle)
        def _():
            for c in ORDER:
                if c < CHUNKS // 2:
                    self.along(c, 0).wait_send()
                else:
                    self.back(c, 0).wait_send()

        @pl.when(self.lead)
        def _():
            for c in ORDER:
                for which in range(2):
                    self.share(c, which, which).wait_send()

        @pl.when(self.cross)
        def _():
            for c in ORDER:
                self.across(c).wait_send()


def inner_sum(copies, me, partial, total, work):
    first, first_in, second_in, third_in, fourth_in = work
    sibling = moved(me, core=1)
    core, x, y, z = me["core"], me["x"], me["hi"] * 2 + me["lo"], me["z"]
    copy = copies.start(partial.at[rows((1 - core) * 128, 128)], first_in, sibling)
    yield
    copy.wait_recv()
    first[...] = partial[rows(core * 128, 128), :] + first_in[...]
    sent = [
        copies.start(first.at[rows(((y + d) % 4) * 32, 32)], second_in.at[d - 1], moved(me, y=d)) for d in (1, 2, 3)
    ]
    yield
    for copy in sent:
        copy.wait_recv()
    mine = third_in.at[z]
    mine[...] = first[rows(y * 32, 32), :] + second_in[0] + second_in[1] + second_in[2]
    sent = [copies.start(mine, mine, moved(me, z=d)) for d in (1, 2, 3)]
    yield
    for copy in sent:
        copy.wait_recv()
    mine = fourth_in.at[x]
    mine[...] = third_in[0] + third_in[1] + third_in[2] + third_in[3]
    sent = [copies.start(mine, mine, moved(me, x=d)) for d in (1, 2, 3)]
    yield
    for copy in sent:
        copy.wait_recv()
    mine = total.at[rows(core * 128 + y * 32, 32)]
    mine[...] = fourth_in[0] + fourth_in[1] + fourth_in[2] + fourth_in[3]
    sent = [copies.start(mine, mine, moved(me, y=d)) for d in (1, 2, 3)]
    yield
    for copy in sent:
        copy.wait_recv()
    mine = total.at[rows(core * 128, 128)]
    copy = copies.start(mine, mine, sibling)
    yield
    copy.wait_recv()


def step_all(running):
    still = []
    for item in running:
        if next(item, "done") != "done":
            still.append(item)
    return still


def gather_kernel(
    halves_ref, rest_hbm, vec_hbm, tri_hbm, vec_high, vec_low, w_high, w_low, w_ref,
    vec_ref, rest_ref, tri_ref, av_col, av_row, vec_row, inner_ref, vec_middle,
    tiles, tile_high, tile_low, col_high, col_low, parts, rest_part, partial, row_sum, sibling_in, row_relay, col_relay,
    row_unit, col_unit, pair_in, swap_out, swap_in,
    first, first_in, second_in, third_in, fourth_in,
    load_sems, send_sems, recv_sems, vec_send_sems, vec_recv_sems,
):
    me = place()
    row, col, core = me["row"], me["col"], me["core"]
    x, lo, z, hi = me["x"], me["lo"], me["z"], me["hi"]
    sibling = moved(me, core=1)

    row_shift = (x - (x // 2 + 2 * core) + 4) % 4
    row_half = (lo + hi + x) % 2
    as_row = (((z + row_shift) % 4) * 2 + row_half, row + 8 * core)
    row_of = col % 8
    as_col = at(row_of // 2, row_of % 2, (x - row_of // 2 + z + 4) % 4, (lo + row_of + hi) % 2, col // 8)
    alone = jnp.logical_and(as_row[0] == row, as_row[1] == col)

    loads = [
        pltpu.make_async_copy(source, target, load_sems.at[i])
        for i, (source, target) in enumerate(
            ((vec_hbm, vec_ref), (halves_ref, tiles), (rest_hbm, rest_ref), (tri_hbm, tri_ref))
        )
    ]
    for load in loads:
        load.start()

    barrier = pltpu.get_barrier_semaphore()
    near = [moved(me, x=d) for d in (1, 2, 3)] + [moved(me, y=d) for d in (1, 2, 3)]
    near += [moved(me, z=d) for d in (1, 2, 3)] + [sibling]
    for device in near:
        pl.semaphore_signal(barrier, inc=1, device_id=device, device_id_type=MESH)

    @pl.when(jnp.logical_not(alone))
    def _():
        for device in (as_row, as_col):
            pl.semaphore_signal(barrier, inc=1, device_id=device, device_id_type=MESH)

    pl.semaphore_wait(barrier, len(near) + jnp.where(alone, 0, 2).astype(jnp.int32))

    copies = Copies(send_sems, recv_sems)
    z_ring = (z, row_shift, moved(me, z=1), moved(me, z=3))
    x_ring = (x, 0, moved(me, x=1), moved(me, x=3))
    spread = Spread(me, vec_ref, vec_row, vec_send_sems, vec_recv_sems)
    loads[0].wait()
    spread.begin()
    vec_high[0], vec_low[0] = split(vec_ref[...])
    loads[1].wait()

    def facts(position):
        block_row = row + 8 * position
        return block_row >= col, jnp.where(block_row == col, 0.5, 1.0).astype(jnp.float32)

    def upper(which):
        return vec_high[which, 0:HALF], vec_low[which, 0:HALF]

    def lower(which):
        return vec_high[which, HALF:TILE], vec_low[which, HALF:TILE]

    def whole(which):
        return vec_high[which], vec_low[which]

    def row_part(position):
        is_lower, weight = facts(position)
        tile_high[position], tile_low[position] = split(tiles[position])
        tile = tile_high.at[position], tile_low.at[position]

        @pl.when(is_lower)
        def _():
            parts[1 + position, 0:HALF] = product((tile[0][...], tile[1][...]), whole(0), NN) * weight
            parts[1 + position, HALF:TILE] = jnp.zeros((HALF, WIDTH), jnp.float32)

        @pl.when(jnp.logical_not(is_lower))
        def _():
            parts[1 + position] = product((tile[0][...], tile[1][...]), lower(0), TN)

    def col_part(position):
        is_lower, weight = facts(position)
        tile = tile_high.at[position], tile_low.at[position]

        @pl.when(is_lower)
        def _():
            parts[0] += product((tile[0][...], tile[1][...]), upper(1 + position), TN) * weight

        @pl.when(jnp.logical_not(is_lower))
        def _():
            parts[0, HALF:TILE] += product((tile[0][...], tile[1][...]), whole(1 + position), NN)

    row_partner = moved(me, y=2)
    col_partner = at(x, 1 - lo, z, hi, core)
    row_part(1 - core)
    pair = copies.start(parts.at[2 - core], sibling_in, sibling)
    spread.serve(0)
    row_part(core)
    spread.serve(1)
    spread.serve(2)
    rest_rows = rows(HALF + row * REST, REST)
    loads[2].wait()
    block = split(rest_ref[...])
    rest_part[...] = product(block, whole(0), NN) * 0.5
    parts[0] = product(block, (vec_high[0, rest_rows, :], vec_low[0, rest_rows, :]), TN) * 0.5
    spread.serve(3)
    spread.serve(4)
    pair.wait_recv()
    row_sum[...] = parts[1 + core] + sibling_in[...]
    spread.serve(5)
    spread.serve(6)
    spread.serve(7)
    spread.half_end()
    early = spread.early
    vec_high[1 + early], vec_low[1 + early] = split(vec_row[early])
    col_part(early)
    spread.end()
    row_scatter = ring_scatter(copies, row_sum, row_unit, row_relay, *z_ring, row_half, row_partner, pair_in.at[0])
    next(row_scatter)
    vec_high[2 - early], vec_low[2 - early] = split(vec_row[1 - early])
    col_part(1 - early)
    col_high[...], col_low[...] = split(parts[0])
    parts[0, rest_rows, :] += rest_part[...]
    columns = ring_scatter(copies, parts.at[0], col_unit, col_relay, *x_ring, lo, col_partner, pair_in.at[1])
    next(columns)
    partial[...] = product(whole(0), (col_high[...], col_low[...]), TN)
    inner = inner_sum(
        copies, me, partial, inner_ref, (first, first_in, second_in, third_in, fourth_in)
    )
    next(inner)
    loads[3].wait()
    tri = split(tri_ref[...])
    next(row_scatter)
    next(inner)
    next(row_scatter)
    next(columns)
    next(row_scatter)
    next(columns)
    next(row_scatter)
    next(inner)
    next(columns)
    step_all([row_scatter])
    keep_row, keep_col = rows(row_half * PIECE, PIECE), rows(lo * PIECE, PIECE)
    swap_out[0] = product(split(row_unit[keep_row, :] + pair_in[0]), tri, NN)
    row_copy = copies.make(swap_out.at[0], swap_in.at[0], as_row)

    @pl.when(jnp.logical_not(alone))
    def _():
        row_copy.start()

    next(columns)
    next(inner)
    step_all([columns])
    swap_out[1] = product(split(col_unit[keep_col, :] + pair_in[1]), tri, NN)
    col_copy = copies.make(swap_out.at[1], swap_in.at[1], as_col)

    @pl.when(jnp.logical_not(alone))
    def _():
        col_copy.start()

    @pl.when(alone)
    def _():
        swap_in[...] = swap_out[...]

    next(inner)

    @pl.when(jnp.logical_not(alone))
    def _():
        row_copy.wait()

    av_col[rows(x * UNIT + lo * PIECE, PIECE), :] = swap_out[1] + swap_in[0]
    columns = ring_gather(copies, av_col, *x_ring, lo, col_partner)
    next(columns)
    next(inner)

    @pl.when(jnp.logical_not(alone))
    def _():
        col_copy.wait()

    av_row[core, rows(((z + row_shift) % 4) * UNIT + row_half * PIECE, PIECE), :] = swap_out[0] + swap_in[1]
    rows_in = ring_gather(copies, av_row.at[core], *z_ring, row_half, row_partner, sibling)
    next(rows_in)
    next(columns)
    step_all([inner])
    next(rows_in)
    next(columns)
    whole_inner = inner_ref[...] + inner_ref[...].T
    middle = split(product(split(product(tri, split(whole_inner), TN)), tri, NN) * 0.5)
    vec_middle[0] = product(whole(0), middle, NN)
    next(rows_in)
    next(columns)
    vec_middle[1] = product(whole(1), middle, NN)
    next(rows_in)
    next(columns)
    vec_middle[2] = product(whole(2), middle, NN)
    step_all([columns])
    w = av_col[...] - vec_middle[0]
    w_ref[...] = w
    w_high[0], w_low[0] = split(w)
    next(rows_in)
    w_high[1 + core], w_low[1 + core] = split(av_row[core] - vec_middle[1 + core])
    step_all([rows_in])
    w_high[2 - core], w_low[2 - core] = split(av_row[1 - core] - vec_middle[2 - core])
    copies.finish()
    spread.finish()


def update_kernel(
    halves_ref, rest_ref, vec_high, vec_low, w_high, w_low, w_ref, out_ref, out_rest, out_w,
    tiles, rest, store_sems, side_sems,
):
    row, col = lax.axis_index("row"), lax.axis_index("col")
    count, _, size = tiles.shape
    each = TILE // size

    def place_of(ref, at_step):
        return ref.at[at_step // each, :, pl.ds(pl.multiple_of((at_step % each) * size, size), size)]

    def store(at_step):
        return pltpu.make_async_copy(tiles.at[at_step], place_of(out_ref, at_step), store_sems.at[at_step])

    w_copy = pltpu.make_async_copy(w_ref, out_w, side_sems.at[0])
    rest_in = pltpu.make_async_copy(rest_ref, rest, side_sems.at[1])
    rest_out = pltpu.make_async_copy(rest, out_rest, side_sems.at[2])
    rest_in.start()
    w_copy.start()
    rest_rows = rows(HALF + row * REST, REST)
    update = product(
        (vec_high[0, rest_rows, :], vec_low[0, rest_rows, :]), (w_high[0], w_low[0]), NT
    ) + product((w_high[0, rest_rows, :], w_low[0, rest_rows, :]), (vec_high[0], vec_low[0]), NT)
    rest_in.wait()
    rest[...] = rest[...] - update
    rest_out.start()

    def one(at_step, carry):
        position = at_step // each
        is_lower = row + 8 * position >= col
        high_rows = rows(jnp.where(is_lower, 0, HALF), HALF)
        low_rows = rows((at_step % each) * size, size)
        low_at = jnp.where(is_lower, 0, 1 + position)
        high_at = jnp.where(is_lower, 1 + position, 0)
        update = product(
            (vec_high[high_at, high_rows, :], vec_low[high_at, high_rows, :]),
            (w_high[low_at, low_rows, :], w_low[low_at, low_rows, :]),
            NT,
        ) + product(
            (w_high[high_at, high_rows, :], w_low[high_at, high_rows, :]),
            (vec_high[low_at, low_rows, :], vec_low[low_at, low_rows, :]),
            NT,
        )
        tiles[at_step] = place_of(halves_ref, at_step)[...] - update
        store(at_step).start()
        return carry

    lax.fori_loop(0, count, one, 0)
    for at_step in range(count):
        store(at_step).wait()
    w_copy.wait()
    rest_out.wait()


def shards(halves, diag_rest, panel_vectors, tri_factor):
    vmem = pl.BlockSpec(memory_space=pltpu.VMEM)
    outside = pl.BlockSpec(memory_space=pltpu.HBM)
    f32 = jnp.float32
    block = (TILE, WIDTH)

    def buffer(*shape):
        return pltpu.VMEM(shape, f32)

    held = pltpu.with_memory_space_constraint
    diag_rest, panel_vectors, tri_factor = (held(value, pltpu.HBM) for value in (diag_rest, panel_vectors, tri_factor))
    terms = jax.ShapeDtypeStruct((3,) + block, jnp.bfloat16)
    handed = pl.pallas_call(
        gather_kernel,
        out_shape=[terms, terms, terms, terms, jax.ShapeDtypeStruct(block, f32)],
        in_specs=[outside] * 4,
        out_specs=[vmem] * 5,
        scratch_shapes=[
            buffer(*block),
            buffer(REST, TILE),
            buffer(WIDTH, WIDTH),
            buffer(*block),
            buffer(2, *block),
            buffer(2, *block),
            buffer(WIDTH, WIDTH),
            buffer(3, *block),
            buffer(2, HALF, TILE),
            pltpu.VMEM((2, HALF, TILE), jnp.bfloat16),
            pltpu.VMEM((2, HALF, TILE), jnp.bfloat16),
            pltpu.VMEM(block, jnp.bfloat16),
            pltpu.VMEM(block, jnp.bfloat16),
            buffer(3, *block),
            buffer(REST, WIDTH),
            buffer(WIDTH, WIDTH),
            buffer(*block),
            buffer(*block),
            buffer(16, PIECE // 2, WIDTH),
            buffer(16, PIECE // 2, WIDTH),
            buffer(UNIT, WIDTH),
            buffer(UNIT, WIDTH),
            buffer(2, PIECE, WIDTH),
            buffer(2, PIECE, WIDTH),
            buffer(2, PIECE, WIDTH),
            buffer(128, WIDTH),
            buffer(128, WIDTH),
            buffer(3, 32, WIDTH),
            buffer(4, 32, WIDTH),
            buffer(4, 32, WIDTH),
            pltpu.SemaphoreType.DMA((4,)),
            pltpu.SemaphoreType.DMA((96,)),
            pltpu.SemaphoreType.DMA((96,)),
            pltpu.SemaphoreType.DMA((5 * CHUNKS,)),
            pltpu.SemaphoreType.DMA((5 * CHUNKS,)),
        ],
        compiler_params=pltpu.CompilerParams(
            collective_id=0, has_side_effects=True, vmem_limit_bytes=44 * 2**20
        ),
        name="gather",
    )(halves, diag_rest, panel_vectors, tri_factor)

    size = 256
    count = 2 * TILE // size
    return pl.pallas_call(
        update_kernel,
        out_shape=[
            jax.ShapeDtypeStruct(halves.shape, f32),
            jax.ShapeDtypeStruct(diag_rest.shape, f32),
            jax.ShapeDtypeStruct(panel_vectors.shape, f32),
        ],
        in_specs=[vmem, outside] + [vmem] * 5,
        out_specs=[outside] * 3,
        scratch_shapes=[
            buffer(count, HALF, size),
            buffer(REST, TILE),
            pltpu.SemaphoreType.DMA((count,)),
            pltpu.SemaphoreType.DMA((3,)),
        ],
        compiler_params=pltpu.CompilerParams(vmem_limit_bytes=24 * 2**20),
        name="update",
    )(halves, diag_rest, *handed)


def solution(mesh):
    return jax.shard_map(
        shards,
        mesh=mesh,
        in_specs=(P(None, "row", "col"), P(("col", "row"), None), P("col", None), P()),
        out_specs=(P(None, "row", "col"), P(("col", "row"), None), P("col", None)),
        check_vma=False,
    )
```

```python
import functools

import jax
import jax.numpy as jnp
from jax import lax
from jax.experimental import pallas as pl
from jax.experimental.pallas import tpu as pltpu
from jax.sharding import PartitionSpec as P

MESH = pl.DeviceIdType.MESH
NN = (((1,), (0,)), ((), ()))
TN = (((0,), (0,)), ((), ()))
NT = (((1,), (1,)), ((), ()))
TILE = 1024
HALF = 512
WIDTH = 256
UNIT = 256
PIECE = 128
REST = 64


def split(value):
    high = value.astype(jnp.bfloat16)
    low = (value - high.astype(jnp.float32)).astype(jnp.bfloat16)
    return high, low


def product(left, right, dims):
    def dot(a, b):
        return lax.dot_general(a, b, dims, preferred_element_type=jnp.float32)

    return dot(left[0], right[0]) + (dot(left[0], right[1]) + dot(left[1], right[0]))


def rows(start, size):
    return pl.ds(pl.multiple_of(start, 8), size)


def place():
    row, col = lax.axis_index("row"), lax.axis_index("col")
    return dict(row=row, col=col, x=row // 2, lo=row % 2, z=col // 4, hi=(col // 2) % 2, core=col % 2)


def at(x, lo, z, hi, core):
    return (x * 2 + lo, z * 4 + hi * 2 + core)


def moved(me, x=0, y=0, z=0, core=0):
    y_at = (me["hi"] * 2 + me["lo"] + y) % 4
    return at((me["x"] + x) % 4, y_at % 2, (me["z"] + z) % 4, y_at // 2, (me["core"] + core) % 2)


class Copies:
    def __init__(self, send_sems, recv_sems):
        self.send_sems, self.recv_sems, self.used, self.started = send_sems, recv_sems, 0, []

    def make(self, source, target, device):
        copy = pltpu.make_async_remote_copy(
            src_ref=source,
            dst_ref=target,
            send_sem=self.send_sems.at[self.used],
            recv_sem=self.recv_sems.at[self.used],
            device_id=device,
            device_id_type=MESH,
        )
        self.used += 1
        return copy

    def start(self, source, target, device):
        copy = self.make(source, target, device)
        copy.start()
        self.started.append(copy)
        return copy

    def finish(self):
        for copy in self.started:
            copy.wait_send()


def ring_scatter(copies, source, out, relay, index, shift, plus, minus, kept, partner, pair_in):
    size = PIECE // 2
    given = 1 - kept

    def part(step, which, at_half):
        return source.at[rows(((index + step + shift) % 4) * UNIT + which * PIECE + at_half * size, size)]

    def far(base, which):
        return (
            copies.start(part(2, which, 0), relay.at[base], plus),
            copies.start(part(2, which, 1), relay.at[base + 1], minus),
        )

    def near(base, which):
        return (
            copies.start(part(1, which, 1), relay.at[base + 2], plus),
            copies.start(part(3, which, 0), relay.at[base + 3], minus),
        )

    def passed(base, which, arriving):
        arriving[0].wait_recv()
        relay[base + 6] = relay[base] + part(1, which, 0)[...]
        to_plus = copies.start(relay.at[base + 6], relay.at[base + 4], plus)
        arriving[1].wait_recv()
        relay[base + 7] = relay[base + 1] + part(3, which, 1)[...]
        return to_plus, copies.start(relay.at[base + 7], relay.at[base + 5], minus)

    def total(base, which, arriving):
        for copy in arriving:
            copy.wait_recv()
        out[rows(which * PIECE, size), :] = part(0, which, 0)[...] + (relay[base + 4] + relay[base + 3])
        out[rows(which * PIECE + size, size), :] = part(0, which, 1)[...] + (relay[base + 2] + relay[base + 5])

    far_given = far(0, given)
    near_given = near(0, given)
    far_kept = far(8, kept)
    yield
    sum_given = passed(0, given, far_given)
    near_kept = near(8, kept)
    yield
    sum_kept = passed(8, kept, far_kept)
    yield
    total(0, given, near_given + sum_given)
    pair = copies.start(out.at[rows(given * PIECE, PIECE)], pair_in, partner)
    yield
    total(8, kept, near_kept + sum_kept)
    yield
    pair.wait_recv()


def ring_gather(copies, block, index, shift, plus, minus, kept, partner, sibling=None):
    def piece(step, which):
        return block.at[rows(((index + step + shift) % 4) * UNIT + which * PIECE, PIECE)]

    given = 1 - kept
    shared = []

    def part(step, which, at_half):
        start = ((index + step + shift) % 4) * UNIT + which * PIECE + at_half * (PIECE // 2)
        return block.at[rows(start, PIECE // 2)]

    def share(ref):
        if sibling is not None:
            shared.append(copies.start(ref, ref, sibling))

    def send(ref, device):
        return copies.start(ref, ref, device)

    own = piece(0, kept)
    pair = [send(part(0, kept, half), partner) for half in (0, 1)]
    own_plus, own_minus = send(own, plus), send(own, minus)
    share(own)
    yield
    other_plus, other_minus = [], []
    for half in (0, 1):
        pair[half].wait_recv()
        other_minus.append(send(part(0, given, half), minus))
        other_plus.append(send(part(0, given, half), plus))
    share(piece(0, given))
    yield
    own_plus.wait_recv()
    far_plus = send(piece(3, kept), plus)
    share(piece(3, kept))
    own_minus.wait_recv()
    share(piece(1, kept))
    yield
    far_minus = []
    for half in (0, 1):
        other_minus[half].wait_recv()
        far_minus.append(send(part(1, given, half), minus))
    share(piece(1, given))
    for copy in other_plus:
        copy.wait_recv()
    share(piece(3, given))
    yield
    far_plus.wait_recv()
    share(piece(2, kept))
    for half in (0, 1):
        far_minus[half].wait_recv()
        share(part(2, given, half))
    yield
    for copy in shared:
        copy.wait_recv()


CHUNKS = 16
CHUNK = TILE // CHUNKS
ORDER = [half + c for c in range(CHUNKS // 2) for half in (0, CHUNKS // 2)]


class Spread:
    def __init__(self, me, vec_ref, vec_row, send_sems, recv_sems):
        x, lo, z, hi, core = me["x"], me["lo"], me["z"], me["hi"], me["core"]
        self.vec_ref, self.vec_row, self.send_sems, self.recv_sems = vec_ref, vec_row, send_sems, recv_sems
        self.lead = core == lo
        line = hi == x % 2
        end = z % 2 == x // 2
        self.source = jnp.logical_and(jnp.logical_and(self.lead, line), end)
        self.cross = jnp.logical_and(jnp.logical_and(jnp.logical_not(self.lead), line), end)
        self.target = jnp.logical_and(jnp.logical_and(self.lead, jnp.logical_not(line)), end)
        self.ends = jnp.logical_and(self.lead, end)
        self.middle = jnp.logical_and(self.lead, jnp.logical_not(end))
        self.follow = jnp.logical_not(self.lead)
        self.plus, self.minus, self.sibling = moved(me, z=1), moved(me, z=3), moved(me, core=1)
        self.over = at(x, core, z, 1 - hi, core)
        self.own = z // 2
        self.from_minus = ((z + 3) % 4) // 2
        self.early = jnp.where(end, self.own, self.from_minus)

    def chunk(self, block, c):
        return self.vec_row.at[block, pl.ds(c * CHUNK, CHUNK)]

    def copy(self, slot, source, target, device):
        return pltpu.make_async_remote_copy(
            src_ref=source,
            dst_ref=target,
            send_sem=self.send_sems.at[slot],
            recv_sem=self.recv_sems.at[slot],
            device_id=device,
            device_id_type=MESH,
        )

    def mine(self, c):
        return self.vec_ref.at[pl.ds(c * CHUNK, CHUNK)]

    def along(self, c, block, source=None):
        here = self.chunk(block, c)
        return self.copy(c, here if source is None else source, here, self.plus)

    def back(self, c, block, source=None):
        here = self.chunk(block, c)
        return self.copy(CHUNKS + c, here if source is None else source, here, self.minus)

    def across(self, c):
        return self.copy(2 * CHUNKS + c, self.mine(c), self.chunk(self.own, c), self.over)

    def share(self, c, block, which, source=None):
        here = self.chunk(block, c)
        return self.copy((3 + which) * CHUNKS + c, here if source is None else source, here, self.sibling)

    def begin(self):
        @pl.when(self.source)
        def _():
            for c in ORDER:
                self.along(c, self.own, self.mine(c)).start()
                self.back(c, self.own, self.mine(c)).start()
                self.share(c, self.own, 0, self.mine(c)).start()
            self.vec_row[self.own] = self.vec_ref[...]

        @pl.when(self.cross)
        def _():
            for c in ORDER:
                self.across(c).start()

    def serve(self, *steps):
        for step in steps:
            self.pass_on(ORDER[2 * step])
            self.pass_on(ORDER[2 * step + 1])

    def pass_on(self, c):
        @pl.when(self.target)
        def _():
            self.across(c).wait_recv()
            self.along(c, self.own).start()
            self.back(c, self.own).start()
            self.share(c, self.own, 0).start()

        @pl.when(self.middle)
        def _():
            block = self.from_minus
            self.along(c, block).wait_recv()
            if c < CHUNKS // 2:
                self.along(c, block).start()
            self.share(c, block, 0).start()
            self.back(c, 1 - block).wait_recv()
            if c >= CHUNKS // 2:
                self.back(c, 1 - block).start()
            self.share(c, 1 - block, 1).start()

    def half_end(self):
        @pl.when(self.follow)
        def _():
            for c in ORDER:
                self.share(c, 0, 0).wait_recv()

    def end(self):
        @pl.when(self.ends)
        def _():
            for c in ORDER:
                copy = self.along(c, 1 - self.own) if c < CHUNKS // 2 else self.back(c, 1 - self.own)
                copy.wait_recv()
                self.share(c, 1 - self.own, 1).start()

        @pl.when(self.follow)
        def _():
            for c in ORDER:
                self.share(c, 1, 1).wait_recv()

    def finish(self):
        @pl.when(self.ends)
        def _():
            for c in ORDER:
                self.along(c, self.own).wait_send()
                self.back(c, self.own).wait_send()

        @pl.when(self.middle)
        def _():
            for c in ORDER:
                if c < CHUNKS // 2:
                    self.along(c, 0).wait_send()
                else:
                    self.back(c, 0).wait_send()

        @pl.when(self.lead)
        def _():
            for c in ORDER:
                for which in range(2):
                    self.share(c, which, which).wait_send()

        @pl.when(self.cross)
        def _():
            for c in ORDER:
                self.across(c).wait_send()


def inner_sum(copies, me, partial, total, work):
    first, first_in, second_in, third_in, fourth_in = work
    sibling = moved(me, core=1)
    core, x, y, z = me["core"], me["x"], me["hi"] * 2 + me["lo"], me["z"]
    copy = copies.start(partial.at[rows((1 - core) * 128, 128)], first_in, sibling)
    yield
    copy.wait_recv()
    first[...] = partial[rows(core * 128, 128), :] + first_in[...]
    sent = [
        copies.start(first.at[rows(((y + d) % 4) * 32, 32)], second_in.at[d - 1], moved(me, y=d)) for d in (1, 2, 3)
    ]
    yield
    for copy in sent:
        copy.wait_recv()
    mine = third_in.at[z]
    mine[...] = first[rows(y * 32, 32), :] + second_in[0] + second_in[1] + second_in[2]
    sent = [copies.start(mine, mine, moved(me, z=d)) for d in (1, 2, 3)]
    yield
    for copy in sent:
        copy.wait_recv()
    mine = fourth_in.at[x]
    mine[...] = third_in[0] + third_in[1] + third_in[2] + third_in[3]
    sent = [copies.start(mine, mine, moved(me, x=d)) for d in (1, 2, 3)]
    yield
    for copy in sent:
        copy.wait_recv()
    mine = total.at[rows(core * 128 + y * 32, 32)]
    mine[...] = fourth_in[0] + fourth_in[1] + fourth_in[2] + fourth_in[3]
    sent = [copies.start(mine, mine, moved(me, y=d)) for d in (1, 2, 3)]
    yield
    for copy in sent:
        copy.wait_recv()
    mine = total.at[rows(core * 128, 128)]
    copy = copies.start(mine, mine, sibling)
    yield
    copy.wait_recv()


def step_all(running):
    still = []
    for item in running:
        if next(item, "done") != "done":
            still.append(item)
    return still


def gather_kernel(
    halves_ref, rest_hbm, vec_hbm, tri_hbm, vec_high, vec_low, w_high, w_low, w_ref,
    vec_ref, rest_ref, tri_ref, av_col, av_row, vec_row, inner_ref, vec_middle,
    tiles, tile_high, tile_low, col_high, col_low, parts, rest_part, partial, row_sum, sibling_in, row_relay, col_relay,
    row_unit, col_unit, pair_in, swap_out, swap_in,
    first, first_in, second_in, third_in, fourth_in,
    load_sems, send_sems, recv_sems, vec_send_sems, vec_recv_sems,
):
    me = place()
    row, col, core = me["row"], me["col"], me["core"]
    x, lo, z, hi = me["x"], me["lo"], me["z"], me["hi"]
    sibling = moved(me, core=1)

    row_shift = (x - (x // 2 + 2 * core) + 4) % 4
    row_half = (lo + hi + x) % 2
    as_row = (((z + row_shift) % 4) * 2 + row_half, row + 8 * core)
    row_of = col % 8
    as_col = at(row_of // 2, row_of % 2, (x - row_of // 2 + z + 4) % 4, (lo + row_of + hi) % 2, col // 8)
    alone = jnp.logical_and(as_row[0] == row, as_row[1] == col)

    loads = [
        pltpu.make_async_copy(source, target, load_sems.at[i])
        for i, (source, target) in enumerate(
            ((vec_hbm, vec_ref), (halves_ref, tiles), (rest_hbm, rest_ref), (tri_hbm, tri_ref))
        )
    ]
    for load in loads:
        load.start()

    barrier = pltpu.get_barrier_semaphore()
    near = [moved(me, x=d) for d in (1, 2, 3)] + [moved(me, y=d) for d in (1, 2, 3)]
    near += [moved(me, z=d) for d in (1, 2, 3)] + [sibling]
    for device in near:
        pl.semaphore_signal(barrier, inc=1, device_id=device, device_id_type=MESH)

    @pl.when(jnp.logical_not(alone))
    def _():
        for device in (as_row, as_col):
            pl.semaphore_signal(barrier, inc=1, device_id=device, device_id_type=MESH)

    pl.semaphore_wait(barrier, len(near) + jnp.where(alone, 0, 2).astype(jnp.int32))

    copies = Copies(send_sems, recv_sems)
    z_ring = (z, row_shift, moved(me, z=1), moved(me, z=3))
    x_ring = (x, 0, moved(me, x=1), moved(me, x=3))
    spread = Spread(me, vec_ref, vec_row, vec_send_sems, vec_recv_sems)
    loads[0].wait()
    spread.begin()
    vec_high[0], vec_low[0] = split(vec_ref[...])
    loads[1].wait()

    def facts(position):
        block_row = row + 8 * position
        return block_row >= col, jnp.where(block_row == col, 0.5, 1.0).astype(jnp.float32)

    def upper(which):
        return vec_high[which, 0:HALF], vec_low[which, 0:HALF]

    def lower(which):
        return vec_high[which, HALF:TILE], vec_low[which, HALF:TILE]

    def whole(which):
        return vec_high[which], vec_low[which]

    def row_part(position):
        is_lower, weight = facts(position)
        tile_high[position], tile_low[position] = split(tiles[position])
        tile = tile_high.at[position], tile_low.at[position]

        @pl.when(is_lower)
        def _():
            parts[1 + position, 0:HALF] = product((tile[0][...], tile[1][...]), whole(0), NN) * weight
            parts[1 + position, HALF:TILE] = jnp.zeros((HALF, WIDTH), jnp.float32)

        @pl.when(jnp.logical_not(is_lower))
        def _():
            parts[1 + position] = product((tile[0][...], tile[1][...]), lower(0), TN)

    def col_part(position):
        is_lower, weight = facts(position)
        tile = tile_high.at[position], tile_low.at[position]

        @pl.when(is_lower)
        def _():
            parts[0] += product((tile[0][...], tile[1][...]), upper(1 + position), TN) * weight

        @pl.when(jnp.logical_not(is_lower))
        def _():
            parts[0, HALF:TILE] += product((tile[0][...], tile[1][...]), whole(1 + position), NN)

    row_partner = moved(me, y=2)
    col_partner = at(x, 1 - lo, z, hi, core)
    row_part(1 - core)
    pair = copies.start(parts.at[2 - core], sibling_in, sibling)
    spread.serve(0)
    row_part(core)
    spread.serve(1)
    spread.serve(2)
    rest_rows = rows(HALF + row * REST, REST)
    loads[2].wait()
    block = split(rest_ref[...])
    rest_part[...] = product(block, whole(0), NN) * 0.5
    parts[0] = product(block, (vec_high[0, rest_rows, :], vec_low[0, rest_rows, :]), TN) * 0.5
    spread.serve(3)
    spread.serve(4)
    pair.wait_recv()
    row_sum[...] = parts[1 + core] + sibling_in[...]
    spread.serve(5)
    spread.serve(6)
    spread.serve(7)
    spread.half_end()
    early = spread.early
    vec_high[1 + early], vec_low[1 + early] = split(vec_row[early])
    col_part(early)
    spread.end()
    row_scatter = ring_scatter(copies, row_sum, row_unit, row_relay, *z_ring, row_half, row_partner, pair_in.at[0])
    next(row_scatter)
    vec_high[2 - early], vec_low[2 - early] = split(vec_row[1 - early])
    col_part(1 - early)
    col_high[...], col_low[...] = split(parts[0])
    parts[0, rest_rows, :] += rest_part[...]
    columns = ring_scatter(copies, parts.at[0], col_unit, col_relay, *x_ring, lo, col_partner, pair_in.at[1])
    next(columns)
    partial[...] = product(whole(0), (col_high[...], col_low[...]), TN)
    inner = inner_sum(
        copies, me, partial, inner_ref, (first, first_in, second_in, third_in, fourth_in)
    )
    next(inner)
    loads[3].wait()
    tri = split(tri_ref[...])
    next(row_scatter)
    next(inner)
    next(row_scatter)
    next(columns)
    next(row_scatter)
    next(columns)
    next(row_scatter)
    next(inner)
    next(columns)
    step_all([row_scatter])
    keep_row, keep_col = rows(row_half * PIECE, PIECE), rows(lo * PIECE, PIECE)
    swap_out[0] = product(split(row_unit[keep_row, :] + pair_in[0]), tri, NN)
    row_copy = copies.make(swap_out.at[0], swap_in.at[0], as_row)

    @pl.when(jnp.logical_not(alone))
    def _():
        row_copy.start()

    next(columns)
    next(inner)
    step_all([columns])
    swap_out[1] = product(split(col_unit[keep_col, :] + pair_in[1]), tri, NN)
    col_copy = copies.make(swap_out.at[1], swap_in.at[1], as_col)

    @pl.when(jnp.logical_not(alone))
    def _():
        col_copy.start()

    @pl.when(alone)
    def _():
        swap_in[...] = swap_out[...]

    next(inner)

    @pl.when(jnp.logical_not(alone))
    def _():
        row_copy.wait()

    av_col[rows(x * UNIT + lo * PIECE, PIECE), :] = swap_out[1] + swap_in[0]
    columns = ring_gather(copies, av_col, *x_ring, lo, col_partner)
    next(columns)
    next(inner)

    @pl.when(jnp.logical_not(alone))
    def _():
        col_copy.wait()

    av_row[core, rows(((z + row_shift) % 4) * UNIT + row_half * PIECE, PIECE), :] = swap_out[0] + swap_in[1]
    rows_in = ring_gather(copies, av_row.at[core], *z_ring, row_half, row_partner, sibling)
    next(rows_in)
    next(columns)
    step_all([inner])
    next(rows_in)
    next(columns)
    whole_inner = inner_ref[...] + inner_ref[...].T
    middle = split(product(split(product(tri, split(whole_inner), TN)), tri, NN) * 0.5)
    vec_middle[0] = product(whole(0), middle, NN)
    next(rows_in)
    next(columns)
    vec_middle[1] = product(whole(1), middle, NN)
    next(rows_in)
    next(columns)
    vec_middle[2] = product(whole(2), middle, NN)
    step_all([columns])
    w = av_col[...] - vec_middle[0]
    w_ref[...] = w
    w_high[0], w_low[0] = split(w)
    next(rows_in)
    w_high[1 + core], w_low[1 + core] = split(av_row[core] - vec_middle[1 + core])
    step_all([rows_in])
    w_high[2 - core], w_low[2 - core] = split(av_row[1 - core] - vec_middle[2 - core])
    copies.finish()
    spread.finish()


def update_kernel(
    halves_ref, rest_ref, vec_high, vec_low, w_high, w_low, w_ref, out_ref, out_rest, out_w,
    tiles, rest, store_sems, side_sems,
):
    row, col = lax.axis_index("row"), lax.axis_index("col")
    count, _, size = tiles.shape
    each = TILE // size

    def place_of(ref, at_step):
        return ref.at[at_step // each, :, pl.ds(pl.multiple_of((at_step % each) * size, size), size)]

    def store(at_step):
        return pltpu.make_async_copy(tiles.at[at_step], place_of(out_ref, at_step), store_sems.at[at_step])

    w_copy = pltpu.make_async_copy(w_ref, out_w, side_sems.at[0])
    rest_in = pltpu.make_async_copy(rest_ref, rest, side_sems.at[1])
    rest_out = pltpu.make_async_copy(rest, out_rest, side_sems.at[2])
    rest_in.start()
    w_copy.start()
    rest_rows = rows(HALF + row * REST, REST)
    update = product(
        (vec_high[0, rest_rows, :], vec_low[0, rest_rows, :]), (w_high[0], w_low[0]), NT
    ) + product((w_high[0, rest_rows, :], w_low[0, rest_rows, :]), (vec_high[0], vec_low[0]), NT)
    rest_in.wait()
    rest[...] = rest[...] - update
    rest_out.start()

    def one(at_step, carry):
        position = at_step // each
        is_lower = row + 8 * position >= col
        high_rows = rows(jnp.where(is_lower, 0, HALF), HALF)
        low_rows = rows((at_step % each) * size, size)
        low_at = jnp.where(is_lower, 0, 1 + position)
        high_at = jnp.where(is_lower, 1 + position, 0)
        update = product(
            (vec_high[high_at, high_rows, :], vec_low[high_at, high_rows, :]),
            (w_high[low_at, low_rows, :], w_low[low_at, low_rows, :]),
            NT,
        ) + product(
            (w_high[high_at, high_rows, :], w_low[high_at, high_rows, :]),
            (vec_high[low_at, low_rows, :], vec_low[low_at, low_rows, :]),
            NT,
        )
        tiles[at_step] = place_of(halves_ref, at_step)[...] - update
        store(at_step).start()
        return carry

    lax.fori_loop(0, count, one, 0, unroll=True)
    for at_step in range(count):
        store(at_step).wait()
    w_copy.wait()
    rest_out.wait()


def shards(halves, diag_rest, panel_vectors, tri_factor):
    vmem = pl.BlockSpec(memory_space=pltpu.VMEM)
    outside = pl.BlockSpec(memory_space=pltpu.HBM)
    f32 = jnp.float32
    block = (TILE, WIDTH)

    def buffer(*shape):
        return pltpu.VMEM(shape, f32)

    held = pltpu.with_memory_space_constraint
    diag_rest, panel_vectors, tri_factor = (held(value, pltpu.HBM) for value in (diag_rest, panel_vectors, tri_factor))
    terms = jax.ShapeDtypeStruct((3,) + block, jnp.bfloat16)
    handed = pl.pallas_call(
        gather_kernel,
        out_shape=[terms, terms, terms, terms, jax.ShapeDtypeStruct(block, f32)],
        in_specs=[outside] * 4,
        out_specs=[vmem] * 5,
        scratch_shapes=[
            buffer(*block),
            buffer(REST, TILE),
            buffer(WIDTH, WIDTH),
            buffer(*block),
            buffer(2, *block),
            buffer(2, *block),
            buffer(WIDTH, WIDTH),
            buffer(3, *block),
            buffer(2, HALF, TILE),
            pltpu.VMEM((2, HALF, TILE), jnp.bfloat16),
            pltpu.VMEM((2, HALF, TILE), jnp.bfloat16),
            pltpu.VMEM(block, jnp.bfloat16),
            pltpu.VMEM(block, jnp.bfloat16),
            buffer(3, *block),
            buffer(REST, WIDTH),
            buffer(WIDTH, WIDTH),
            buffer(*block),
            buffer(*block),
            buffer(16, PIECE // 2, WIDTH),
            buffer(16, PIECE // 2, WIDTH),
            buffer(UNIT, WIDTH),
            buffer(UNIT, WIDTH),
            buffer(2, PIECE, WIDTH),
            buffer(2, PIECE, WIDTH),
            buffer(2, PIECE, WIDTH),
            buffer(128, WIDTH),
            buffer(128, WIDTH),
            buffer(3, 32, WIDTH),
            buffer(4, 32, WIDTH),
            buffer(4, 32, WIDTH),
            pltpu.SemaphoreType.DMA((4,)),
            pltpu.SemaphoreType.DMA((96,)),
            pltpu.SemaphoreType.DMA((96,)),
            pltpu.SemaphoreType.DMA((5 * CHUNKS,)),
            pltpu.SemaphoreType.DMA((5 * CHUNKS,)),
        ],
        compiler_params=pltpu.CompilerParams(
            collective_id=0, has_side_effects=True, vmem_limit_bytes=44 * 2**20
        ),
        name="gather",
    )(halves, diag_rest, panel_vectors, tri_factor)

    size = 256
    count = 2 * TILE // size
    return pl.pallas_call(
        update_kernel,
        out_shape=[
            jax.ShapeDtypeStruct(halves.shape, f32),
            jax.ShapeDtypeStruct(diag_rest.shape, f32),
            jax.ShapeDtypeStruct(panel_vectors.shape, f32),
        ],
        in_specs=[vmem, outside] + [vmem] * 5,
        out_specs=[outside] * 3,
        scratch_shapes=[
            buffer(count, HALF, size),
            buffer(REST, TILE),
            pltpu.SemaphoreType.DMA((count,)),
            pltpu.SemaphoreType.DMA((3,)),
        ],
        compiler_params=pltpu.CompilerParams(vmem_limit_bytes=24 * 2**20),
        name="update",
    )(halves, diag_rest, *handed)


def solution(mesh):
    return jax.shard_map(
        shards,
        mesh=mesh,
        in_specs=(P(None, "row", "col"), P(("col", "row"), None), P("col", None), P()),
        out_specs=(P(None, "row", "col"), P(("col", "row"), None), P("col", None)),
        check_vma=False,
    )
```
